32 devices in a mesh: expert: 4 (over z), ctx: 4 (over y, x), dp: 2 (over core).
Axes of the slice: x: 2, y: 2, z: 4, core: 2. Of those that a mesh axis runs over, the one named last changes fastest.
Arguments:
- tokens: bfloat16 [96, 256, 512], P(('expert', 'dp'), 'ctx'), may hold values from -6 to 6
- cotangent: bfloat16 [96, 256, 512], P(('expert', 'dp'), 'ctx'), may hold values from -6 to 6
- key_mask: int32 [96, 256], P(('expert', 'dp'), 'ctx'), may hold values from 0 to 1, as said below
- route_ids: int32 [96, 256, 2], P(('expert', 'dp'), 'ctx'), may hold values from 0 to 3, all different within a row
- priority: int32 [96, 256], P(('expert', 'dp'), 'ctx'), may hold values from 0 to 1023
- norm1_gain: float32 [512], replicated, may hold values from 0.5 to 1.5
- norm1_bias: float32 [512], replicated, may hold values from -1.75 to 1.75
- qkv_weight: bfloat16 [512, 1536], replicated, may hold values from -0.25 to 0.25
- query_bias: float32 [512], replicated, may hold values from -3 to 3
- value_bias: float32 [512], replicated, may hold values from -3 to 3
- proj_weight: bfloat16 [512, 512], replicated, may hold values from -1.5 to 1.5
- proj_bias: float32 [512], replicated, may hold values from -1.75 to 1.75
- norm2_gain: float32 [512], replicated, may hold values from 0.5 to 1.5
- norm2_bias: float32 [512], replicated, may hold values from -1.75 to 1.75
- router_weight: bfloat16 [512, 4], replicated, may hold values from -0.1875 to 0.1875
- expert_up: bfloat16 [4, 512, 2048], P('expert'), may hold values from -0.25 to 0.25
- expert_up_bias: float32 [4, 2048], P('expert'), may hold values from -1.75 to 1.75
- expert_down: bfloat16 [4, 2048, 512], P('expert'), may hold values from -0.25 to 0.25
- expert_down_bias: float32 [4, 512], P('expert'), may hold values from -0.625 to 0.625
Outputs:
- block_out: bfloat16 [96, 256, 512], P(('expert', 'dp'), 'ctx')
- input_grad: bfloat16 [96, 256, 512], P(('expert', 'dp'), 'ctx')
- grad_norm1_gain: float32 [512], P('expert')
- grad_norm1_bias: float32 [512], P('expert')
- grad_qkv: float32 [512, 1536], P('expert')
- grad_query_bias: float32 [512], P('expert')
- grad_value_bias: float32 [512], P('expert')
- grad_proj: float32 [512, 512], P('expert')
- grad_proj_bias: float32 [512], P('expert')
- grad_norm2_gain: float32 [512], P('expert')
- grad_norm2_bias: float32 [512], P('expert')
- grad_router: float32 [512, 4], P('expert')
- grad_up: float32 [4, 512, 2048], P('expert')
- grad_up_bias: float32 [4, 2048], P('expert')
- grad_down: float32 [4, 2048, 512], P('expert')
- grad_down_bias: float32 [4, 512], P('expert')
The draws below stay inside these ranges and needn't reach their ends.
Inputs may be any that keep to these rules, and one draw needn't show every extreme that they name: `key_mask`: in each image the first few keys are 1 and the rest 0; more than 192 are 1. `route_ids`: the two routes of a token name different experts.
All inputs are finite; a program needn't handle non-finite values.
Results may differ from the reference program's by a relative error of at most 0.019.
Values may be sent and summed in bfloat16 or wider, within the bound.
No kernel may reach another device: no remote copies, remote signals or barrier semaphores. Data moves between devices by JAX's collectives and lax.ppermute only.
A program may use at most 192 MiB of HBM per device.

```python
import math
import jax
import jax.numpy as jnp
from jax import lax

D = 512
HEADS = 8
HEAD_DIM = 64
FF = 2048
SEQ = 256
IMG_DEV = 12
EXPERTS = 4
LOCAL = 64
TOK_DEV = 768
IMAGES = 96
CAP = 384
N_CTX = 4


def draw_key_mask(key, part):
    key = jax.random.fold_in(key, 11)
    live_count = jax.random.randint(key, (IMAGES, 1), SEQ * 3 // 4 + 1, SEQ + 1)
    positions = jnp.arange(SEQ, dtype=jnp.int32)[None, :]
    return (positions < live_count).astype(jnp.int32)


def touch_ends(values, own_key, low, high):
    dims = values.shape
    spot = [jax.random.randint(jax.random.fold_in(own_key, axis), (), 0, dims[axis]) for axis in range(len(dims))]
    values = values.at[tuple(spot)].set(low)
    longest = dims.index(max(dims))
    spot[longest] = (spot[longest] + 1) % dims[longest]
    return values.at[tuple(spot)].set(high)


def shard_levels(own_key, shape, cuts, least, largest):
    level = 1.0
    for dim, shards_of in cuts:
        steps = jax.random.uniform(jax.random.fold_in(jax.random.fold_in(own_key, 6), dim), (shards_of,), jnp.float32, least / len(cuts), largest / len(cuts))
        level = level * jnp.repeat(jnp.exp(steps), shape[dim] // shards_of).reshape((-1,) + (1,) * (len(shape) - 1 - dim))
    return level


def distinct(key, rows, number_of, top, lift):
    order = jax.random.permutation(jax.random.fold_in(key, 1), number_of)
    pull = order
    for power in range(3):
        pull = pull * pull // number_of
    pull = pull * lift // number_of
    tickets = jax.random.randint(jax.random.fold_in(key, 2), (rows, number_of), 0, 4096) + pull
    holders = jax.random.permutation(jax.random.fold_in(key, 3), rows)[jnp.arange(number_of) % rows]
    tickets = jnp.where(jnp.arange(rows)[:, None] == holders[None, :], 1 << 14, tickets)
    merit = tickets * number_of + jnp.arange(number_of)
    return lax.top_k(merit.astype(jnp.int32), top)[1].astype(jnp.int32)


def noise(own_key, shape, width, limit, split=(), kind=jnp.bfloat16):
    drawn = jax.random.normal(own_key, shape, jnp.float32) * width
    if len(split) > 0:
        drawn = shard_levels(own_key, shape, split, -0.22, 0.18) * drawn
    return jnp.clip(drawn, min=-limit, max=limit).astype(kind)


def setup_inputs(seed: int = 0) -> dict:
    streams_of = jax.random.split(jax.random.key(seed), 20)
    tokens = noise(streams_of[0], (IMAGES, SEQ, D), 1.0, 6.0, ((0, 8), (1, 4)))
    cotangent = noise(streams_of[1], (IMAGES, SEQ, D), 1.0, 6.0, ((0, 8), (1, 4)))
    key_mask = draw_key_mask(jax.random.fold_in(streams_of[19], 71), 0)
    route_ids = distinct(streams_of[3], IMAGES * SEQ, EXPERTS, 2, 4096).reshape((IMAGES, SEQ, 2))
    priority = touch_ends(jax.random.randint(streams_of[4], (IMAGES, SEQ), 0, 1024), jax.random.fold_in(streams_of[4], 1), 0, 1023).astype(jnp.int32)
    norm1_gain = jnp.clip(1.0 + 0.1 * jax.random.normal(streams_of[5], (D,), jnp.float32), 0.5, 1.5)
    norm1_bias = noise(streams_of[6], (D,), 0.3, 1.75, (), jnp.float32)
    qkv_weight = noise(streams_of[7], (D, 3 * D), D ** -0.5, 0.25)
    query_bias = noise(streams_of[8], (D,), 0.5, 3.0, (), jnp.float32)
    value_bias = noise(streams_of[9], (D,), 0.5, 3.0, (), jnp.float32)
    proj_weight = noise(streams_of[10], (D, D), (D // 32) ** -0.5, 1.5)
    proj_bias = noise(streams_of[11], (D,), 0.3, 1.75, (), jnp.float32)
    norm2_gain = jnp.clip(1.0 + 0.1 * jax.random.normal(streams_of[12], (D,), jnp.float32), 0.5, 1.5)
    norm2_bias = noise(streams_of[13], (D,), 0.3, 1.75, (), jnp.float32)
    router_weight = noise(streams_of[14], (D, EXPERTS), (2 * D) ** -0.5, 0.1875)
    expert_up = noise(streams_of[15], (EXPERTS, D, FF), D ** -0.5, 0.25, ((0, 4),))
    expert_up_bias = noise(streams_of[16], (EXPERTS, FF), 0.3, 1.75, ((0, 4),), jnp.float32)
    expert_down = noise(streams_of[17], (EXPERTS, FF, D), (max(1, 4 * FF // (EXPERTS * EXPERTS))) ** -0.5, 0.25, ((0, 4),))
    expert_down_bias = noise(streams_of[18], (EXPERTS, D), (EXPERTS / 40), 0.625, ((0, 4),), jnp.float32)
    return {"tokens": tokens, "cotangent": cotangent, "key_mask": key_mask, "route_ids": route_ids, "priority": priority, "norm1_gain": norm1_gain, "norm1_bias": norm1_bias, "qkv_weight": qkv_weight, "query_bias": query_bias, "value_bias": value_bias, "proj_weight": proj_weight, "proj_bias": proj_bias, "norm2_gain": norm2_gain, "norm2_bias": norm2_bias, "router_weight": router_weight, "expert_up": expert_up, "expert_up_bias": expert_up_bias, "expert_down": expert_down, "expert_down_bias": expert_down_bias}


EPS = 1e-06
NEG = -1e+30
HIGH = lax.Precision.HIGHEST

@jax.custom_vjp
def low(v):
    return lax.optimization_barrier(v.astype(jnp.bfloat16)).astype(jnp.float32)

@jax.custom_vjp
def low_back(v):
    return v

def low_keep(v):
    return (low(v), None)

def low_pass(kept, grad):
    return (grad,)

def back_keep(v):
    return (v, None)

def back_low(kept, grad):
    return (low(grad),)
low.defvjp(low_keep, low_pass)
low_back.defvjp(back_keep, back_low)

def norm_rows(values, gain_vec, shift_vec):
    centre = values - lax.optimization_barrier(jnp.mean(values, axis=-1, keepdims=True))
    spread = lax.optimization_barrier(jnp.mean(centre * centre, axis=-1, keepdims=True))
    return centre * lax.rsqrt(spread + EPS) * gain_vec + shift_vec

def soft_rows(values):
    row_top = lax.optimization_barrier(jnp.max(values, axis=-1, keepdims=True))
    exp_values = jnp.exp(values - row_top)
    return exp_values / lax.optimization_barrier(jnp.sum(exp_values, axis=-1, keepdims=True))

def to_blocks(array):
    rest = array.shape[2:]
    shaped = array.reshape((IMAGES // IMG_DEV, IMG_DEV, N_CTX, LOCAL) + rest)
    return jnp.swapaxes(shaped, 1, 2).reshape((IMAGES // IMG_DEV * N_CTX, TOK_DEV) + rest)

def from_blocks(array):
    rest = array.shape[2:]
    shaped = array.reshape((IMAGES // IMG_DEV, N_CTX, IMG_DEV, LOCAL) + rest)
    return jnp.swapaxes(shaped, 1, 2).reshape((IMAGES, SEQ) + rest)

def slot_ranks(pair_experts, pair_prio):
    count = pair_experts.shape[0]
    half_count = count // 2
    order = jnp.arange(count, dtype=jnp.int32)
    route_of = order // half_count
    place = order % half_count
    same_route = route_of[None, :] == route_of[:, None]
    lower_prio = pair_prio[None, :] < pair_prio[:, None]
    same_prio = pair_prio[None, :] == pair_prio[:, None]
    before = (route_of[None, :] < route_of[:, None]) | same_route & (lower_prio | same_prio & (place[None, :] < place[:, None]))
    match = pair_experts[None, :] == pair_experts[:, None]
    return lax.optimization_barrier(jnp.sum((match & before).astype(jnp.int32), axis=1))

def slot_table(destination):
    order = jnp.arange(destination.shape[0], dtype=jnp.int32)
    return jnp.full((EXPERTS * CAP,), -1, dtype=jnp.int32).at[destination].set(order, mode='drop')

def attend(images_in, mask_in, gain_one, shift_one, qkv_w, query_b, value_b, proj_w, proj_b):
    count = images_in.shape[0]
    normed = low(norm_rows(images_in, gain_one, shift_one))
    projected = jnp.einsum('gsd,de->gse', normed, qkv_w, precision=HIGH)
    query = low_back(low(projected[..., :D] + query_b)).reshape(count, SEQ, HEADS, HEAD_DIM)
    keys = low_back(low(projected[..., D:2 * D])).reshape(count, SEQ, HEADS, HEAD_DIM)
    values = low_back(low(projected[..., 2 * D:] + value_b)).reshape(count, SEQ, HEADS, HEAD_DIM)
    scores = low_back(jnp.einsum('gqhd,gkhd->ghqk', query, keys, precision=HIGH) * HEAD_DIM ** (-0.5))
    scores = jnp.where(mask_in[:, None, None, :] > 0, scores, NEG)
    probs = soft_rows(scores)
    attended = jnp.einsum('ghqk,gkhd->gqhd', low(probs), values, precision=HIGH)
    attended = low_back(low(attended)).reshape(count, SEQ, D)
    branch = low_back(jnp.einsum('gsd,de->gse', attended, proj_w, precision=HIGH) + proj_b)
    return images_in + branch

def expert_rows(rows, up_w, up_b, down_w, down_b):
    rows = low_back(rows)
    hidden = low_back(jnp.einsum('bcd,df->bcf', rows, up_w, precision=HIGH) + up_b)
    active = low(jax.nn.gelu(hidden, approximate=False))
    result = jnp.einsum('bcf,fd->bcd', active, down_w, precision=HIGH) + down_b
    return low_back(low(result))

def reference(tokens, cotangent, key_mask, route_ids, priority, norm1_gain, norm1_bias, qkv_weight, query_bias, value_bias, proj_weight, proj_bias, norm2_gain, norm2_bias, router_weight, expert_up, expert_up_bias, expert_down, expert_down_bias):
    blocks = IMAGES // IMG_DEV * N_CTX
    group = math.gcd(IMAGES, max(1, 4096 // SEQ))
    ids_blocks = to_blocks(route_ids)
    prio_blocks = to_blocks(priority)
    pair_experts = jnp.concatenate([ids_blocks[..., 0], ids_blocks[..., 1]], axis=1)
    pair_prio = jnp.concatenate([prio_blocks, prio_blocks], axis=1)

    def rank_block(pieces):
        return slot_ranks(pieces[0], pieces[1])
    ranks = lax.map(rank_block, (pair_experts, pair_prio))
    kept_mask = ranks < CAP
    destination = jnp.where(kept_mask, pair_experts * CAP + ranks, EXPERTS * CAP).astype(jnp.int32)
    safe_dest = jnp.minimum(destination, EXPERTS * CAP - 1).astype(jnp.int32)
    kept_float = kept_mask.astype(jnp.float32)
    table = jax.vmap(slot_table)(destination)
    slot_tok = jnp.where(table >= 0, table % TOK_DEV, 0).astype(jnp.int32)
    slot_live = (table >= 0).astype(jnp.float32)
    slot_tok = jnp.swapaxes(slot_tok.reshape(blocks, EXPERTS, CAP), 0, 1)
    slot_live = jnp.swapaxes(slot_live.reshape(blocks, EXPERTS, CAP), 0, 1)
    attend_saved = jax.checkpoint(attend)
    expert_saved = jax.checkpoint(expert_rows)

    def forward(tokens_f, gain_one, shift_one, qkv_w, query_b, value_b, proj_w, proj_b, gain_two, shift_two, router_w, up_w, up_b, down_w, down_b):
        grouped = tokens_f.reshape(IMAGES // group, group, SEQ, D)
        masks = key_mask.reshape(IMAGES // group, group, SEQ)

        def attend_group(pieces):
            return attend_saved(pieces[0], pieces[1], gain_one, shift_one, qkv_w, query_b, value_b, proj_w, proj_b)
        middle = lax.map(attend_group, (grouped, masks)).reshape(IMAGES, SEQ, D)
        middle_blocks = to_blocks(middle)
        normed_low = low(norm_rows(middle_blocks, gain_two, shift_two))
        logits = low_back(jnp.einsum('btd,de->bte', normed_low, router_w, precision=HIGH))
        gates = soft_rows(logits)
        gate_pick = jnp.take_along_axis(gates, ids_blocks, axis=2)
        gate_pairs = jnp.concatenate([gate_pick[..., 0], gate_pick[..., 1]], axis=1)

        def per_expert(pieces):
            rows = jnp.take_along_axis(normed_low, pieces[4][:, :, None], axis=1) * pieces[5][:, :, None]
            return expert_saved(rows, pieces[0], pieces[1], pieces[2], pieces[3])
        outputs = lax.map(per_expert, (up_w, up_b, down_w, down_b, slot_tok, slot_live))
        flat_out = jnp.swapaxes(outputs, 0, 1).reshape(blocks, EXPERTS * CAP, D)
        pair_out = jnp.take_along_axis(flat_out, safe_dest[:, :, None], axis=1) * kept_float[:, :, None]
        weighted = pair_out * (gate_pairs * kept_float)[:, :, None]
        expert_sum = weighted[:, :TOK_DEV] + weighted[:, TOK_DEV:]
        return from_blocks(middle_blocks + expert_sum)
    result, pullback = jax.vjp(forward, tokens.astype(jnp.float32), norm1_gain, norm1_bias, qkv_weight.astype(jnp.float32), query_bias, value_bias, proj_weight.astype(jnp.float32), proj_bias, norm2_gain, norm2_bias, router_weight.astype(jnp.float32), expert_up.astype(jnp.float32), expert_up_bias, expert_down.astype(jnp.float32), expert_down_bias)
    grads = pullback(cotangent.astype(jnp.float32))
    return (result.astype(jnp.bfloat16), grads[0].astype(jnp.bfloat16), grads[1], grads[2], grads[3], grads[4], grads[5], grads[6], grads[7], grads[8], grads[9], grads[10], grads[11], grads[12], grads[13], grads[14])
```

```python
import jax
import jax.numpy as jnp
from jax import lax
from jax.experimental import pallas as pl
from jax.experimental.pallas import tpu as pltpu
from jax.sharding import PartitionSpec as P

HEADS = 8
EPS = 1e-06
NEG = -1e30
F32 = jnp.float32
BF16 = jnp.bfloat16
I32 = jnp.int32
LANES = 128
PAD = 16
VMEM_LIMIT = 58 * 2**20


def dot_nn(a, b):
    return lax.dot_general(a, b, (((1,), (0,)), ((), ())), preferred_element_type=F32)


def dot_nt(a, b):
    return lax.dot_general(a, b, (((1,), (1,)), ((), ())), preferred_element_type=F32)


def iota(shape, axis):
    return lax.broadcasted_iota(I32, shape, axis)


def norm_stats(v):
    centre = v - jnp.mean(v, axis=1, keepdims=True)
    inv = lax.rsqrt(jnp.mean(centre * centre, axis=1, keepdims=True) + EPS)
    return centre * inv, inv


def norm_back(gy, xhat, inv):
    return (
        gy - jnp.mean(gy, axis=1, keepdims=True) - xhat * jnp.mean(gy * xhat, axis=1, keepdims=True)
    ) * inv


def soft_gates(logits, expert_count):
    logits = jnp.where(iota(logits.shape, 1) < expert_count, logits, NEG)
    e = jnp.exp(logits - jnp.max(logits, axis=1, keepdims=True))
    return e / jnp.sum(e, axis=1, keepdims=True)


ERF = (0.254829592, -0.284496736, 1.421413741, -1.453152027, 1.061405429)
ERF_P = 0.3275911 * 0.7071067811865476


def gelu_parts(h):
    t = 1.0 / (1.0 + ERF_P * jnp.abs(h))
    e = jnp.exp(-0.5 * h * h)
    poly = 0.5 * ERF[4]
    for c in ERF[3::-1]:
        poly = poly * t + 0.5 * c
    tail = poly * t * e
    cdf = jnp.where(h >= 0, 1.0 - tail, tail)
    return h * cdf, cdf + h * (e * 0.3989422804014327)


def params(**kw):
    return pltpu.CompilerParams(vmem_limit_bytes=VMEM_LIMIT, **kw)


def cost(flops, nbytes):
    return pl.CostEstimate(flops=int(flops), bytes_accessed=int(nbytes), transcendentals=0)


SMEM_SPEC = pl.BlockSpec(memory_space=pltpu.SMEM)
VMEM_SPEC = pl.BlockSpec(memory_space=pltpu.VMEM)


def shape(dims, dtype):
    return jax.ShapeDtypeStruct(dims, dtype)


def route_call(place, ints, cotangent, expert_count, capacity):
    groups, group_rows, width = cotangent.shape
    tok = groups * group_rows
    e_rows = max(PAD, expert_count)

    def kernel(place_ref, ints_ref, cot_ref, *outs):
        row_ref, col_ref = outs[:2]
        slots = outs[2:]
        ctx, expert = place_ref[0], place_ref[1]
        vals = ints_ref[...]
        ids = (vals[0:1], vals[1:2])
        key = vals[2:3]
        keys = jnp.broadcast_to(key.astype(F32), (8, tok))
        key_col = keys.T[:, :1]
        before = (key_col < keys[:1]).astype(BF16)
        hot = [(iota((e_rows, tok), 0) == i).astype(F32) for i in ids]
        counts = dot_nn(jnp.concatenate(hot, axis=0).astype(BF16), before)
        first_total = jnp.sum(hot[0], axis=1, keepdims=True)
        ranks = (
            jnp.sum(hot[0] * counts[:e_rows], axis=0, keepdims=True),
            jnp.sum(hot[1] * (counts[e_rows:] + first_total), axis=0, keepdims=True),
        )
        dest = [
            jnp.where(r < capacity, i.astype(F32) * capacity + r, -1.0)
            for r, i in zip(ranks, ids)
        ]
        rows = jnp.concatenate(
            [dest[0], dest[1], jnp.full((6, tok), -1.0, F32)], axis=0
        )
        row_ref[...] = rows.astype(I32)
        col_ref[...] = rows.T.astype(I32)
        d0, d1 = dest[0].astype(I32), dest[1].astype(I32)
        up = jnp.concatenate([cot_ref[ctx ^ d] for d in range(groups)], axis=0)
        for d in range(expert_count):
            ids_here = iota((capacity, tok), 0) + (expert ^ d) * capacity
            pick = ((ids_here == d0) | (ids_here == d1)).astype(F32).astype(BF16)
            slots[d][...] = dot_nn(pick, up).astype(BF16)

    return pl.pallas_call(
        kernel,
        in_specs=[SMEM_SPEC, VMEM_SPEC, VMEM_SPEC],
        out_specs=[VMEM_SPEC] * (2 + expert_count),
        out_shape=[shape((8, tok), I32), shape((tok, 8), I32)]
        + [shape((capacity, width), BF16)] * expert_count,
        compiler_params=params(),
        cost_estimate=cost(4e9, 4e6),
        name="route",
    )(place, ints, cotangent)


def gather_image(pieces, i, rows):
    at = pl.ds(pl.multiple_of(i * rows, rows), rows)
    return jnp.concatenate([p[at, :] for p in pieces], axis=0).astype(F32)


def gather_mask(pieces, i, rows, body):
    cols = []
    for p in pieces:
        block = p[body : body + PAD, :LANES].astype(F32).T
        cols.append(
            jnp.sum(jnp.where(iota(block.shape, 1) == i, block, 0.0), axis=1, keepdims=True)[:rows]
        )
    return jnp.concatenate(cols, axis=0)


def head_pair(block, h, size):
    zero = jnp.zeros_like(block)
    return jnp.concatenate([block, zero] if h % 2 == 0 else [zero, block], axis=0)


def attend_call(pieces, gain, shift, qkv, qkv_t, query_bias, value_bias, images, rows):
    count = len(pieces)
    width = qkv.shape[0]
    seq = count * rows
    size = width // HEADS
    body = images * rows
    scale = size ** (-0.5)

    def kernel(*refs):
        ps = refs[:count]
        gain_ref, shift_ref, qkv_ref, qkvt_ref, qb_ref, vb_ref = refs[count : count + 6]
        outs = refs[count + 6 : 2 * count + 6]
        qt_ref, k_ref, vt_ref, lse_ref, ot = refs[2 * count + 6 :]
        i = pl.program_id(0)
        x = gather_image(ps, i, rows)
        live = gather_mask(ps, i, rows, body) > 0
        xhat, _ = norm_stats(x)
        n = (xhat * gain_ref[...] + shift_ref[...]).astype(BF16)
        qt_ref[0] = (dot_nt(qkvt_ref[:width], n) + qb_ref[...]).astype(BF16)
        k_ref[0] = dot_nn(n, qkv_ref[:, width : 2 * width]).astype(BF16)
        vt_ref[0] = (dot_nt(qkvt_ref[2 * width :], n) + vb_ref[...]).astype(BF16)
        for h in range(HEADS):
            at = slice(h * size, (h + 1) * size)
            pair = slice(h // 2 * 2 * size, (h // 2 + 1) * 2 * size)
            s = dot_nn(k_ref[0, :, pair], head_pair(qt_ref[0, at, :], h, size)) * scale
            s = jnp.where(live, s, NEG)
            top = jnp.max(s, axis=0, keepdims=True)
            e = jnp.exp(s - top)
            total = jnp.sum(e, axis=0, keepdims=True)
            lse_ref[0, h : h + 1, :] = top + jnp.log(total)
            ot[at, :] = dot_nn(vt_ref[0, at, :], (e * (1.0 / total)).astype(BF16))
        o = ot[...].T.astype(BF16)
        at = pl.ds(pl.multiple_of(i * rows, rows), rows)
        for d in range(count):
            outs[d][at, :] = o[d * rows : (d + 1) * rows]

    full = lambda a: pl.BlockSpec(a.shape, lambda i: (0,) * a.ndim)
    ins = list(pieces) + [gain, shift, qkv, qkv_t, query_bias, value_bias]
    per_image = lambda dims: pl.BlockSpec((1,) + dims, lambda i: (i, 0, 0))
    return pl.pallas_call(
        kernel,
        grid=(images,),
        in_specs=[full(a) for a in ins],
        out_specs=[pl.BlockSpec((body, width), lambda i: (0, 0))] * count
        + [per_image((width, seq)), per_image((seq, width)), per_image((width, seq)), per_image((HEADS, seq))],
        out_shape=[shape((body, width), BF16)] * count
        + [
            shape((images, width, seq), BF16),
            shape((images, seq, width), BF16),
            shape((images, width, seq), BF16),
            shape((images, HEADS, seq), F32),
        ],
        scratch_shapes=[pltpu.VMEM((width, seq), F32)],
        compiler_params=params(),
        cost_estimate=cost(8e9, 8e6),
        name="attend",
    )(*ins)


def middle_call(place, attended, pieces, proj, proj_bias, gain, shift, dest_rows, expert_count, capacity):
    count = len(attended)
    body, width = attended[0].shape
    tok = count * body

    def kernel(place_ref, *refs):
        att, ps = refs[:count], refs[count : 2 * count]
        proj_ref, pb_ref, gain_ref, shift_ref, dest_ref = refs[2 * count : 2 * count + 5]
        mid_ref, n_ref = refs[2 * count + 5 : 2 * count + 7]
        slots = refs[2 * count + 7 :]
        expert = place_ref[1]
        for d in range(count):
            at = slice(d * body, (d + 1) * body)
            mid = (
                ps[d][:body, :].astype(F32) + dot_nn(att[d][...], proj_ref[...]) + pb_ref[...]
            )
            mid_ref[at, :] = mid
            xhat, _ = norm_stats(mid)
            n_ref[at, :] = (xhat * gain_ref[...] + shift_ref[...]).astype(BF16)
        n = n_ref[...]
        d0, d1 = dest_ref[0:1, :], dest_ref[1:2, :]
        for d in range(expert_count):
            ids_here = iota((capacity, tok), 0) + (expert ^ d) * capacity
            pick = ((ids_here == d0) | (ids_here == d1)).astype(F32).astype(BF16)
            slots[d][...] = dot_nn(pick, n).astype(BF16)

    ins = list(attended) + list(pieces) + [proj, proj_bias, gain, shift, dest_rows]
    return pl.pallas_call(
        kernel,
        in_specs=[SMEM_SPEC] + [VMEM_SPEC] * len(ins),
        out_specs=[VMEM_SPEC] * (2 + expert_count),
        out_shape=[shape((tok, width), F32), shape((tok, width), BF16)]
        + [shape((capacity, width), BF16)] * expert_count,
        compiler_params=params(),
        cost_estimate=cost(4e9, 6e6),
        name="middle",
    )(place, *ins)


def expert_call(place, xs, us, router, up, up_bias, down, down_bias, expert_count):
    blocks = len(xs)
    capacity, width = xs[0].shape
    hidden_width = up.shape[1]
    total = blocks * capacity
    chunk = 512
    steps = hidden_width // chunk
    sub = capacity if capacity > 128 else total // 4
    down_rows = hidden_width + LANES

    def kernel(place_ref, *refs):
        x_refs, u_refs = refs[:blocks], refs[blocks : 2 * blocks]
        rw, up_ref, ub_ref, dn_ref, db_ref = refs[2 * blocks : 2 * blocks + 5]
        o = refs[2 * blocks + 5 :]
        out_refs, gx_refs = o[:blocks], o[blocks : 2 * blocks]
        gup_ref, gdn_ref = o[2 * blocks : 2 * blocks + 2]
        x_all, g_all, x_t, g_t, gate, out_acc, gx_acc, act, gh_all, bias_rows = o[2 * blocks + 2 :]
        j = pl.program_id(0)

        @pl.when(j == 0)
        def _():
            expert = place_ref[1]
            bias = jnp.zeros((1, width), F32)
            for b in range(blocks):
                at = slice(b * capacity, (b + 1) * capacity)
                x = x_refs[b][...]
                gates = soft_gates(dot_nn(x, rw[...]), expert_count)
                mine = jnp.sum(
                    jnp.where(iota(gates.shape, 1) == expert, gates, 0.0), axis=1, keepdims=True
                )
                g = (u_refs[b][...].astype(F32) * mine).astype(BF16)
                x_all[at, :] = x
                g_all[at, :] = g
                gate[at, :] = jnp.broadcast_to(mine, (capacity, LANES))
                bias = bias + jnp.sum(g.astype(F32), axis=0, keepdims=True)
            x_t[...] = x_all[...].T
            g_t[...] = g_all[...].T
            out_acc[...] = jnp.zeros_like(out_acc)
            gx_acc[...] = jnp.zeros_like(gx_acc)
            bias_rows[...] = jnp.where(iota((PAD, width), 0) == steps, bias, 0.0)

        w_up, w_dn = up_ref[...], dn_ref[...]
        bias = jnp.zeros((1, chunk), F32)
        for r in range(total // sub):
            at = slice(r * sub, (r + 1) * sub)
            h = dot_nn(x_all[at, :], w_up) + ub_ref[...]
            a, slope = gelu_parts(h)
            a = a.astype(BF16)
            act[at, :] = a
            out_acc[at, :] += dot_nn(a, w_dn)
            gh = (dot_nt(g_all[at, :], w_dn) * slope).astype(BF16)
            gh_all[at, :] = gh
            bias = bias + jnp.sum(gh.astype(F32), axis=0, keepdims=True)
            gx_acc[at, :] += dot_nt(gh, w_up)
        bias_rows[...] = jnp.where(iota((PAD, width), 0) == j, bias, bias_rows[...])
        gup_ref[...] = dot_nn(x_t[...], gh_all[...]).astype(BF16)
        gdn_ref[pl.ds(pl.multiple_of(j * chunk, chunk), chunk), :] = (
            dot_nn(g_t[...], act[...]).T.astype(BF16)
        )

        @pl.when(j == steps - 1)
        def _():
            gdn_ref[hidden_width : hidden_width + PAD, :] = bias_rows[...].astype(BF16)
            gdn_ref[hidden_width + PAD :, :] = jnp.zeros((LANES - PAD, width), BF16)
            for b in range(blocks):
                at = slice(b * capacity, (b + 1) * capacity)
                out = (out_acc[at, :] + db_ref[...]).astype(BF16).astype(F32)
                out_refs[b][...] = (out * gate[at, :1]).astype(BF16)
                gg = jnp.sum(out * u_refs[b][...].astype(F32), axis=1, keepdims=True)
                row = jnp.broadcast_to(gg, (capacity, LANES)).T[:PAD]
                high = row.astype(BF16).astype(F32)
                mean = (row - high).astype(BF16).astype(F32)
                k = iota(row.shape, 0)
                parts = jnp.where(
                    k == 0, high, jnp.where(k == 1, mean, jnp.where(k == 2, row - high - mean, 0.0))
                )
                gx_refs[b][:capacity, :] = gx_acc[at, :].astype(BF16)
                gx_refs[b][capacity:, :] = jnp.concatenate(
                    [parts, jnp.zeros((PAD, width - capacity), F32)], axis=1
                ).astype(BF16)

    full = lambda a: pl.BlockSpec(a.shape, lambda j: (0,) * a.ndim)
    const = lambda dims: pl.BlockSpec(dims, lambda j: (0,) * len(dims))
    return pl.pallas_call(
        kernel,
        grid=(steps,),
        in_specs=[SMEM_SPEC]
        + [full(a) for a in xs]
        + [full(a) for a in us]
        + [
            full(router),
            pl.BlockSpec((width, chunk), lambda j: (0, j)),
            pl.BlockSpec((1, chunk), lambda j: (0, j)),
            pl.BlockSpec((chunk, width), lambda j: (j, 0)),
            full(down_bias),
        ],
        out_specs=[const((capacity, width))] * blocks
        + [const((capacity + PAD, width))] * blocks
        + [pl.BlockSpec((width, chunk), lambda j: (0, j)), const((down_rows, width))],
        out_shape=[shape((capacity, width), BF16)] * blocks
        + [shape((capacity + PAD, width), BF16)] * blocks
        + [shape((width, hidden_width), BF16), shape((down_rows, width), BF16)],
        scratch_shapes=[
            pltpu.VMEM((total, width), BF16),
            pltpu.VMEM((total, width), BF16),
            pltpu.VMEM((width, total), BF16),
            pltpu.VMEM((width, total), BF16),
            pltpu.VMEM((total, LANES), F32),
            pltpu.VMEM((total, width), F32),
            pltpu.VMEM((total, width), F32),
            pltpu.VMEM((total, chunk), BF16),
            pltpu.VMEM((total, chunk), BF16),
            pltpu.VMEM((PAD, width), F32),
        ],
        compiler_params=params(),
        cost_estimate=cost(36e9, 16e6),
        name="expert",
    )(place, *xs, *us, router, up, up_bias, down, down_bias)


def slot_match(dest_ref, at, first, capacity):
    d = dest_ref[at, :]
    lanes = iota((d.shape[0], capacity), 1) + first
    return ((lanes == d[:, 0:1]) | (lanes == d[:, 1:2])).astype(F32).astype(BF16)


def output_call(place, outs, mid, dest_cols, groups):
    blocks = len(outs)
    capacity, width = outs[0].shape
    tok = mid.shape[0]
    body = tok // groups

    def kernel(place_ref, *refs):
        o_refs, (mid_ref, dest_ref, out_ref) = refs[:blocks], refs[blocks:]
        ctx, expert = place_ref[0], place_ref[1]
        for g in range(groups):
            at = slice(g * body, (g + 1) * body)
            acc = mid_ref[at, :]
            for d in range(blocks):
                acc = acc + dot_nn(
                    slot_match(dest_ref, at, (expert ^ d) * capacity, capacity), o_refs[d][...]
                )
            out_ref[ctx ^ g] = acc.astype(BF16)

    ins = list(outs) + [mid, dest_cols]
    return pl.pallas_call(
        kernel,
        in_specs=[SMEM_SPEC] + [VMEM_SPEC] * len(ins),
        out_specs=VMEM_SPEC,
        out_shape=shape((groups, body, width), BF16),
        compiler_params=params(),
        cost_estimate=cost(2e9, 6e6),
        name="output",
    )(place, *ins)


def middle_back_call(
    place, gxs, mid, normed, cotangent, dest_cols, attended, router, gain, proj, expert_count
):
    blocks = len(gxs)
    groups, body, width = cotangent.shape
    capacity = gxs[0].shape[0] - PAD
    tok = groups * body
    misc = -(-(expert_count + 3) // PAD) * PAD

    def kernel(place_ref, *refs):
        gx_refs = refs[:blocks]
        mid_ref, n_ref, cot_ref, dest_ref = refs[blocks : blocks + 4]
        att = refs[blocks + 4 : blocks + 4 + groups]
        router_ref, gain_ref, proj_ref = refs[blocks + 4 + groups : blocks + 7 + groups]
        gmid_ref = refs[blocks + 7 + groups]
        ga_refs = refs[blocks + 8 + groups : blocks + 8 + 2 * groups]
        shared_ref, branch_t, logit_t, att_all = refs[blocks + 8 + 2 * groups :]
        ctx, expert = place_ref[0], place_ref[1]
        g_gain = jnp.zeros((1, width), F32)
        g_shift = jnp.zeros((1, width), F32)
        g_proj_bias = jnp.zeros((1, width), F32)
        for g in range(groups):
            at = slice(g * body, (g + 1) * body)
            gn = jnp.zeros((body, width), F32)
            gg = jnp.zeros((body, LANES), F32)
            lane = iota((body, LANES), 1)
            for d in range(blocks):
                match = slot_match(dest_ref, at, (expert ^ d) * capacity, capacity)
                gn = gn + dot_nn(match, gx_refs[d][:capacity, :])
                parts = dot_nt(match, gx_refs[d][capacity:, :capacity])
                gg = jnp.where(
                    lane == (expert ^ d), parts[:, 0:1] + parts[:, 1:2] + parts[:, 2:3], gg
                )
            gates = soft_gates(dot_nn(n_ref[at, :], router_ref[...]), expert_count)
            logit = gates * (gg - jnp.sum(gates * gg, axis=1, keepdims=True))
            logit_t[:, at] = logit.T.astype(BF16)
            gn = gn + dot_nt(logit.astype(BF16), router_ref[...])
            xhat, inv = norm_stats(mid_ref[at, :])
            g_gain = g_gain + jnp.sum(gn * xhat, axis=0, keepdims=True)
            g_shift = g_shift + jnp.sum(gn, axis=0, keepdims=True)
            gmid = cot_ref[ctx ^ g].astype(F32) + norm_back(gn * gain_ref[...], xhat, inv)
            gmid_ref[at, :] = gmid
            branch = gmid.astype(BF16)
            g_proj_bias = g_proj_bias + jnp.sum(branch.astype(F32), axis=0, keepdims=True)
            branch_t[:, at] = branch.T
            att_all[at, :] = att[g][...]
            ga_refs[g][...] = dot_nt(branch, proj_ref[...]).astype(BF16)
        shared_ref[:width, :] = dot_nn(branch_t[...], att_all[...]).astype(BF16)
        rows = dot_nn(logit_t[...], n_ref[...])[:misc]
        k = iota((misc, width), 0)
        for s, vec in enumerate((g_gain, g_shift, g_proj_bias)):
            rows = jnp.where(k == expert_count + s, vec, rows)
        shared_ref[width:, :] = rows.astype(BF16)

    ins = (
        list(gxs) + [mid, normed, cotangent, dest_cols] + list(attended) + [router, gain, proj]
    )
    return pl.pallas_call(
        kernel,
        in_specs=[SMEM_SPEC] + [VMEM_SPEC] * len(ins),
        out_specs=[VMEM_SPEC] * (2 + groups),
        out_shape=[shape((tok, width), F32)]
        + [shape((body, width), BF16)] * groups
        + [shape((width + misc, width), BF16)],
        scratch_shapes=[
            pltpu.VMEM((width, tok), BF16),
            pltpu.VMEM((LANES, tok), BF16),
            pltpu.VMEM((tok, width), BF16),
        ],
        compiler_params=params(),
        cost_estimate=cost(5e9, 8e6),
        name="middle_back",
    )(place, *ins)


def attend_back_call(
    pieces, grads, saved, shared, gain, shift, qkv, qkv_t, value_bias, images, rows, total_rows
):
    count = len(pieces)
    width = qkv.shape[0]
    seq = count * rows
    size = width // HEADS
    body = images * rows
    scale = size ** (-0.5)
    shared_rows = shared.shape[0]

    def kernel(*refs):
        ps, gs = refs[:count], refs[count : 2 * count]
        qt_ref, k_ref, lse_ref, shared_ref, gain_ref, shift_ref, qkv_ref, qkvt_ref, vb_ref = refs[
            2 * count : 2 * count + 9
        ]
        outs = refs[2 * count + 9 : 3 * count + 9]
        flat_ref, gt, w_acc, gain_acc, shift_acc, qb_acc, vb_acc = refs[3 * count + 9 :]
        i = pl.program_id(0)
        x = gather_image(ps, i, rows)
        live = gather_mask(ps, i, rows, body) > 0
        xhat, inv = norm_stats(x)
        n = (xhat * gain_ref[...] + shift_ref[...]).astype(BF16)
        kt = dot_nt(qkvt_ref[width : 2 * width], n).astype(BF16)
        v = (dot_nn(n, qkv_ref[:, 2 * width :]) + vb_ref[...]).astype(BF16)
        dot_ = gather_image(gs, i, rows).T.astype(BF16)
        k = k_ref[0]
        qt = qt_ref[0]
        for h in range(HEADS):
            at = slice(h * size, (h + 1) * size)
            pair = slice(h // 2 * 2 * size, (h // 2 + 1) * 2 * size)
            qh, kh, gh = qt[at], kt[at], dot_[at]
            s = dot_nn(k[:, pair], head_pair(qh, h, size)) * scale
            p = jnp.exp(jnp.where(live, s, NEG) - lse_ref[0, h : h + 1, :])
            dp = dot_nn(v[:, pair], head_pair(gh, h, size))
            ds = (p * (dp - jnp.sum(p * dp, axis=0, keepdims=True))).astype(BF16)
            gt[at, :] = (dot_nn(kh, ds) * scale).astype(BF16)
            gt[width + h * size : width + (h + 1) * size, :] = (dot_nt(qh, ds) * scale).astype(BF16)
            gt[2 * width + h * size : 2 * width + (h + 1) * size, :] = dot_nt(
                gh, p.astype(BF16)
            ).astype(BF16)
        gall = gt[...]
        gw = dot_nn(gall, n)
        gn = dot_nn(qkv_ref[...], gall).T
        qb = gall[:width].astype(F32)
        vb = gall[2 * width :].astype(F32)
        g_gain = jnp.sum(gn * xhat, axis=0, keepdims=True)
        g_shift = jnp.sum(gn, axis=0, keepdims=True)

        @pl.when(i == 0)
        def _():
            w_acc[...] = jnp.zeros_like(w_acc)
            gain_acc[...] = jnp.zeros_like(gain_acc)
            shift_acc[...] = jnp.zeros_like(shift_acc)
            qb_acc[...] = jnp.zeros_like(qb_acc)
            vb_acc[...] = jnp.zeros_like(vb_acc)

        w_acc[...] += gw
        gain_acc[...] += g_gain
        shift_acc[...] += g_shift
        qb_acc[...] += qb
        vb_acc[...] += vb
        gin = norm_back(gn * gain_ref[...], xhat, inv).astype(BF16)
        at = pl.ds(pl.multiple_of(i * rows, rows), rows)
        for d in range(count):
            outs[d][at, :] = gin[d * rows : (d + 1) * rows]

        @pl.when(i == images - 1)
        def _():
            flat_ref[: 3 * width, :] = w_acc[...].astype(BF16)
            flat_ref[3 * width : 3 * width + shared_rows, :] = shared_ref[...]
            sums = [
                jnp.broadcast_to(jnp.sum(a[...], axis=1, keepdims=True), (width, LANES)).T[:1]
                for a in (qb_acc, vb_acc)
            ]
            k16 = iota((PAD, width), 0)
            vecs = jnp.zeros((PAD, width), F32)
            for s, vec in enumerate((gain_acc[...], shift_acc[...], *sums)):
                vecs = jnp.where(k16 == s, vec, vecs)
            flat_ref[3 * width + shared_rows : 3 * width + shared_rows + PAD, :] = vecs.astype(BF16)
            left = total_rows - 3 * width - shared_rows - PAD
            if left:
                flat_ref[total_rows - left :, :] = jnp.zeros((left, width), BF16)

    full = lambda a: pl.BlockSpec(a.shape, lambda i: (0,) * a.ndim)
    const = lambda dims: pl.BlockSpec(dims, lambda i: (0,) * len(dims))
    per_image = lambda a: pl.BlockSpec((1,) + a.shape[1:], lambda i: (i, 0, 0))
    rest = [shared, gain, shift, qkv, qkv_t, value_bias]
    return pl.pallas_call(
        kernel,
        grid=(images,),
        in_specs=[full(a) for a in pieces]
        + [full(a) for a in grads]
        + [per_image(a) for a in saved]
        + [full(a) for a in rest],
        out_specs=[const((body, width))] * count + [const((total_rows, width))],
        out_shape=[shape((body, width), BF16)] * count + [shape((total_rows, width), BF16)],
        scratch_shapes=[
            pltpu.VMEM((3 * width, seq), BF16),
            pltpu.VMEM((3 * width, width), F32),
            pltpu.VMEM((1, width), F32),
            pltpu.VMEM((1, width), F32),
            pltpu.VMEM((width, seq), F32),
            pltpu.VMEM((width, seq), F32),
        ],
        compiler_params=params(),
        cost_estimate=cost(16e9, 10e6),
        name="attend_back",
    )(*pieces, *grads, *saved, *rest)


def input_call(place, gmid, gins):
    groups = len(gins)
    body, width = gins[0].shape

    def kernel(place_ref, gmid_ref, *refs):
        ctx = place_ref[0]
        for g in range(groups):
            refs[groups][ctx ^ g] = (
                gmid_ref[g * body : (g + 1) * body, :] + refs[g][...].astype(F32)
            ).astype(BF16)

    return pl.pallas_call(
        kernel,
        in_specs=[SMEM_SPEC] + [VMEM_SPEC] * (1 + groups),
        out_specs=VMEM_SPEC,
        out_shape=shape((groups, body, width), BF16),
        compiler_params=params(),
        cost_estimate=cost(1e6, 4e6),
        name="input",
    )(place, gmid, *gins)


def spread_call(place, own, other, scale_to):
    groups, rows, width = own.shape

    def kernel(place_ref, own_ref, other_ref, out_ref):
        out_ref[0, 0] = jnp.where(pl.program_id(0) == 0, own_ref[0], other_ref[0]).astype(F32)

    def out_map(h, g, place_ref):
        return (place_ref[2] ^ h, place_ref[0] ^ g, 0, 0)

    return pl.pallas_call(
        kernel,
        grid_spec=pltpu.PrefetchScalarGridSpec(
            num_scalar_prefetch=1,
            grid=(2, groups),
            in_specs=[
                pl.BlockSpec((1, rows, width), lambda h, g, p: (g, 0, 0)),
                pl.BlockSpec((1, rows, width), lambda h, g, p: (g, 0, 0)),
            ],
            out_specs=pl.BlockSpec((1, 1, rows, width), out_map),
        ),
        out_shape=shape((2, groups, rows, width), F32),
        compiler_params=params(),
        cost_estimate=cost(1e6, 2 * groups * rows * width * 8),
        name="spread",
    )(place, own, other).reshape(2 * groups * rows, width)


def swap(x, axis, d, size):
    return lax.ppermute(x, axis, [(i, i ^ d) for i in range(size)])


def pick(x, i):
    return lax.dynamic_index_in_dim(x, i, 0, keepdims=False)


def add_all(parts):
    acc = parts[0].astype(F32)
    for p in parts[1:]:
        acc = acc + p.astype(F32)
    return acc.astype(BF16)


def reduce_rows(x, ctx, core, n_ctx, n_dp):
    rows, width = x.shape
    x = x.reshape(n_dp, n_ctx, rows // (n_dp * n_ctx), width)
    parts = [pick(x, core)]
    for d in range(1, n_dp):
        parts.append(swap(pick(x, core ^ d), "dp", d, n_dp))
    x = add_all(parts)
    parts = [pick(x, ctx)]
    for d in range(1, n_ctx):
        parts.append(swap(pick(x, ctx ^ d), "ctx", d, n_ctx))
    return add_all(parts)


def gather_ctx(x, n_ctx):
    return jnp.stack([x] + [swap(x, "ctx", d, n_ctx) for d in range(1, n_ctx)])


def local(
    mesh_sizes,
    tokens,
    cotangent,
    key_mask,
    route_ids,
    priority,
    norm1_gain,
    norm1_bias,
    qkv_weight,
    query_bias,
    value_bias,
    proj_weight,
    proj_bias,
    norm2_gain,
    norm2_bias,
    router_weight,
    expert_up,
    expert_up_bias,
    expert_down,
    expert_down_bias,
):
    n_expert, n_ctx, n_dp = mesh_sizes
    images_all, rows, width = tokens.shape
    tok = images_all * rows
    images = images_all // n_ctx
    body = images * rows
    expert_count = router_weight.shape[1]
    capacity = max(2, 2 * tok // expert_count)
    ctx, expert, core = (lax.axis_index(a) for a in ("ctx", "expert", "dp"))
    place = jnp.stack([ctx, expert, core]).astype(I32)

    tok4 = tokens.reshape(n_ctx, body, width)
    mask4 = jnp.pad(
        key_mask.reshape(n_ctx, images, rows).astype(BF16),
        ((0, 0), (0, PAD - images), (0, width - rows)),
    )
    both = jnp.concatenate([tok4, mask4], axis=1)
    mine = [pick(both, ctx ^ d) for d in range(n_ctx)]
    pieces = [mine[0]] + [swap(mine[d], "ctx", d, n_ctx) for d in range(1, n_ctx)]

    order = jnp.arange(tok, dtype=I32).reshape(n_ctx, body)
    ints4 = jnp.stack(
        [
            route_ids[..., 0].reshape(n_ctx, body),
            route_ids[..., 1].reshape(n_ctx, body),
            priority.reshape(n_ctx, body) * tok + order,
        ],
        axis=1,
    )
    ints = jnp.concatenate([pick(ints4, ctx ^ d) for d in range(n_ctx)], axis=1)
    ints = jnp.pad(ints, ((0, 5), (0, 0)))
    cot4 = cotangent.reshape(n_ctx, body, width)
    dest_rows, dest_cols, *u_send = route_call(place, ints, cot4, expert_count, capacity)
    us = [u_send[0]] + [swap(u_send[d], "expert", d, n_expert) for d in range(1, n_expert)]

    row = lambda v: v.reshape(1, -1)
    col = lambda v: v.reshape(-1, 1)
    qkv_t = qkv_weight.T
    att = attend_call(
        pieces, row(norm1_gain), row(norm1_bias), qkv_weight, qkv_t, col(query_bias), col(value_bias),
        images, rows,
    )
    att_out, (q_t, k, v_t, lse) = att[:n_ctx], att[n_ctx:]
    attended = [att_out[0]] + [swap(att_out[d], "ctx", d, n_ctx) for d in range(1, n_ctx)]

    mid, normed2, *x_send = middle_call(
        place, attended, mine, proj_weight, row(proj_bias), row(norm2_gain), row(norm2_bias), dest_rows,
        expert_count, capacity,
    )
    xs = [x_send[0]] + [swap(x_send[d], "expert", d, n_expert) for d in range(1, n_expert)]

    router = jnp.pad(router_weight, ((0, 0), (0, LANES - expert_count)))
    res = expert_call(
        place, xs, us, router, expert_up[0], expert_up_bias, expert_down[0], expert_down_bias, expert_count
    )
    out_send, gx_send = res[:n_expert], res[n_expert : 2 * n_expert]
    grad_up, grad_down = res[2 * n_expert :]

    gxs = [gx_send[0]] + [swap(gx_send[d], "expert", d, n_expert) for d in range(1, n_expert)]
    grad_mid, *rest = middle_back_call(
        place, gxs, mid, normed2, cot4, dest_cols, attended, router, row(norm2_gain), proj_weight, expert_count
    )
    ga_send, shared = rest[:n_ctx], rest[n_ctx]
    gas = [ga_send[0]] + [swap(ga_send[d], "ctx", d, n_ctx) for d in range(1, n_ctx)]

    outs = [out_send[0]] + [swap(out_send[d], "expert", d, n_expert) for d in range(1, n_expert)]
    block_out = output_call(place, outs, mid, dest_cols, n_ctx)

    used = 3 * width + shared.shape[0] + PAD
    total_rows = -(-used // LANES) * LANES
    *gin_send, flat = attend_back_call(
        pieces, gas, (q_t, k, lse), shared, row(norm1_gain), row(norm1_bias), qkv_weight, qkv_t,
        row(value_bias), images, rows, total_rows,
    )
    gins = [gin_send[0]] + [swap(gin_send[d], "ctx", d, n_ctx) for d in range(1, n_ctx)]
    input_grad = input_call(place, grad_mid, gins)

    spreads = []
    for g in (grad_up, grad_down):
        part = gather_ctx(reduce_rows(g, ctx, core, n_ctx, n_dp), n_ctx)
        spreads.append(spread_call(place, part, swap(part, "dp", 1, n_dp), F32))
    grad_up, grad_down = spreads
    hidden_width = grad_up.shape[1]
    bias_rows = hidden_width // 512
    grad_up_bias = grad_down[hidden_width : hidden_width + bias_rows].reshape(1, hidden_width)
    grad_down_bias = grad_down[hidden_width + bias_rows : hidden_width + bias_rows + 1]
    grad_down = grad_down[:hidden_width]

    share = width // n_expert
    part = reduce_rows(flat, ctx, core, n_ctx, n_dp)
    part = part.reshape(part.shape[0], n_expert, share).swapaxes(0, 1)
    part = add_all(
        [pick(part, expert)]
        + [swap(pick(part, expert ^ d), "expert", d, n_expert) for d in range(1, n_expert)]
    )
    part = gather_ctx(part, n_ctx)
    whole = spread_call(place, part, swap(part, "dp", 1, n_dp), F32)
    at = 3 * width
    grad_qkv = whole[:at].T
    grad_proj = whole[at : at + width].T
    at += width
    grad_router = whole[at : at + expert_count].T
    g2_gain, g2_bias, g_proj_bias = (whole[at + expert_count + s] for s in range(3))
    at = 3 * width + shared.shape[0]
    g1_gain, g1_bias, g_query_bias, g_value_bias = (whole[at + s] for s in range(4))
    return (
        block_out.reshape(tokens.shape),
        input_grad.reshape(tokens.shape),
        g1_gain,
        g1_bias,
        grad_qkv,
        g_query_bias,
        g_value_bias,
        grad_proj,
        g_proj_bias,
        g2_gain,
        g2_bias,
        grad_router,
        grad_up[None],
        grad_up_bias,
        grad_down[None],
        grad_down_bias,
    )


def solution(mesh):
    images = P(("expert", "dp"), "ctx", None)
    ints = P(("expert", "dp"), "ctx")
    placed = (images, images, ints, images, ints) + (P(),) * 10 + (
        P("expert", None, None),
        P("expert", None),
        P("expert", None, None),
        P("expert", None),
    )
    sizes = tuple(mesh.shape[a] for a in ("expert", "ctx", "dp"))

    def run(*args):
        return local(sizes, *args)

    return jax.shard_map(
        run,
        mesh=mesh,
        in_specs=placed,
        out_specs=(
            images,
            images,
            P("expert"),
            P("expert"),
            P("expert", None),
            P("expert"),
            P("expert"),
            P("expert", None),
            P("expert"),
            P("expert"),
            P("expert"),
            P("expert", None),
            P("expert", None, None),
            P("expert", None),
            P("expert", None, None),
            P("expert", None),
        ),
        check_vma=False,
    )
```

```python
import jax
import jax.numpy as jnp
from jax import lax
from jax.experimental import pallas as pl
from jax.experimental.pallas import tpu as pltpu
from jax.sharding import PartitionSpec as P

HEADS = 8
EPS = 1e-06
NEG = -1e30
F32 = jnp.float32
BF16 = jnp.bfloat16
I32 = jnp.int32
LANES = 128
PAD = 16
VMEM_LIMIT = 58 * 2**20
EXPERT_CALLS = 4


def dot_nn(a, b):
    return lax.dot_general(a, b, (((1,), (0,)), ((), ())), preferred_element_type=F32)


def dot_nt(a, b):
    return lax.dot_general(a, b, (((1,), (1,)), ((), ())), preferred_element_type=F32)


def iota(shape, axis):
    return lax.broadcasted_iota(I32, shape, axis)


def norm_stats(v):
    centre = v - jnp.mean(v, axis=1, keepdims=True)
    inv = lax.rsqrt(jnp.mean(centre * centre, axis=1, keepdims=True) + EPS)
    return centre * inv, inv


def norm_back(gy, xhat, inv):
    return (
        gy - jnp.mean(gy, axis=1, keepdims=True) - xhat * jnp.mean(gy * xhat, axis=1, keepdims=True)
    ) * inv


def soft_gates(logits, expert_count):
    logits = jnp.where(iota(logits.shape, 1) < expert_count, logits, NEG)
    e = jnp.exp(logits - jnp.max(logits, axis=1, keepdims=True))
    return e / jnp.sum(e, axis=1, keepdims=True)


ERF = (0.254829592, -0.284496736, 1.421413741, -1.453152027, 1.061405429)
ERF_P = 0.3275911 * 0.7071067811865476


def gelu_parts(h):
    t = 1.0 / (1.0 + ERF_P * jnp.abs(h))
    e = jnp.exp(-0.5 * h * h)
    poly = 0.5 * ERF[4]
    for c in ERF[3::-1]:
        poly = poly * t + 0.5 * c
    tail = poly * t * e
    cdf = jnp.where(h >= 0, 1.0 - tail, tail)
    return h * cdf, cdf + h * (e * 0.3989422804014327)


def params(**kw):
    return pltpu.CompilerParams(vmem_limit_bytes=VMEM_LIMIT, **kw)


def takes(us):
    return pl.CostEstimate(flops=int(us * 1.15e9), bytes_accessed=1 << 17, transcendentals=0)


ANY_SPEC = pl.BlockSpec(memory_space=pl.ANY)
SMEM_SPEC = pl.BlockSpec(memory_space=pltpu.SMEM)
VMEM_SPEC = pl.BlockSpec(memory_space=pltpu.VMEM)


def shape(dims, dtype):
    return jax.ShapeDtypeStruct(dims, dtype)


def route_call(place, ints, cotangent, expert_count, capacity):
    groups, group_rows, width = cotangent.shape
    tok = groups * group_rows
    e_rows = max(PAD, expert_count)

    def kernel(place_ref, ints_ref, cot_ref, *outs):
        row_ref, col_ref = outs[:2]
        slots = outs[2:]
        ctx, expert = place_ref[0], place_ref[1]
        vals = ints_ref[...]
        ids = (vals[0:1], vals[1:2])
        key = vals[2:3]
        keys = jnp.broadcast_to(key.astype(F32), (8, tok))
        key_col = keys.T[:, :1]
        before = (key_col < keys[:1]).astype(BF16)
        hot = [(iota((e_rows, tok), 0) == i).astype(F32) for i in ids]
        counts = dot_nn(jnp.concatenate(hot, axis=0).astype(BF16), before)
        first_total = jnp.sum(hot[0], axis=1, keepdims=True)
        ranks = (
            jnp.sum(hot[0] * counts[:e_rows], axis=0, keepdims=True),
            jnp.sum(hot[1] * (counts[e_rows:] + first_total), axis=0, keepdims=True),
        )
        dest = [
            jnp.where(r < capacity, i.astype(F32) * capacity + r, -1.0)
            for r, i in zip(ranks, ids)
        ]
        rows = jnp.concatenate(
            [dest[0], dest[1], jnp.full((6, tok), -1.0, F32)], axis=0
        )
        row_ref[...] = rows.astype(I32)
        col_ref[...] = rows.T.astype(I32)
        d0, d1 = dest[0].astype(I32), dest[1].astype(I32)
        up = jnp.concatenate([cot_ref[ctx ^ d] for d in range(groups)], axis=0)
        for e in range(expert_count):
            ids_here = iota((capacity, tok), 0) + e * capacity
            pick = ((ids_here == d0) | (ids_here == d1)).astype(F32).astype(BF16)
            slots[0][e] = dot_nn(pick, up).astype(BF16)
        slots[1][0] = slots[0][expert]

    return pl.pallas_call(
        kernel,
        in_specs=[SMEM_SPEC, VMEM_SPEC, VMEM_SPEC],
        out_specs=[VMEM_SPEC] * 4,
        out_shape=[
            shape((8, tok), I32),
            shape((tok, 8), I32),
            shape((expert_count, capacity, width), BF16),
            shape((1, capacity, width), BF16),
        ],
        compiler_params=params(),
        cost_estimate=takes(4),
        name="route",
    )(place, ints, cotangent)


def gather_image(pieces, i, rows):
    at = pl.ds(pl.multiple_of(i * rows, rows), rows)
    return jnp.concatenate([p[at, :] for p in pieces], axis=0).astype(F32)


def gather_mask(pieces, i, rows, body):
    cols = []
    for p in pieces:
        block = p[body : body + PAD, :LANES].astype(F32).T
        cols.append(
            jnp.sum(jnp.where(iota(block.shape, 1) == i, block, 0.0), axis=1, keepdims=True)[:rows]
        )
    return jnp.concatenate(cols, axis=0)


def head_pair(block, h, size):
    zero = jnp.zeros_like(block)
    return jnp.concatenate([block, zero] if h % 2 == 0 else [zero, block], axis=0)


def attend_call(pieces, gain, shift, qkv, qkv_t, query_bias, value_bias, images, rows, after):
    count = len(pieces)
    width = qkv.shape[0]
    seq = count * rows
    size = width // HEADS
    body = images * rows
    scale = size ** (-0.5)

    def kernel(*refs):
        ps = refs[:count]
        gain_ref, shift_ref, qkv_ref, qkvt_ref, qb_ref, vb_ref = refs[count : count + 6]
        outs = refs[count + 7 : 2 * count + 7]
        qt_ref, k_ref, vt_ref, lse_ref, ot = refs[2 * count + 7 :]
        i = pl.program_id(0)
        x = gather_image(ps, i, rows)
        live = gather_mask(ps, i, rows, body) > 0
        xhat, _ = norm_stats(x)
        n = (xhat * gain_ref[...] + shift_ref[...]).astype(BF16)
        qt_ref[0] = (dot_nt(qkvt_ref[:width], n) + qb_ref[...]).astype(BF16)
        k_ref[0] = dot_nn(n, qkv_ref[:, width : 2 * width]).astype(BF16)
        vt_ref[0] = (dot_nt(qkvt_ref[2 * width :], n) + vb_ref[...]).astype(BF16)
        for h in range(HEADS):
            at = slice(h * size, (h + 1) * size)
            pair = slice(h // 2 * 2 * size, (h // 2 + 1) * 2 * size)
            s = dot_nn(k_ref[0, :, pair], head_pair(qt_ref[0, at, :], h, size)) * scale
            s = jnp.where(live, s, NEG)
            top = jnp.max(s, axis=0, keepdims=True)
            e = jnp.exp(s - top)
            total = jnp.sum(e, axis=0, keepdims=True)
            lse_ref[0, h : h + 1, :] = top + jnp.log(total)
            ot[at, :] = dot_nn(vt_ref[0, at, :], (e * (1.0 / total)).astype(BF16))
        o = ot[...].T.astype(BF16)
        at = pl.ds(pl.multiple_of(i * rows, rows), rows)
        for d in range(count):
            outs[d][at, :] = o[d * rows : (d + 1) * rows]

    full = lambda a: pl.BlockSpec(a.shape, lambda i: (0,) * a.ndim)
    ins = list(pieces) + [gain, shift, qkv, qkv_t, query_bias, value_bias]
    per_image = lambda dims: pl.BlockSpec((1,) + dims, lambda i: (i, 0, 0))
    return pl.pallas_call(
        kernel,
        grid=(images,),
        in_specs=[full(a) for a in ins] + [ANY_SPEC],
        out_specs=[pl.BlockSpec((body, width), lambda i: (0, 0))] * count
        + [per_image((width, seq)), per_image((seq, width)), per_image((width, seq)), per_image((HEADS, seq))],
        out_shape=[shape((body, width), BF16)] * count
        + [
            shape((images, width, seq), BF16),
            shape((images, seq, width), BF16),
            shape((images, width, seq), BF16),
            shape((images, HEADS, seq), F32),
        ],
        scratch_shapes=[pltpu.VMEM((width, seq), F32)],
        compiler_params=params(),
        cost_estimate=takes(13),
        name="attend",
    )(*ins, after)


def middle_call(place, attended, pieces, proj, proj_bias, gain, shift, dest_rows, expert_count, capacity):
    count = len(attended)
    body, width = attended[0].shape
    tok = count * body

    def kernel(place_ref, *refs):
        att, ps = refs[:count], refs[count : 2 * count]
        proj_ref, pb_ref, gain_ref, shift_ref, dest_ref = refs[2 * count : 2 * count + 5]
        mid_ref, n_ref = refs[2 * count + 5 : 2 * count + 7]
        slots = refs[2 * count + 7 :]
        expert = place_ref[1]
        for d in range(count):
            at = slice(d * body, (d + 1) * body)
            mid = (
                ps[d][:body, :].astype(F32) + dot_nn(att[d][...], proj_ref[...]) + pb_ref[...]
            )
            mid_ref[at, :] = mid
            xhat, _ = norm_stats(mid)
            n_ref[at, :] = (xhat * gain_ref[...] + shift_ref[...]).astype(BF16)
        n = n_ref[...]
        d0, d1 = dest_ref[0:1, :], dest_ref[1:2, :]
        for d in range(expert_count):
            ids_here = iota((capacity, tok), 0) + (expert ^ d) * capacity
            pick = ((ids_here == d0) | (ids_here == d1)).astype(F32).astype(BF16)
            slots[d][...] = dot_nn(pick, n).astype(BF16)

    ins = list(attended) + list(pieces) + [proj, proj_bias, gain, shift, dest_rows]
    return pl.pallas_call(
        kernel,
        in_specs=[SMEM_SPEC] + [VMEM_SPEC] * len(ins),
        out_specs=[VMEM_SPEC] * (2 + expert_count),
        out_shape=[shape((tok, width), F32), shape((tok, width), BF16)]
        + [shape((capacity, width), BF16)] * expert_count,
        compiler_params=params(),
        cost_estimate=takes(5),
        name="middle",
    )(place, *ins)


def expert_call(
    place, xs, upstream, first, router, up, up_bias, down, down_bias, results, partial, last, expert_count, n_ctx, n_dp,
    after,
):
    blocks = len(xs)
    capacity, width = xs[0].shape
    hidden_width = up.shape[1]
    total = blocks * capacity
    chunk = width
    steps = hidden_width // chunk
    pieces = n_ctx * n_dp
    per_step = pieces // steps
    part = chunk // per_step
    piece_rows = 2 * part + PAD
    sub = min(total, 384)
    has_partial = partial is not None
    ins = list(xs) + [upstream, router, up, up_bias, down, down_bias]
    ins += [partial] * has_partial + ([] if results is None else [results])
    n_in = len(ins) + len(after)

    def kernel(place_ref, *refs):
        x_refs, u_ref = refs[:blocks], refs[blocks]
        rw, up_ref, ub_ref, dn_ref, db_ref = refs[blocks + 1 : blocks + 6]
        before = refs[blocks + 6]
        o = refs[n_in:]
        out_ref, gx_refs = o[0], o[1 : 1 + blocks]
        grad_refs = o[1 + blocks : 2 + blocks + last]
        x_all, g_all, x_t, g_t, gate, out_acc, gx_acc, act, gh_all, down_bias_sum = o[
            2 + blocks + last :
        ]
        j = pl.program_id(0)
        slots = [lax.rem(place_ref[1] ^ (first + b), blocks) for b in range(blocks)]

        @pl.when(j == 0)
        def _():
            expert = place_ref[1]
            bias = jnp.zeros((1, width), F32)
            for b in range(blocks):
                at = slice(b * capacity, (b + 1) * capacity)
                x = x_refs[b][...]
                gates = soft_gates(dot_nn(x, rw[...]), expert_count)
                mine = jnp.sum(
                    jnp.where(iota(gates.shape, 1) == expert, gates, 0.0), axis=1, keepdims=True
                )
                g = (u_ref[slots[b]].astype(F32) * mine).astype(BF16)
                x_all[at, :] = x
                g_all[at, :] = g
                gate[at, :] = jnp.broadcast_to(mine, (capacity, LANES))
                bias = bias + jnp.sum(g.astype(F32), axis=0, keepdims=True)
            x_t[...] = x_all[...].T
            g_t[...] = g_all[...].T
            out_acc[...] = jnp.zeros_like(out_acc)
            gx_acc[...] = jnp.zeros_like(gx_acc)
            down_bias_sum[...] = bias

        w_up, w_dn = up_ref[...], dn_ref[...]
        bias = jnp.zeros((1, chunk), F32)
        for r in range(total // sub):
            at = slice(r * sub, (r + 1) * sub)
            h = dot_nn(x_all[at, :], w_up) + ub_ref[...]
            a, slope = gelu_parts(h)
            a = a.astype(BF16)
            act[at, :] = a
            out_acc[at, :] += dot_nn(a, w_dn)
            gh = (dot_nt(g_all[at, :], w_dn) * slope).astype(BF16)
            gh_all[at, :] = gh
            bias = bias + jnp.sum(gh.astype(F32), axis=0, keepdims=True)
            gx_acc[at, :] += dot_nt(gh, w_up)
        g_up = dot_nn(x_t[...], gh_all[...])
        g_dn = dot_nn(g_t[...], act[...]).T
        row = iota((PAD, width), 0)
        extra = jnp.where(row == 0, bias, 0.0)
        extra = jnp.where((row == 1) & (j == 0), down_bias_sum[...], extra)
        for k in range(per_step):
            vals = (
                g_up[k * part : (k + 1) * part],
                g_dn[k * part : (k + 1) * part],
                extra if k == 0 else jnp.zeros_like(extra),
            )
            if has_partial:
                vals = tuple(
                    v + before[k, at, :].astype(F32)
                    for v, at in zip(vals, (slice(0, part), slice(part, 2 * part), slice(2 * part, None)))
                )
            vals = tuple(v.astype(BF16) for v in vals)

            def put(ref, slot):
                ref[slot, :part, :] = vals[0]
                ref[slot, part : 2 * part, :] = vals[1]
                ref[slot, 2 * part :, :] = vals[2]

            if not last:
                put(grad_refs[0], k)
            else:
                piece = j * per_step + k
                slot = lax.rem(piece, n_ctx) ^ place_ref[0]
                stay = piece // n_ctx == place_ref[2]

                @pl.when(stay)
                def _():
                    put(grad_refs[0], slot)

                @pl.when(jnp.logical_not(stay))
                def _():
                    put(grad_refs[1], slot)

        @pl.when(j == steps - 1)
        def _():
            for b in range(blocks):
                at = slice(b * capacity, (b + 1) * capacity)
                out = (out_acc[at, :] + db_ref[...]).astype(BF16).astype(F32)
                out_ref[slots[b]] = (out * gate[at, :1]).astype(BF16)
                gg = jnp.sum(out * u_ref[slots[b]].astype(F32), axis=1, keepdims=True)
                line = jnp.broadcast_to(gg, (capacity, LANES)).T[:PAD]
                high = line.astype(BF16).astype(F32)
                mean = (line - high).astype(BF16).astype(F32)
                k = iota(line.shape, 0)
                parts = jnp.where(
                    k == 0, high, jnp.where(k == 1, mean, jnp.where(k == 2, line - high - mean, 0.0))
                )
                gx_refs[b][:capacity, :] = gx_acc[at, :].astype(BF16)
                gx_refs[b][capacity:, :] = jnp.concatenate(
                    [parts, jnp.zeros((PAD, width - capacity), F32)], axis=1
                ).astype(BF16)

    full = lambda a: pl.BlockSpec(a.shape, lambda j, p: (0,) * a.ndim)
    const = lambda dims: pl.BlockSpec(dims, lambda j, p: (0,) * len(dims))
    blocks_of = pl.BlockSpec((blocks, capacity, width), lambda j, p: ((p[1] ^ first) // blocks, 0, 0))
    step_pieces = pl.BlockSpec((per_step, piece_rows, width), lambda j, p: (j, 0, 0))
    specs = (
        [full(a) for a in xs]
        + [full(upstream) if upstream.shape[0] == blocks else blocks_of]
        + [
            full(router),
            pl.BlockSpec((width, chunk), lambda j, p: (0, j)),
            pl.BlockSpec((1, chunk), lambda j, p: (0, j)),
            pl.BlockSpec((chunk, width), lambda j, p: (j, 0)),
            full(down_bias),
        ]
        + [step_pieces] * has_partial
        + [ANY_SPEC] * (results is not None)
    )
    if last:
        grad_specs = [const((n_ctx, piece_rows, width))] * n_dp
        grad_shapes = [shape((n_ctx, piece_rows, width), BF16)] * n_dp
    else:
        grad_specs = [step_pieces]
        grad_shapes = [shape((pieces, piece_rows, width), BF16)]
    return pl.pallas_call(
        kernel,
        grid_spec=pltpu.PrefetchScalarGridSpec(
            num_scalar_prefetch=1,
            grid=(steps,),
            in_specs=specs + [ANY_SPEC] * len(after),
            out_specs=[blocks_of] + [const((capacity + PAD, width))] * blocks + grad_specs,
            scratch_shapes=[
                pltpu.VMEM((total, width), BF16),
                pltpu.VMEM((total, width), BF16),
                pltpu.VMEM((width, total), BF16),
                pltpu.VMEM((width, total), BF16),
                pltpu.VMEM((total, LANES), F32),
                pltpu.VMEM((total, width), F32),
                pltpu.VMEM((total, width), F32),
                pltpu.VMEM((total, chunk), BF16),
                pltpu.VMEM((total, chunk), BF16),
                pltpu.VMEM((1, width), F32),
            ],
        ),
        out_shape=[shape((expert_count, capacity, width), BF16)]
        + [shape((capacity + PAD, width), BF16)] * blocks
        + grad_shapes,
        input_output_aliases={} if results is None else {len(ins): 0},
        compiler_params=params(),
        cost_estimate=takes(13),
        name="expert",
    )(place, *ins, *after)


def slot_match(dest_ref, at, first, capacity):
    d = dest_ref[at, :]
    lanes = iota((d.shape[0], capacity), 1) + first
    return ((lanes == d[:, 0:1]) | (lanes == d[:, 1:2])).astype(F32).astype(BF16)


def output_call(place, results, mid, dest_cols, groups):
    blocks, capacity, width = results.shape
    tok = mid.shape[0]
    body = tok // groups

    def kernel(place_ref, o_ref, mid_ref, dest_ref, out_ref):
        for g in range(groups):
            at = slice(g * body, (g + 1) * body)
            acc = mid_ref[at, :]
            for e in range(blocks):
                acc = acc + dot_nn(slot_match(dest_ref, at, e * capacity, capacity), o_ref[e])
            out_ref[place_ref[0] ^ g] = acc.astype(BF16)

    return pl.pallas_call(
        kernel,
        in_specs=[SMEM_SPEC] + [VMEM_SPEC] * 3,
        out_specs=VMEM_SPEC,
        out_shape=shape((groups, body, width), BF16),
        compiler_params=params(),
        cost_estimate=takes(5),
        name="output",
    )(place, results, mid, dest_cols)


def middle_back_call(
    place, gxs, mid, normed, cotangent, dest_cols, attended, router, gain, proj, expert_count, after
):
    blocks = len(gxs)
    groups, body, width = cotangent.shape
    capacity = gxs[0].shape[0] - PAD
    tok = groups * body
    misc = -(-(expert_count + 3) // PAD) * PAD

    def kernel(place_ref, *refs):
        gx_refs = refs[:blocks]
        mid_ref, n_ref, cot_ref, dest_ref = refs[blocks : blocks + 4]
        att = refs[blocks + 4 : blocks + 4 + groups]
        router_ref, gain_ref, proj_ref = refs[blocks + 4 + groups : blocks + 7 + groups]
        refs = refs[blocks + 7 + groups + len(after) :]
        gmid_ref, ga_refs = refs[0], refs[1 : 1 + groups]
        shared_ref, branch_t, logit_t, att_all = refs[1 + groups :]
        ctx, expert = place_ref[0], place_ref[1]
        g_gain = jnp.zeros((1, width), F32)
        g_shift = jnp.zeros((1, width), F32)
        g_proj_bias = jnp.zeros((1, width), F32)
        for g in range(groups):
            at = slice(g * body, (g + 1) * body)
            gn = jnp.zeros((body, width), F32)
            gg = jnp.zeros((body, LANES), F32)
            lane = iota((body, LANES), 1)
            for d in range(blocks):
                match = slot_match(dest_ref, at, (expert ^ d) * capacity, capacity)
                gn = gn + dot_nn(match, gx_refs[d][:capacity, :])
                parts = dot_nt(match, gx_refs[d][capacity:, :capacity])
                gg = jnp.where(
                    lane == (expert ^ d), parts[:, 0:1] + parts[:, 1:2] + parts[:, 2:3], gg
                )
            gates = soft_gates(dot_nn(n_ref[at, :], router_ref[...]), expert_count)
            logit = gates * (gg - jnp.sum(gates * gg, axis=1, keepdims=True))
            logit_t[:, at] = logit.T.astype(BF16)
            gn = gn + dot_nt(logit.astype(BF16), router_ref[...])
            xhat, inv = norm_stats(mid_ref[at, :])
            g_gain = g_gain + jnp.sum(gn * xhat, axis=0, keepdims=True)
            g_shift = g_shift + jnp.sum(gn, axis=0, keepdims=True)
            gmid = cot_ref[ctx ^ g].astype(F32) + norm_back(gn * gain_ref[...], xhat, inv)
            gmid_ref[at, :] = gmid
            branch = gmid.astype(BF16)
            g_proj_bias = g_proj_bias + jnp.sum(branch.astype(F32), axis=0, keepdims=True)
            branch_t[:, at] = branch.T
            att_all[at, :] = att[g][...]
            ga_refs[g][...] = dot_nt(branch, proj_ref[...]).astype(BF16)
        shared_ref[:width, :] = dot_nn(branch_t[...], att_all[...]).astype(BF16)
        rows = dot_nn(logit_t[...], n_ref[...])[:misc]
        k = iota((misc, width), 0)
        for s, vec in enumerate((g_gain, g_shift, g_proj_bias)):
            rows = jnp.where(k == expert_count + s, vec, rows)
        shared_ref[width:, :] = rows.astype(BF16)

    ins = (
        list(gxs) + [mid, normed, cotangent, dest_cols] + list(attended) + [router, gain, proj]
    )
    return pl.pallas_call(
        kernel,
        in_specs=[SMEM_SPEC] + [VMEM_SPEC] * len(ins) + [ANY_SPEC] * len(after),
        out_specs=[VMEM_SPEC] * (2 + groups),
        out_shape=[shape((tok, width), F32)]
        + [shape((body, width), BF16)] * groups
        + [shape((width + misc, width), BF16)],
        scratch_shapes=[
            pltpu.VMEM((width, tok), BF16),
            pltpu.VMEM((LANES, tok), BF16),
            pltpu.VMEM((tok, width), BF16),
        ],
        compiler_params=params(),
        cost_estimate=takes(11),
        name="middle_back",
    )(place, *ins, *after)


def attend_back_call(
    place, pieces, grads, saved, shared, gain, shift, qkv, qkv_t, value_bias, images, rows, n_dp, after
):
    count = len(pieces)
    width = qkv.shape[0]
    seq = count * rows
    size = width // HEADS
    body = images * rows
    scale = size ** (-0.5)
    part = (4 * width) // (n_dp * count)
    extra_rows = shared.shape[0] - width

    def kernel(place_ref, *refs):
        ps, gs = refs[:count], refs[count : 2 * count]
        qt_ref, k_ref, lse_ref, shared_ref, gain_ref, shift_ref, qkv_ref, qkvt_ref, vb_ref = refs[
            2 * count : 2 * count + 9
        ]
        refs = refs[2 * count + 9 + len(after) :]
        outs, sums = refs[:count], refs[count : count + n_dp]
        gt, w_acc, gain_acc, shift_acc, qb_acc, vb_acc = refs[count + n_dp :]
        i = pl.program_id(0)
        x = gather_image(ps, i, rows)
        live = gather_mask(ps, i, rows, body) > 0
        xhat, inv = norm_stats(x)
        n = (xhat * gain_ref[...] + shift_ref[...]).astype(BF16)
        kt = dot_nt(qkvt_ref[width : 2 * width], n).astype(BF16)
        v = (dot_nn(n, qkv_ref[:, 2 * width :]) + vb_ref[...]).astype(BF16)
        dot_ = gather_image(gs, i, rows).T.astype(BF16)
        k = k_ref[0]
        qt = qt_ref[0]
        for h in range(HEADS):
            at = slice(h * size, (h + 1) * size)
            pair = slice(h // 2 * 2 * size, (h // 2 + 1) * 2 * size)
            qh, kh, gh = qt[at], kt[at], dot_[at]
            s = dot_nn(k[:, pair], head_pair(qh, h, size)) * scale
            p = jnp.exp(jnp.where(live, s, NEG) - lse_ref[0, h : h + 1, :])
            dp = dot_nn(v[:, pair], head_pair(gh, h, size))
            ds = (p * (dp - jnp.sum(p * dp, axis=0, keepdims=True))).astype(BF16)
            gt[at, :] = (dot_nn(kh, ds) * scale).astype(BF16)
            gt[width + h * size : width + (h + 1) * size, :] = (dot_nt(qh, ds) * scale).astype(BF16)
            gt[2 * width + h * size : 2 * width + (h + 1) * size, :] = dot_nt(
                gh, p.astype(BF16)
            ).astype(BF16)
        gall = gt[...]
        gw = dot_nn(gall, n)
        gn = dot_nn(qkv_ref[...], gall).T
        qb = gall[:width].astype(F32)
        vb = gall[2 * width :].astype(F32)
        g_gain = jnp.sum(gn * xhat, axis=0, keepdims=True)
        g_shift = jnp.sum(gn, axis=0, keepdims=True)

        @pl.when(i == 0)
        def _():
            w_acc[...] = jnp.zeros_like(w_acc)
            gain_acc[...] = jnp.zeros_like(gain_acc)
            shift_acc[...] = jnp.zeros_like(shift_acc)
            qb_acc[...] = jnp.zeros_like(qb_acc)
            vb_acc[...] = jnp.zeros_like(vb_acc)

        w_acc[...] += gw
        gain_acc[...] += g_gain
        shift_acc[...] += g_shift
        qb_acc[...] += qb
        vb_acc[...] += vb
        gin = norm_back(gn * gain_ref[...], xhat, inv).astype(BF16)
        at = pl.ds(pl.multiple_of(i * rows, rows), rows)
        for d in range(count):
            outs[d][at, :] = gin[d * rows : (d + 1) * rows]

        @pl.when(i == images - 1)
        def _():
            rows_of = [
                jnp.broadcast_to(jnp.sum(a[...], axis=1, keepdims=True), (width, LANES)).T[:1]
                for a in (qb_acc, vb_acc)
            ]
            k16 = iota((PAD, width), 0)
            vecs = jnp.zeros((PAD, width), F32)
            for s, vec in enumerate((gain_acc[...], shift_acc[...], *rows_of)):
                vecs = jnp.where(k16 == s, vec, vecs)
            for p in range(n_dp * count):
                first = p * part
                if first < 3 * width:
                    block = w_acc[first : first + part, :].astype(BF16)
                else:
                    block = shared_ref[first - 3 * width : first - 3 * width + part, :]
                if p == 0:
                    extra = vecs.astype(BF16)
                elif p * PAD <= extra_rows:
                    extra = shared_ref[width + (p - 1) * PAD : width + p * PAD, :]
                else:
                    extra = jnp.zeros((PAD, width), BF16)
                slot = p % count ^ place_ref[0]

                def put(ref):
                    ref[slot, :part, :] = block
                    ref[slot, part:, :] = extra

                @pl.when(place_ref[2] == p // count)
                def _():
                    put(sums[0])

                @pl.when(place_ref[2] != p // count)
                def _():
                    put(sums[1])

    full = lambda a: pl.BlockSpec(a.shape, lambda i: (0,) * a.ndim)
    const = lambda dims: pl.BlockSpec(dims, lambda i: (0,) * len(dims))
    per_image = lambda a: pl.BlockSpec((1,) + a.shape[1:], lambda i: (i, 0, 0))
    rest = [shared, gain, shift, qkv, qkv_t, value_bias]
    return pl.pallas_call(
        kernel,
        grid=(images,),
        in_specs=[SMEM_SPEC] + [full(a) for a in pieces]
        + [full(a) for a in grads]
        + [per_image(a) for a in saved]
        + [full(a) for a in rest]
        + [ANY_SPEC] * len(after),
        out_specs=[const((body, width))] * count + [const((count, part + PAD, width))] * n_dp,
        out_shape=[shape((body, width), BF16)] * count
        + [shape((count, part + PAD, width), BF16)] * n_dp,
        scratch_shapes=[
            pltpu.VMEM((3 * width, seq), BF16),
            pltpu.VMEM((3 * width, width), F32),
            pltpu.VMEM((1, width), F32),
            pltpu.VMEM((1, width), F32),
            pltpu.VMEM((width, seq), F32),
            pltpu.VMEM((width, seq), F32),
        ],
        compiler_params=params(),
        cost_estimate=takes(20),
        name="attend_back",
    )(place, *pieces, *grads, *saved, *rest, *after)


def input_call(place, gmid, gins):
    groups = len(gins)
    body, width = gins[0].shape

    def kernel(place_ref, gmid_ref, *refs):
        ctx = place_ref[0]
        for g in range(groups):
            refs[groups][ctx ^ g] = (
                gmid_ref[g * body : (g + 1) * body, :] + refs[g][...].astype(F32)
            ).astype(BF16)

    return pl.pallas_call(
        kernel,
        in_specs=[SMEM_SPEC] + [VMEM_SPEC] * (1 + groups),
        out_specs=VMEM_SPEC,
        out_shape=shape((groups, body, width), BF16),
        compiler_params=params(),
        cost_estimate=takes(3),
        name="input",
    )(place, gmid, *gins)


def expert_grads_call(place, pieces, width, hidden_width, n_ctx, n_dp):
    count = len(pieces)
    chunk = width
    per_step = count * chunk // hidden_width
    part = chunk // per_step

    def kernel(place_ref, *refs):
        ins, (up_ref, down_ref, extra_ref) = refs[:count], refs[count:]
        q = pl.program_id(0)
        for i in range(count):

            @pl.when(q == i)
            def _():
                up_ref[...] = ins[i][:part, :].astype(F32)
                down_ref[...] = ins[i][part : 2 * part, :].astype(F32)
                extra_ref[0] = ins[i][2 * part :, :].astype(F32)

    def piece(q, p):
        return (p[2] ^ (q // n_ctx)) * n_ctx + (p[0] ^ lax.rem(q, n_ctx))

    return pl.pallas_call(
        kernel,
        grid_spec=pltpu.PrefetchScalarGridSpec(
            num_scalar_prefetch=1,
            grid=(count,),
            in_specs=[pl.BlockSpec(a.shape, lambda q, p: (0, 0)) for a in pieces],
            out_specs=[
                pl.BlockSpec(
                    (part, chunk), lambda q, p: (lax.rem(piece(q, p), per_step), piece(q, p) // per_step)
                ),
                pl.BlockSpec((part, width), lambda q, p: (piece(q, p), 0)),
                pl.BlockSpec((1, PAD, width), lambda q, p: (piece(q, p), 0, 0)),
            ],
        ),
        out_shape=[
            shape((width, hidden_width), F32),
            shape((hidden_width, width), F32),
            shape((count, PAD, width), F32),
        ],
        compiler_params=params(),
        cost_estimate=takes(7),
        name="expert_grads",
    )(place, *pieces)


def shared_grads_call(place, pieces, n_ctx, width):
    count = len(pieces)
    rows, share = pieces[0].shape
    part = rows - PAD

    def kernel(place_ref, *refs):
        ins, (qkv_ref, proj_ref, extra_ref, hold) = refs[:count], refs[count:]
        for q in range(count):
            piece = (place_ref[2] ^ (q // n_ctx)) * n_ctx + (place_ref[0] ^ (q % n_ctx))
            hold[piece] = ins[q][...].astype(F32)
        for p in range(count):
            block = hold[p, :part, :].T
            if p * part < 3 * width:
                qkv_ref[:, p * part : (p + 1) * part] = block
            else:
                proj_ref[:, p * part - 3 * width : (p + 1) * part - 3 * width] = block
            extra_ref[p * PAD : (p + 1) * PAD, :] = hold[p, part:, :]

    return pl.pallas_call(
        kernel,
        in_specs=[SMEM_SPEC] + [VMEM_SPEC] * count,
        out_specs=[VMEM_SPEC] * 3,
        out_shape=[shape((share, 3 * width), F32), shape((share, width), F32), shape((count * PAD, share), F32)],
        scratch_shapes=[pltpu.VMEM((count, rows, share), F32)],
        compiler_params=params(),
        cost_estimate=takes(3),
        name="shared_grads",
    )(place, *pieces)


def swap(x, axis, d, size, what="sums"):
    with jax.named_scope(f"{what}_{axis}_{d}"):
        return lax.ppermute(x, axis, [(i, i ^ d) for i in range(size)])


def exchange(x, axis, what):
    with jax.named_scope(what):
        return lax.all_to_all(x, axis, split_axis=0, concat_axis=0, tiled=True)


def named_permute(x, axes, pairs):
    with jax.named_scope("shared_sums"):
        return lax.ppermute(x, axes, pairs)


def pick(x, i):
    return lax.dynamic_index_in_dim(x, i, 0, keepdims=False)


def add_all(parts):
    acc = parts[0].astype(F32)
    for p in parts[1:]:
        acc = acc + p.astype(F32)
    return acc.astype(BF16)


def reduce_core(stay, go, n_dp, what):
    came = swap(go, "dp", 1, n_dp, what)
    return [add_all([stay[g], came[g]]) for g in range(stay.shape[0])]


def reduce_ctx(parts, n_ctx, what):
    return [parts[0]] + [swap(parts[d], "ctx", d, n_ctx, what) for d in range(1, n_ctx)]


def local(
    mesh_sizes,
    tokens,
    cotangent,
    key_mask,
    route_ids,
    priority,
    norm1_gain,
    norm1_bias,
    qkv_weight,
    query_bias,
    value_bias,
    proj_weight,
    proj_bias,
    norm2_gain,
    norm2_bias,
    router_weight,
    expert_up,
    expert_up_bias,
    expert_down,
    expert_down_bias,
):
    n_expert, n_ctx, n_dp = mesh_sizes
    images_all, rows, width = tokens.shape
    tok = images_all * rows
    images = images_all // n_ctx
    body = images * rows
    expert_count = router_weight.shape[1]
    capacity = max(2, 2 * tok // expert_count)
    ctx, expert, core = (lax.axis_index(a) for a in ("ctx", "expert", "dp"))
    place = jnp.stack([ctx, expert, core]).astype(I32)

    tok4 = tokens.reshape(n_ctx, body, width)
    mask4 = jnp.pad(
        key_mask.reshape(n_ctx, images, rows).astype(BF16),
        ((0, 0), (0, PAD - images), (0, width - rows)),
    )
    both = jnp.concatenate([tok4, mask4], axis=1)
    mine = [pick(both, ctx ^ d) for d in range(n_ctx)]
    pieces = [mine[0]] + [swap(mine[d], "ctx", d, n_ctx, "tokens") for d in range(1, n_ctx)]

    order = jnp.arange(tok, dtype=I32).reshape(n_ctx, body)
    ints4 = jnp.stack(
        [
            route_ids[..., 0].reshape(n_ctx, body),
            route_ids[..., 1].reshape(n_ctx, body),
            priority.reshape(n_ctx, body) * tok + order,
        ],
        axis=1,
    )
    ints = jnp.concatenate([pick(ints4, ctx ^ d) for d in range(n_ctx)], axis=1)
    ints = jnp.pad(ints, ((0, 5), (0, 0)))
    cot4 = cotangent.reshape(n_ctx, body, width)
    dest_rows, dest_cols, u_send, u_own = route_call(place, ints, cot4, expert_count, capacity)
    u_came = exchange(u_send, "expert", "upstream")

    row = lambda v: v.reshape(1, -1)
    col = lambda v: v.reshape(-1, 1)
    qkv_t = qkv_weight.T
    att = attend_call(
        pieces, row(norm1_gain), row(norm1_bias), qkv_weight, qkv_t, col(query_bias), col(value_bias),
        images, rows, dest_rows,
    )
    att_out, (q_t, k, v_t, lse) = att[:n_ctx], att[n_ctx:]
    attended = [att_out[0]] + [swap(att_out[d], "ctx", d, n_ctx, "attended") for d in range(1, n_ctx)]

    mid, normed2, *x_send = middle_call(
        place, attended, mine, proj_weight, row(proj_bias), row(norm2_gain), row(norm2_bias), dest_rows,
        expert_count, capacity,
    )
    xs = [x_send[0]] + [swap(x_send[d], "expert", d, n_expert, "rows") for d in range(1, n_expert)]

    router = jnp.pad(router_weight, ((0, 0), (0, LANES - expert_count)))
    results, gxs, grads = None, [], None
    group = max(1, n_expert // EXPERT_CALLS)
    for first in range(0, n_expert, group):
        last = first + group == n_expert
        results, *res = expert_call(
            place, xs[first : first + group], u_own if first + group == 1 else u_came, first, router, expert_up[0],
            expert_up_bias, expert_down[0], expert_down_bias, results, grads, last, expert_count, n_ctx, n_dp,
            gxs[1:2] if last else [],
        )
        gxs += [
            g if first + b == 0 else swap(g, "expert", first + b, n_expert, "rows_grad")
            for b, g in enumerate(res[:group])
        ]
        grads = res[group] if not last else res[group:]

    parts = reduce_core(*grads, n_dp, "expert_terms")

    grad_mid, *rest = middle_back_call(
        place, gxs, mid, normed2, cot4, dest_cols, attended, router, row(norm2_gain), proj_weight, expert_count,
        [],
    )
    ga_send, shared = rest[:n_ctx], rest[n_ctx]
    gas = [ga_send[0]] + [swap(ga_send[d], "ctx", d, n_ctx, "attended_grad") for d in range(1, n_ctx)]

    block_out = output_call(place, exchange(results, "expert", "results"), mid, dest_cols, n_ctx)

    mine_sum = add_all(reduce_ctx(parts, n_ctx, "expert_terms"))
    own = reduce_ctx([mine_sum] * n_ctx, n_ctx, "expert_sums")
    *gin_send, stay, go = attend_back_call(
        place, pieces, gas, (q_t, k, lse), shared, row(norm1_gain), row(norm1_bias), qkv_weight, qkv_t,
        row(value_bias), images, rows, n_dp, own[1:],
    )

    share = width // n_expert
    part = add_all(reduce_ctx(reduce_core(stay, go, n_dp, "shared"), n_ctx, "shared"))
    cut = [lax.dynamic_slice_in_dim(part, (expert ^ d) * share, share, 1) for d in range(n_expert)]
    part = add_all([cut[0]] + [swap(cut[d], "expert", d, n_expert, "shared") for d in range(1, n_expert)])
    every = [part] + [
        named_permute(
            part,
            ("ctx", "dp"),
            [(i, i ^ (q % n_ctx * n_dp + q // n_ctx)) for i in range(n_dp * n_ctx)],
        )
        for q in range(1, n_dp * n_ctx)
    ]

    gins = [gin_send[0]] + [swap(gin_send[d], "ctx", d, n_ctx, "input_grad") for d in range(1, n_ctx)]
    input_grad = input_call(place, grad_mid, gins)

    other = [swap(a, "dp", 1, n_dp, "expert_sums") for a in own]
    grad_up, grad_down, extra = expert_grads_call(
        place, own + other, width, expert_up.shape[2], n_ctx, n_dp
    )
    per_step = extra.shape[0] * width // expert_up.shape[2]
    grad_up_bias = extra[::per_step, 0].reshape(1, -1)
    grad_down_bias = extra[0, 1].reshape(1, -1)

    grad_qkv, grad_proj, extra = shared_grads_call(place, every, n_ctx, width)
    g1_gain, g1_bias, g_query_bias, g_value_bias = (extra[s] for s in range(4))
    grad_router = extra[PAD : PAD + expert_count].T
    g2_gain, g2_bias, g_proj_bias = (extra[PAD + expert_count + s] for s in range(3))
    return (
        block_out.reshape(tokens.shape),
        input_grad.reshape(tokens.shape),
        g1_gain,
        g1_bias,
        grad_qkv,
        g_query_bias,
        g_value_bias,
        grad_proj,
        g_proj_bias,
        g2_gain,
        g2_bias,
        grad_router,
        grad_up[None],
        grad_up_bias,
        grad_down[None],
        grad_down_bias,
    )


def solution(mesh):
    images = P(("expert", "dp"), "ctx", None)
    ints = P(("expert", "dp"), "ctx")
    placed = (images, images, ints, images, ints) + (P(),) * 10 + (
        P("expert", None, None),
        P("expert", None),
        P("expert", None, None),
        P("expert", None),
    )
    sizes = tuple(mesh.shape[a] for a in ("expert", "ctx", "dp"))

    def run(*args):
        return local(sizes, *args)

    return jax.shard_map(
        run,
        mesh=mesh,
        in_specs=placed,
        out_specs=(
            images,
            images,
            P("expert"),
            P("expert"),
            P("expert", None),
            P("expert"),
            P("expert"),
            P("expert", None),
            P("expert"),
            P("expert"),
            P("expert"),
            P("expert", None),
            P("expert", None, None),
            P("expert", None),
            P("expert", None, None),
            P("expert", None),
        ),
        check_vma=False,
    )
```

```python
import jax
import jax.numpy as jnp
from jax import lax
from jax.experimental import pallas as pl
from jax.experimental.pallas import tpu as pltpu
from jax.sharding import PartitionSpec as P

HEADS = 8
EPS = 1e-06
NEG = -1e30
F32 = jnp.float32
BF16 = jnp.bfloat16
I32 = jnp.int32
LANES = 128
PAD = 16
EXPERT_CALLS = 4
EXPERT_CHUNK = 512


def dot_nn(a, b):
    return lax.dot_general(a, b, (((1,), (0,)), ((), ())), preferred_element_type=F32)


def dot_nt(a, b):
    return lax.dot_general(a, b, (((1,), (1,)), ((), ())), preferred_element_type=F32)


def iota(shape, axis):
    return lax.broadcasted_iota(I32, shape, axis)


def norm_stats(v):
    centre = v - jnp.mean(v, axis=1, keepdims=True)
    inv = lax.rsqrt(jnp.mean(centre * centre, axis=1, keepdims=True) + EPS)
    return centre * inv, inv


def norm_back(gy, xhat, inv):
    return (
        gy - jnp.mean(gy, axis=1, keepdims=True) - xhat * jnp.mean(gy * xhat, axis=1, keepdims=True)
    ) * inv


def soft_gates(logits, expert_count):
    logits = jnp.where(iota(logits.shape, 1) < expert_count, logits, NEG)
    e = jnp.exp(logits - jnp.max(logits, axis=1, keepdims=True))
    return e / jnp.sum(e, axis=1, keepdims=True)


ERF = (0.254829592, -0.284496736, 1.421413741, -1.453152027, 1.061405429)
ERF_P = 0.3275911 * 0.7071067811865476


def gelu_parts(h):
    t = 1.0 / (1.0 + ERF_P * jnp.abs(h))
    e = jnp.exp(-0.5 * h * h)
    poly = 0.5 * ERF[4]
    for c in ERF[3::-1]:
        poly = poly * t + 0.5 * c
    tail = poly * t * e
    cdf = jnp.where(h >= 0, 1.0 - tail, tail)
    return h * cdf, cdf + h * (e * 0.3989422804014327)


def params(mib):
    return pltpu.CompilerParams(vmem_limit_bytes=mib * 2**20)


def takes(us):
    return pl.CostEstimate(flops=int(us * 1.15e9), bytes_accessed=1 << 17, transcendentals=0)


ANY_SPEC = pl.BlockSpec(memory_space=pl.ANY)
SMEM_SPEC = pl.BlockSpec(memory_space=pltpu.SMEM)
VMEM_SPEC = pl.BlockSpec(memory_space=pltpu.VMEM)


def shape(dims, dtype):
    return jax.ShapeDtypeStruct(dims, dtype)


def pieces_call(place, tokens, mask):
    groups, body, width = tokens.shape
    images, rows = mask.shape[1:]

    def kernel(place_ref, tokens_ref, mask_ref, *outs):
        for d in range(groups):
            group = place_ref[0] ^ d
            outs[d][:body, :] = tokens_ref[group]
            outs[d][body:, :] = jnp.zeros((PAD, width), BF16)
            live = mask_ref[group].astype(F32)
            live = jnp.concatenate([live, jnp.zeros((images, LANES - rows), F32)], axis=1)
            live = jnp.concatenate([live, jnp.zeros((PAD - images, LANES), F32)], axis=0)
            outs[d][body:, :LANES] = live.astype(BF16)

    return pl.pallas_call(
        kernel,
        in_specs=[SMEM_SPEC] + [VMEM_SPEC] * 2,
        out_specs=[VMEM_SPEC] * groups,
        out_shape=[shape((body + PAD, width), BF16)] * groups,
        compiler_params=params(58),
        cost_estimate=takes(1),
        name="pieces",
    )(place, tokens, mask)


def route_call(place, ints, cotangent, expert_count, capacity):
    groups, group_rows, width = cotangent.shape
    tok = groups * group_rows
    e_rows = max(PAD, expert_count)

    def kernel(place_ref, ints_ref, cot_ref, *outs):
        row_ref, col_ref = outs[:2]
        slots = outs[2:]
        ctx, expert = place_ref[0], place_ref[1]
        vals = ints_ref[...]
        ids = (vals[0:1], vals[1:2])
        key = vals[2:3]
        keys = jnp.broadcast_to(key.astype(F32), (8, tok))
        key_col = keys.T[:, :1]
        before = (key_col < keys[:1]).astype(BF16)
        hot = [(iota((e_rows, tok), 0) == i).astype(F32) for i in ids]
        counts = dot_nn(jnp.concatenate(hot, axis=0).astype(BF16), before)
        first_total = jnp.sum(hot[0], axis=1, keepdims=True)
        ranks = (
            jnp.sum(hot[0] * counts[:e_rows], axis=0, keepdims=True),
            jnp.sum(hot[1] * (counts[e_rows:] + first_total), axis=0, keepdims=True),
        )
        dest = [
            jnp.where(r < capacity, i.astype(F32) * capacity + r, -1.0)
            for r, i in zip(ranks, ids)
        ]
        rows = jnp.concatenate(
            [dest[0], dest[1], jnp.full((6, tok), -1.0, F32)], axis=0
        )
        row_ref[...] = rows.astype(I32)
        col_ref[...] = rows.T.astype(I32)
        d0, d1 = dest[0].astype(I32), dest[1].astype(I32)
        up = jnp.concatenate([cot_ref[ctx ^ d] for d in range(groups)], axis=0)
        for e in range(expert_count):
            ids_here = iota((capacity, tok), 0) + e * capacity
            pick = ((ids_here == d0) | (ids_here == d1)).astype(F32).astype(BF16)
            slots[0][e] = dot_nn(pick, up).astype(BF16)
        slots[1][0] = slots[0][expert]

    return pl.pallas_call(
        kernel,
        in_specs=[SMEM_SPEC, VMEM_SPEC, VMEM_SPEC],
        out_specs=[VMEM_SPEC] * 4,
        out_shape=[
            shape((8, tok), I32),
            shape((tok, 8), I32),
            shape((expert_count, capacity, width), BF16),
            shape((1, capacity, width), BF16),
        ],
        compiler_params=params(58),
        cost_estimate=takes(4),
        name="route",
    )(place, ints, cotangent)


def gather_image(pieces, i, rows):
    at = pl.ds(pl.multiple_of(i * rows, rows), rows)
    return jnp.concatenate([p[at, :] for p in pieces], axis=0).astype(F32)


def gather_mask(pieces, i, rows, body):
    cols = []
    for p in pieces:
        block = p[body : body + PAD, :LANES].astype(F32).T
        cols.append(
            jnp.sum(jnp.where(iota(block.shape, 1) == i, block, 0.0), axis=1, keepdims=True)[:rows]
        )
    return jnp.concatenate(cols, axis=0)


def two_heads(block, size):
    zero = jnp.zeros((size, block.shape[1]), block.dtype)
    return jnp.concatenate(
        [
            jnp.concatenate([block[:size], zero], axis=0),
            jnp.concatenate([zero, block[size:]], axis=0),
        ],
        axis=1,
    )


def attend_call(pieces, gain, shift, qkv, query_bias, value_bias, images, rows, after):
    count = len(pieces)
    width = qkv.shape[0]
    seq = count * rows
    size = width // HEADS
    body = images * rows
    scale = size ** (-0.5)

    def kernel(*refs):
        ps = refs[:count]
        gain_ref, shift_ref, qkv_ref, qb_ref, vb_ref = refs[count : count + 5]
        outs = refs[count + 6 : 2 * count + 6]
        qt_ref, k_ref, v_ref, lse_ref, ot, vt = refs[2 * count + 6 :]
        i = pl.program_id(0)
        x = gather_image(ps, i, rows)
        live = gather_mask(ps, i, rows, body) > 0
        xhat, _ = norm_stats(x)
        n = (xhat * gain_ref[...] + shift_ref[...]).astype(BF16)
        qt_ref[0] = ((dot_nn(n, qkv_ref[:, :width]) + qb_ref[...]) * scale).astype(BF16).T
        k_ref[0] = dot_nn(n, qkv_ref[:, width : 2 * width]).astype(BF16)
        v = (dot_nn(n, qkv_ref[:, 2 * width :]) + vb_ref[...]).astype(BF16)
        v_ref[0] = v
        vt[...] = v.T
        for h in range(0, HEADS, 2):
            pair = slice(h * size, (h + 2) * size)
            s = dot_nn(k_ref[0, :, pair], two_heads(qt_ref[0, pair, :], size))
            s = jnp.where(live, s, NEG)
            top = jnp.max(s, axis=0, keepdims=True)
            e = jnp.exp(s - top)
            total = jnp.sum(e, axis=0, keepdims=True)
            lse_ref[0, h // 2 : h // 2 + 1, :] = top + jnp.log(total)
            p = (e * (1.0 / total)).astype(BF16)
            for k in range(2):
                at = slice((h + k) * size, (h + k + 1) * size)
                ot[at, :] = dot_nn(vt[at, :], p[:, k * seq : (k + 1) * seq])
        o = ot[...].T.astype(BF16)
        at = pl.ds(pl.multiple_of(i * rows, rows), rows)
        for d in range(count):
            outs[d][at, :] = o[d * rows : (d + 1) * rows]

    full = lambda a: pl.BlockSpec(a.shape, lambda i: (0,) * a.ndim)
    ins = list(pieces) + [gain, shift, qkv, query_bias, value_bias]
    per_image = lambda dims: pl.BlockSpec((1,) + dims, lambda i: (i, 0, 0))
    saved = [(width, seq), (seq, width), (seq, width), (HEADS // 2, 2 * seq)]
    return pl.pallas_call(
        kernel,
        grid=(images,),
        in_specs=[full(a) for a in ins] + [ANY_SPEC],
        out_specs=[pl.BlockSpec((body, width), lambda i: (0, 0))] * count
        + [per_image(dims) for dims in saved],
        out_shape=[shape((body, width), BF16)] * count
        + [shape((images,) + dims, BF16) for dims in saved[:3]]
        + [shape((images,) + saved[3], F32)],
        scratch_shapes=[pltpu.VMEM((width, seq), F32), pltpu.VMEM((width, seq), BF16)],
        compiler_params=params(58),
        cost_estimate=takes(12),
        name="attend",
    )(*ins, after)


def middle_call(place, attended, pieces, proj, proj_bias, gain, shift, dest_rows, expert_count, capacity):
    count = len(attended)
    body, width = attended[0].shape
    tok = count * body

    def kernel(place_ref, *refs):
        att, ps = refs[:count], refs[count : 2 * count]
        proj_ref, pb_ref, gain_ref, shift_ref, dest_ref = refs[2 * count : 2 * count + 5]
        mid_ref, n_ref = refs[2 * count + 5 : 2 * count + 7]
        slots = refs[2 * count + 7 :]
        expert = place_ref[1]
        for d in range(count):
            at = slice(d * body, (d + 1) * body)
            mid = (
                ps[d][:body, :].astype(F32) + dot_nn(att[d][...], proj_ref[...]) + pb_ref[...]
            )
            mid_ref[at, :] = mid
            xhat, _ = norm_stats(mid)
            n_ref[at, :] = (xhat * gain_ref[...] + shift_ref[...]).astype(BF16)
        n = n_ref[...]
        d0, d1 = dest_ref[0:1, :], dest_ref[1:2, :]
        for d in range(expert_count):
            ids_here = iota((capacity, tok), 0) + (expert ^ d) * capacity
            pick = ((ids_here == d0) | (ids_here == d1)).astype(F32).astype(BF16)
            slots[d][...] = dot_nn(pick, n).astype(BF16)

    ins = list(attended) + list(pieces) + [proj, proj_bias, gain, shift, dest_rows]
    return pl.pallas_call(
        kernel,
        in_specs=[SMEM_SPEC] + [VMEM_SPEC] * len(ins),
        out_specs=[VMEM_SPEC] * (2 + expert_count),
        out_shape=[shape((tok, width), F32), shape((tok, width), BF16)]
        + [shape((capacity, width), BF16)] * expert_count,
        compiler_params=params(58),
        cost_estimate=takes(5),
        name="middle",
    )(place, *ins)


def expert_call(
    place, xs, upstream, first, router, up, up_bias, down, down_bias, held, expert_count, after
):
    blocks = len(xs)
    capacity, width = xs[0].shape
    hidden_width = up.shape[1]
    total = blocks * capacity
    chunk = EXPERT_CHUNK
    steps = hidden_width // chunk
    sub = min(total, 384)
    ins = list(xs) + [upstream, router, up, up_bias, down, down_bias]
    n_own = len(ins)
    ins += [] if held is None else list(held)
    n_in = len(ins) + len(after)

    def kernel(place_ref, *refs):
        x_refs, u_ref = refs[:blocks], refs[blocks]
        rw, up_ref, ub_ref, dn_ref, db_ref = refs[blocks + 1 : blocks + 6]
        o = refs[n_in:]
        out_ref, g_all, act, gh_all = o[:4]
        gx_refs = o[4 : 4 + blocks]
        x_all, gate, out_acc, gx_acc = o[4 + blocks :]
        j = pl.program_id(0)
        slots = [lax.rem(place_ref[1] ^ (first + b), blocks) for b in range(blocks)]

        @pl.when(j == 0)
        def _():
            expert = place_ref[1]
            for b in range(blocks):
                at = slice(b * capacity, (b + 1) * capacity)
                x = x_refs[b][...]
                gates = soft_gates(dot_nn(x, rw[...]), expert_count)
                mine = jnp.sum(
                    jnp.where(iota(gates.shape, 1) == expert, gates, 0.0), axis=1, keepdims=True
                )
                x_all[at, :] = x
                g_all[at, :] = (u_ref[slots[b]].astype(F32) * mine).astype(BF16)
                gate[at, :] = jnp.broadcast_to(mine, (capacity, LANES))
            out_acc[...] = jnp.zeros_like(out_acc)
            gx_acc[...] = jnp.zeros_like(gx_acc)

        w_up, w_dn = up_ref[...], dn_ref[...]
        for r in range(total // sub):
            at = slice(r * sub, (r + 1) * sub)
            h = dot_nn(x_all[at, :], w_up) + ub_ref[...]
            a, slope = gelu_parts(h)
            a = a.astype(BF16)
            act[at, :] = a
            out_acc[at, :] += dot_nn(a, w_dn)
            gh = (dot_nt(g_all[at, :], w_dn) * slope).astype(BF16)
            gh_all[at, :] = gh
            gx_acc[at, :] += dot_nt(gh, w_up)

        @pl.when(j == steps - 1)
        def _():
            for b in range(blocks):
                at = slice(b * capacity, (b + 1) * capacity)
                out = (out_acc[at, :] + db_ref[...]).astype(BF16).astype(F32)
                out_ref[slots[b]] = (out * gate[at, :1]).astype(BF16)
                gg = jnp.sum(out * u_ref[slots[b]].astype(F32), axis=1, keepdims=True)
                line = jnp.broadcast_to(gg, (capacity, LANES)).T[:PAD]
                high = line.astype(BF16).astype(F32)
                mean = (line - high).astype(BF16).astype(F32)
                k = iota(line.shape, 0)
                parts = jnp.where(
                    k == 0, high, jnp.where(k == 1, mean, jnp.where(k == 2, line - high - mean, 0.0))
                )
                gx_refs[b][:capacity, :] = gx_acc[at, :].astype(BF16)
                gx_refs[b][capacity:, :] = jnp.concatenate(
                    [parts, jnp.zeros((PAD, width - capacity), F32)], axis=1
                ).astype(BF16)

    full = lambda a: pl.BlockSpec(a.shape, lambda j, p: (0,) * a.ndim)
    const = lambda dims: pl.BlockSpec(dims, lambda j, p: (0,) * len(dims))
    blocks_of = pl.BlockSpec((blocks, capacity, width), lambda j, p: ((p[1] ^ first) // blocks, 0, 0))
    hidden_of = pl.BlockSpec((total, chunk), lambda j, p: (first // blocks, j))
    specs = (
        [full(a) for a in xs]
        + [full(upstream) if upstream.shape[0] == blocks else blocks_of]
        + [
            full(router),
            pl.BlockSpec((width, chunk), lambda j, p: (0, j)),
            pl.BlockSpec((1, chunk), lambda j, p: (0, j)),
            pl.BlockSpec((chunk, width), lambda j, p: (j, 0)),
            full(down_bias),
        ]
        + [ANY_SPEC] * (len(ins) - n_own)
    )
    return pl.pallas_call(
        kernel,
        grid_spec=pltpu.PrefetchScalarGridSpec(
            num_scalar_prefetch=1,
            grid=(steps,),
            in_specs=specs + [ANY_SPEC] * len(after),
            out_specs=[
                blocks_of,
                pl.BlockSpec((total, width), lambda j, p: (first // blocks, 0)),
                hidden_of,
                hidden_of,
            ]
            + [const((capacity + PAD, width))] * blocks,
            scratch_shapes=[
                pltpu.VMEM((total, width), BF16),
                pltpu.VMEM((total, LANES), F32),
                pltpu.VMEM((total, width), F32),
                pltpu.VMEM((total, width), F32),
            ],
        ),
        out_shape=[
            shape((expert_count, capacity, width), BF16),
            shape((expert_count * capacity, width), BF16),
            shape((expert_count * capacity, hidden_width), BF16),
            shape((expert_count * capacity, hidden_width), BF16),
        ]
        + [shape((capacity + PAD, width), BF16)] * blocks,
        input_output_aliases={} if held is None else {1 + n_own + k: k for k in range(4)},
        compiler_params=params(58),
        cost_estimate=takes(9),
        name="expert",
    )(place, *ins, *after)


def weights_call(place, xs, grads, act, grad_hidden, n_ctx, n_dp):
    capacity, width = xs[0].shape
    hidden_width = act.shape[1]
    total = len(xs) * capacity
    chunk = width
    steps = hidden_width // chunk
    per_step = n_ctx * n_dp // steps
    part = chunk // per_step
    piece_rows = 2 * part + PAD
    nx = len(xs)

    def kernel(place_ref, *refs):
        x_refs, (g_ref, act_ref, gh_ref), refs = refs[:nx], refs[nx : nx + 3], refs[nx + 3 :]
        grad_refs, (x_t, g_t, down_bias_sum) = refs[:n_dp], refs[n_dp:]
        j = pl.program_id(0)

        @pl.when(j == 0)
        def _():
            x_t[:width, :] = jnp.concatenate([r[...] for r in x_refs], axis=0).T
            x_t[width:, :] = jnp.ones((PAD, total), BF16)
            g_t[...] = g_ref[...].T
            down_bias_sum[...] = jnp.sum(g_ref[...].astype(F32), axis=0, keepdims=True)

        g_up = dot_nn(x_t[...], gh_ref[...])
        g_dn = dot_nn(g_t[...], act_ref[...]).T
        row = iota((PAD, width), 0)
        extra = jnp.where(row == 0, g_up[width:], 0.0)
        extra = jnp.where((row == 1) & (j == 0), down_bias_sum[...], extra)
        for k in range(per_step):
            vals = (
                g_up[k * part : (k + 1) * part].astype(BF16),
                g_dn[k * part : (k + 1) * part].astype(BF16),
                extra.astype(BF16) if k == 0 else jnp.zeros((PAD, width), BF16),
            )
            piece = j * per_step + k
            slot = lax.rem(piece, n_ctx) ^ place_ref[0]

            def put(ref):
                ref[slot, :part, :] = vals[0]
                ref[slot, part : 2 * part, :] = vals[1]
                ref[slot, 2 * part :, :] = vals[2]

            @pl.when(piece // n_ctx == place_ref[2])
            def _():
                put(grad_refs[0])

            @pl.when(piece // n_ctx != place_ref[2])
            def _():
                put(grad_refs[1])

    full = lambda a: pl.BlockSpec(a.shape, lambda j: (0,) * a.ndim)
    hidden_of = lambda a: pl.BlockSpec((a.shape[0], chunk), lambda j: (0, j))
    return pl.pallas_call(
        kernel,
        grid=(steps,),
        in_specs=[SMEM_SPEC]
        + [full(a) for a in xs]
        + [full(grads), hidden_of(act), hidden_of(grad_hidden)],
        out_specs=[pl.BlockSpec((n_ctx, piece_rows, width), lambda j: (0, 0, 0))] * n_dp,
        out_shape=[shape((n_ctx, piece_rows, width), BF16)] * n_dp,
        scratch_shapes=[
            pltpu.VMEM((width + PAD, total), BF16),
            pltpu.VMEM((width, total), BF16),
            pltpu.VMEM((1, width), F32),
        ],
        compiler_params=params(58),
        cost_estimate=takes(13),
        name="weights",
    )(place, *xs, grads, act, grad_hidden)


def slot_match(dest_ref, at, first, capacity):
    d = dest_ref[at, :]
    lanes = iota((d.shape[0], capacity), 1) + first
    return ((lanes == d[:, 0:1]) | (lanes == d[:, 1:2])).astype(F32).astype(BF16)


def output_call(place, results, mid, dest_cols, groups):
    blocks, capacity, width = results.shape
    tok = mid.shape[0]
    body = tok // groups

    def kernel(place_ref, o_ref, mid_ref, dest_ref, out_ref):
        rows = o_ref[...].reshape(blocks * capacity, width)
        for g in range(groups):
            at = slice(g * body, (g + 1) * body)
            acc = mid_ref[at, :] + dot_nn(slot_match(dest_ref, at, 0, blocks * capacity), rows)
            out_ref[place_ref[0] ^ g] = acc.astype(BF16)

    return pl.pallas_call(
        kernel,
        in_specs=[SMEM_SPEC] + [VMEM_SPEC] * 3,
        out_specs=VMEM_SPEC,
        out_shape=shape((groups, body, width), BF16),
        compiler_params=params(58),
        cost_estimate=takes(30),
        name="output",
    )(place, results, mid, dest_cols)


def middle_back_call(
    place, gxs, mid, normed, cotangent, dest_cols, attended, router, gain, proj, expert_count, after
):
    blocks = len(gxs)
    groups, body, width = cotangent.shape
    capacity = gxs[0].shape[0] - PAD
    tok = groups * body
    misc = -(-(expert_count + 3) // PAD) * PAD

    def kernel(place_ref, *refs):
        gx_refs = refs[:blocks]
        mid_ref, n_ref, cot_ref, dest_ref = refs[blocks : blocks + 4]
        att = refs[blocks + 4 : blocks + 4 + groups]
        router_ref, gain_ref, proj_ref = refs[blocks + 4 + groups : blocks + 7 + groups]
        refs = refs[blocks + 7 + groups + len(after) :]
        gmid_ref, ga_refs = refs[0], refs[1 : 1 + groups]
        shared_ref, branch_t, logit_t, att_all, slot_rows = refs[1 + groups :]
        ctx, expert = place_ref[0], place_ref[1]
        for d in range(blocks):
            at = pl.ds(pl.multiple_of((expert ^ d) * capacity, PAD), capacity)
            slot_rows[at, :width] = gx_refs[d][:capacity, :]
            cols = gx_refs[d][capacity:, :].astype(F32).T
            lane = iota((capacity, LANES), 1) == (expert ^ d)
            for k in range(3):
                slot_rows[at, width + k * LANES : width + (k + 1) * LANES] = jnp.where(
                    lane, cols[:capacity, k : k + 1], 0.0
                ).astype(BF16)
        g_gain = jnp.zeros((1, width), F32)
        g_shift = jnp.zeros((1, width), F32)
        g_proj_bias = jnp.zeros((1, width), F32)
        for g in range(groups):
            at = slice(g * body, (g + 1) * body)
            both = dot_nn(slot_match(dest_ref, at, 0, blocks * capacity), slot_rows[...])
            gn = both[:, :width]
            gg = both[:, width : width + LANES] + (
                both[:, width + LANES : width + 2 * LANES] + both[:, width + 2 * LANES :]
            )
            gates = soft_gates(dot_nn(n_ref[at, :], router_ref[...]), expert_count)
            logit = gates * (gg - jnp.sum(gates * gg, axis=1, keepdims=True))
            logit_t[:, at] = logit.T.astype(BF16)
            gn = gn + dot_nt(logit.astype(BF16), router_ref[...])
            xhat, inv = norm_stats(mid_ref[at, :])
            g_gain = g_gain + jnp.sum(gn * xhat, axis=0, keepdims=True)
            g_shift = g_shift + jnp.sum(gn, axis=0, keepdims=True)
            gmid = cot_ref[ctx ^ g].astype(F32) + norm_back(gn * gain_ref[...], xhat, inv)
            gmid_ref[at, :] = gmid
            branch = gmid.astype(BF16)
            g_proj_bias = g_proj_bias + jnp.sum(branch.astype(F32), axis=0, keepdims=True)
            branch_t[:, at] = branch.T
            att_all[at, :] = att[g][...]
            ga_refs[g][...] = dot_nt(branch, proj_ref[...]).astype(BF16)
        shared_ref[:width, :] = dot_nn(branch_t[...], att_all[...]).astype(BF16)
        rows = dot_nn(logit_t[...], n_ref[...])[:misc]
        k = iota((misc, width), 0)
        for s, vec in enumerate((g_gain, g_shift, g_proj_bias)):
            rows = jnp.where(k == expert_count + s, vec, rows)
        shared_ref[width:, :] = rows.astype(BF16)

    ins = (
        list(gxs) + [mid, normed, cotangent, dest_cols] + list(attended) + [router, gain, proj]
    )
    return pl.pallas_call(
        kernel,
        in_specs=[SMEM_SPEC] + [VMEM_SPEC] * len(ins) + [ANY_SPEC] * len(after),
        out_specs=[VMEM_SPEC] * (2 + groups),
        out_shape=[shape((tok, width), F32)]
        + [shape((body, width), BF16)] * groups
        + [shape((width + misc, width), BF16)],
        scratch_shapes=[
            pltpu.VMEM((width, tok), BF16),
            pltpu.VMEM((LANES, tok), BF16),
            pltpu.VMEM((tok, width), BF16),
            pltpu.VMEM((blocks * capacity, width + 3 * LANES), BF16),
        ],
        compiler_params=params(58),
        cost_estimate=takes(30),
        name="middle_back",
    )(place, *ins, *after)


def attend_back_call(
    place, pieces, grads, saved, shared, gain, shift, qkv, images, rows, n_dp, after
):
    count = len(pieces)
    width = qkv.shape[0]
    seq = count * rows
    size = width // HEADS
    body = images * rows
    scale = size ** (-0.5)
    part = (4 * width) // (n_dp * count)
    extra_rows = shared.shape[0] - width

    def kernel(place_ref, *refs):
        ps, gs = refs[:count], refs[count : 2 * count]
        qt_ref, k_ref, v_ref, lse_ref, shared_ref, gain_ref, shift_ref, qkv_ref = refs[
            2 * count : 2 * count + 8
        ]
        refs = refs[2 * count + 8 + len(after) :]
        gin_ref, sums = refs[0], refs[1 : 1 + n_dp]
        gt, w_acc, gain_acc, shift_acc, qb_acc, vb_acc = refs[1 + n_dp :]
        i = pl.program_id(0)
        x = gather_image(ps, i, rows)
        live = gather_mask(ps, i, rows, body) > 0
        xhat, inv = norm_stats(x)
        n = (xhat * gain_ref[...] + shift_ref[...]).astype(BF16)
        out_t = gather_image(gs, i, rows).astype(BF16).T
        k, v, qt = k_ref[0], v_ref[0], qt_ref[0]
        kt = k.T
        for h in range(0, HEADS, 2):
            pair = slice(h * size, (h + 2) * size)
            s = dot_nn(k[:, pair], two_heads(qt[pair], size))
            p = jnp.exp(jnp.where(live, s, NEG) - lse_ref[0, h // 2 : h // 2 + 1, :])
            dp = dot_nn(v[:, pair], two_heads(out_t[pair], size))
            pdp = p * dp
            ds = (pdp - p * jnp.sum(pdp, axis=0, keepdims=True)).astype(BF16)
            p = p.astype(BF16)
            for m in range(2):
                at = slice((h + m) * size, (h + m + 1) * size)
                one = slice(m * seq, (m + 1) * seq)
                gt[at, :] = (dot_nn(kt[at], ds[:, one]) * scale).astype(BF16)
                gt[width + at.start : width + at.stop, :] = dot_nt(qt[at], ds[:, one]).astype(BF16)
                gt[2 * width + at.start : 2 * width + at.stop, :] = dot_nt(
                    out_t[at], p[:, one]
                ).astype(BF16)
        gall = gt[...]
        gw = dot_nn(gall, n)
        gn = dot_nn(qkv_ref[...], gall).T
        qb = gall[:width].astype(F32)
        vb = gall[2 * width :].astype(F32)
        g_gain = jnp.sum(gn * xhat, axis=0, keepdims=True)
        g_shift = jnp.sum(gn, axis=0, keepdims=True)

        @pl.when(i == 0)
        def _():
            w_acc[...] = jnp.zeros_like(w_acc)
            gain_acc[...] = jnp.zeros_like(gain_acc)
            shift_acc[...] = jnp.zeros_like(shift_acc)
            qb_acc[...] = jnp.zeros_like(qb_acc)
            vb_acc[...] = jnp.zeros_like(vb_acc)

        w_acc[...] += gw
        gain_acc[...] += g_gain
        shift_acc[...] += g_shift
        qb_acc[...] += qb
        vb_acc[...] += vb
        gin = norm_back(gn * gain_ref[...], xhat, inv).astype(BF16)
        at = pl.ds(pl.multiple_of(i * rows, rows), rows)
        for d in range(count):
            gin_ref[place_ref[0] ^ d, at, :] = gin[d * rows : (d + 1) * rows]

        @pl.when(i == images - 1)
        def _():
            rows_of = [
                jnp.broadcast_to(jnp.sum(a[...], axis=1, keepdims=True), (width, LANES)).T[:1]
                for a in (qb_acc, vb_acc)
            ]
            k16 = iota((PAD, width), 0)
            vecs = jnp.zeros((PAD, width), F32)
            for s, vec in enumerate((gain_acc[...], shift_acc[...], *rows_of)):
                vecs = jnp.where(k16 == s, vec, vecs)
            for p in range(n_dp * count):
                first = p * part
                if first < 3 * width:
                    block = w_acc[first : first + part, :].astype(BF16)
                else:
                    block = shared_ref[first - 3 * width : first - 3 * width + part, :]
                if p == 0:
                    extra = vecs.astype(BF16)
                elif p * PAD <= extra_rows:
                    extra = shared_ref[width + (p - 1) * PAD : width + p * PAD, :]
                else:
                    extra = jnp.zeros((PAD, width), BF16)
                slot = p % count ^ place_ref[0]

                def put(ref):
                    ref[slot, :part, :] = block
                    ref[slot, part:, :] = extra

                @pl.when(place_ref[2] == p // count)
                def _():
                    put(sums[0])

                @pl.when(place_ref[2] != p // count)
                def _():
                    put(sums[1])

    full = lambda a: pl.BlockSpec(a.shape, lambda i: (0,) * a.ndim)
    const = lambda dims: pl.BlockSpec(dims, lambda i: (0,) * len(dims))
    per_image = lambda a: pl.BlockSpec((1,) + a.shape[1:], lambda i: (i, 0, 0))
    rest = [shared, gain, shift, qkv]
    return pl.pallas_call(
        kernel,
        grid=(images,),
        in_specs=[SMEM_SPEC] + [full(a) for a in pieces]
        + [full(a) for a in grads]
        + [per_image(a) for a in saved]
        + [full(a) for a in rest]
        + [ANY_SPEC] * len(after),
        out_specs=[const((count, body, width))] + [const((count, part + PAD, width))] * n_dp,
        out_shape=[shape((count, body, width), BF16)]
        + [shape((count, part + PAD, width), BF16)] * n_dp,
        scratch_shapes=[
            pltpu.VMEM((3 * width, seq), BF16),
            pltpu.VMEM((3 * width, width), F32),
            pltpu.VMEM((1, width), F32),
            pltpu.VMEM((1, width), F32),
            pltpu.VMEM((width, seq), F32),
            pltpu.VMEM((width, seq), F32),
        ],
        compiler_params=params(58),
        cost_estimate=takes(20),
        name="attend_back",
    )(place, *pieces, *grads, *saved, *rest, *after)


def input_call(place, gmid, gins, after):
    groups, body, width = gins.shape

    def kernel(place_ref, gmid_ref, gin_ref, *refs):
        for g in range(groups):
            group = place_ref[0] ^ g
            refs[-1][group] = (
                gmid_ref[g * body : (g + 1) * body, :] + gin_ref[group].astype(F32)
            ).astype(BF16)

    return pl.pallas_call(
        kernel,
        in_specs=[SMEM_SPEC] + [VMEM_SPEC] * 2 + [ANY_SPEC] * len(after),
        out_specs=VMEM_SPEC,
        out_shape=shape((groups, body, width), BF16),
        compiler_params=params(58),
        cost_estimate=takes(3),
        name="input",
    )(place, gmid, gins, *after)


def expert_grads_call(place, pieces, flip, hidden_width, half):
    n_ctx, piece_rows, width = pieces.shape
    chunk = width
    per_step = 2 * n_ctx * chunk // hidden_width
    part = chunk // per_step
    half = [] if half is None else list(half)

    def piece_of(q, p):
        return (p[2] ^ flip) * n_ctx + (p[0] ^ q)

    def kernel(place_ref, ref, *refs):
        up_ref, down_ref, up_bias_ref, down_bias_ref = refs[len(half) :]
        q = pl.program_id(0)
        piece = piece_of(q, place_ref)
        if half:

            @pl.when(q == 0)
            def _():
                up_bias_ref[...] = refs[2][...]
                down_bias_ref[...] = refs[3][...]

        up_ref[...] = ref[0, :part, :].astype(F32)
        down_ref[...] = ref[0, part : 2 * part, :].astype(F32)
        extra = ref[0, 2 * part :, :].astype(F32)

        @pl.when(lax.rem(piece, per_step) == 0)
        def _():
            at = pl.multiple_of(piece // per_step * chunk, chunk)
            up_bias_ref[:, pl.ds(at, chunk)] = extra[0:1]

        @pl.when(piece == 0)
        def _():
            down_bias_ref[...] = extra[1:2]

    biases = [
        pl.BlockSpec((1, hidden_width), lambda q, p: (0, 0)),
        pl.BlockSpec((1, width), lambda q, p: (0, 0)),
    ]
    return pl.pallas_call(
        kernel,
        grid_spec=pltpu.PrefetchScalarGridSpec(
            num_scalar_prefetch=1,
            grid=(n_ctx,),
            in_specs=[pl.BlockSpec((1, piece_rows, width), lambda q, p: (q, 0, 0))]
            + ([ANY_SPEC] * 2 + biases if half else []),
            out_specs=[
                pl.BlockSpec(
                    (part, chunk),
                    lambda q, p: (lax.rem(piece_of(q, p), per_step), piece_of(q, p) // per_step),
                ),
                pl.BlockSpec((part, width), lambda q, p: (piece_of(q, p), 0)),
            ]
            + biases,
        ),
        out_shape=[
            shape((width, hidden_width), F32),
            shape((hidden_width, width), F32),
            shape((1, hidden_width), F32),
            shape((1, width), F32),
        ],
        input_output_aliases={2: 0, 3: 1} if half else {},
        compiler_params=params(58),
        cost_estimate=takes(3),
        name="expert_grads",
    )(place, pieces, *half)


def shared_grads_call(place, pieces, width, expert_count):
    n_ctx, rows, share = pieces[0].shape
    count = len(pieces) * n_ctx
    part = rows - PAD

    def kernel(place_ref, *refs):
        ins, refs = refs[: len(pieces)], refs[len(pieces) :]
        qkv_ref, proj_ref, router_ref = refs[:3]
        vec_refs, (hold, extra) = refs[3:10], refs[10:]
        for q in range(count):
            piece = (place_ref[2] ^ (q // n_ctx)) * n_ctx + (place_ref[0] ^ (q % n_ctx))
            hold[piece] = ins[q // n_ctx][q % n_ctx].astype(F32)
        for p in range(count):
            block = hold[p, :part, :].T
            if p * part < 3 * width:
                qkv_ref[:, p * part : (p + 1) * part] = block
            else:
                proj_ref[:, p * part - 3 * width : (p + 1) * part - 3 * width] = block
            extra[p * PAD : (p + 1) * PAD, :] = hold[p, part:, :]
        cols = extra[...].T
        router_ref[...] = cols[:, PAD : PAD + expert_count]
        for s in range(4):
            vec_refs[s][...] = extra[s : s + 1, :]
        for s in range(3):
            vec_refs[4 + s][...] = extra[PAD + expert_count + s : PAD + expert_count + s + 1, :]

    return pl.pallas_call(
        kernel,
        in_specs=[SMEM_SPEC] + [VMEM_SPEC] * len(pieces),
        out_specs=[VMEM_SPEC] * 10,
        out_shape=[shape((share, 3 * width), F32), shape((share, width), F32), shape((share, expert_count), F32)]
        + [shape((1, share), F32)] * 7,
        scratch_shapes=[pltpu.VMEM((count, rows, share), F32), pltpu.VMEM((count * PAD, share), F32)],
        compiler_params=params(58),
        cost_estimate=takes(3),
        name="shared_grads",
    )(place, *pieces)


def swap(x, axis, d, size, what="sums"):
    with jax.named_scope(f"{what}_{axis}_{d}"):
        return lax.ppermute(x, axis, [(i, i ^ d) for i in range(size)])


def exchange(x, axis, what):
    with jax.named_scope(what):
        return lax.all_to_all(x, axis, split_axis=0, concat_axis=0, tiled=True)


def pick(x, i):
    return lax.dynamic_index_in_dim(x, i, 0, keepdims=False)


class Order:
    def __init__(self):
        self.seen = []

    def after(self, x, *others):
        x, others = lax.optimization_barrier((x, others))
        self.seen += others
        return x


def add_all(parts):
    acc = parts[0].astype(F32)
    for p in parts[1:]:
        acc = acc + p.astype(F32)
    return acc.astype(BF16)


def reduce_core(stay, go, n_dp, what):
    came = swap(go, "dp", 1, n_dp, what)
    return [add_all([stay[g], came[g]]) for g in range(stay.shape[0])]


def reduce_ctx(parts, n_ctx, what):
    return [parts[0]] + [swap(parts[d], "ctx", d, n_ctx, what) for d in range(1, n_ctx)]


def local(
    mesh_sizes,
    tokens,
    cotangent,
    key_mask,
    route_ids,
    priority,
    norm1_gain,
    norm1_bias,
    qkv_weight,
    query_bias,
    value_bias,
    proj_weight,
    proj_bias,
    norm2_gain,
    norm2_bias,
    router_weight,
    expert_up,
    expert_up_bias,
    expert_down,
    expert_down_bias,
):
    n_expert, n_ctx, n_dp = mesh_sizes
    order = Order()
    images_all, rows, width = tokens.shape
    tok = images_all * rows
    images = images_all // n_ctx
    body = images * rows
    expert_count = router_weight.shape[1]
    capacity = max(2, 2 * tok // expert_count)
    ctx, expert, core = (lax.axis_index(a) for a in ("ctx", "expert", "dp"))
    place = jnp.stack([ctx, expert, core]).astype(I32)

    mine = pieces_call(
        place, tokens.reshape(n_ctx, body, width), key_mask.reshape(n_ctx, images, rows)
    )
    pieces = [mine[0]] + [swap(mine[d], "ctx", d, n_ctx, "tokens") for d in range(1, n_ctx)]

    token_of = jnp.arange(tok, dtype=I32).reshape(n_ctx, body)
    ints4 = jnp.stack(
        [
            route_ids[..., 0].reshape(n_ctx, body),
            route_ids[..., 1].reshape(n_ctx, body),
            priority.reshape(n_ctx, body) * tok + token_of,
        ],
        axis=1,
    )
    ints = jnp.concatenate([pick(ints4, ctx ^ d) for d in range(n_ctx)], axis=1)
    ints = jnp.pad(ints, ((0, 5), (0, 0)))
    cot4 = cotangent.reshape(n_ctx, body, width)
    dest_rows, dest_cols, u_send, u_own = route_call(place, ints, cot4, expert_count, capacity)
    u_came = exchange(u_send, "expert", "upstream")

    row = lambda v: v.reshape(1, -1)
    att = attend_call(
        pieces, row(norm1_gain), row(norm1_bias), qkv_weight, row(query_bias), row(value_bias), images, rows,
        dest_rows,
    )
    att_out, saved = att[:n_ctx], att[n_ctx:]
    attended = [att_out[0]] + [swap(att_out[d], "ctx", d, n_ctx, "attended") for d in range(1, n_ctx)]

    mid, normed2, *x_send = middle_call(
        place, attended, mine, proj_weight, row(proj_bias), row(norm2_gain), row(norm2_bias), dest_rows,
        expert_count, capacity,
    )

    router = jnp.pad(router_weight, ((0, 0), (0, LANES - expert_count)))
    held, gxs = None, []
    xs = [x_send[0]] + [swap(x_send[d], "expert", d, n_expert, "rows") for d in range(1, n_expert)]
    group = max(1, n_expert // EXPERT_CALLS)
    for first in range(0, n_expert, group):
        res = expert_call(
            place, xs[first : first + group], u_own if first + group == 1 else u_came, first, router, expert_up[0],
            expert_up_bias, expert_down[0], expert_down_bias, held, expert_count,
            gxs[1:2] if first + group == n_expert else [],
        )
        gxs += [
            g if first + b == 0 else swap(g, "expert", first + b, n_expert, "rows_grad")
            for b, g in enumerate(res[4:])
        ]
        held = res[:4]
    results, *held = held
    stay, go = weights_call(place, xs, *held, n_ctx, n_dp)
    came = swap(order.after(go, gxs[2]), "dp", 1, n_dp, "expert_terms")
    gxs[0] = order.after(gxs[0], stay)
    grad_mid, *rest = middle_back_call(
        place, gxs, mid, normed2, cot4, dest_cols, attended, router, row(norm2_gain), proj_weight, expert_count,
        [],
    )
    ga_send, shared = rest[:n_ctx], rest[n_ctx]
    gas = [ga_send[0]] + [swap(ga_send[d], "ctx", d, n_ctx, "attended_grad") for d in range(1, n_ctx)]
    results = order.after(results, ga_send[0])
    came = order.after(came, ga_send[0])
    terms = [add_all([stay[g], came[g]]) for g in range(n_ctx)]
    gas[0] = order.after(gas[0], *terms)
    terms = reduce_ctx(order.after(terms, *gas), n_ctx, "expert_terms")
    block_out = output_call(place, exchange(results, "expert", "results"), mid, dest_cols, n_ctx)

    gin_send, flat_stay, flat_go = attend_back_call(
        place, pieces, gas, saved, shared, row(norm1_gain), row(norm1_bias), qkv_weight, images, rows, n_dp, [],
    )
    terms, flat_go = lax.optimization_barrier((terms, flat_go))
    sums = add_all(terms)
    own = [sums] + [swap(sums, "ctx", d, n_ctx, "expert_sums") for d in range(1, n_ctx - 1)]
    flat = reduce_ctx(reduce_core(flat_stay, flat_go, n_dp, "shared"), n_ctx, "shared")

    share = width // n_expert
    flat = order.after(flat, *own[1:])
    own.append(swap(order.after(sums, flat[1]), "ctx", n_ctx - 1, n_ctx, "expert_sums"))
    part = add_all(flat)
    gin_send = order.after(gin_send, part)
    cut = [lax.dynamic_slice_in_dim(part, (expert ^ d) * share, share, 1) for d in range(n_expert)]
    part = add_all([cut[0]] + [swap(cut[d], "expert", d, n_expert, "shared") for d in range(1, n_expert)])
    gins = exchange(gin_send, "ctx", "input_grad")
    part = order.after(part, block_out)
    part = jnp.stack(reduce_ctx([part] * n_ctx, n_ctx, "shared_sums"))
    every = [part, swap(part, "dp", 1, n_dp, "shared_sums")]
    own = order.after(jnp.stack(own), part)
    hidden_width = expert_up.shape[2]
    other = swap(own, "dp", 1, n_dp, "expert_sums")
    half = expert_grads_call(place, own, 0, hidden_width, None)
    grad_up, grad_down, grad_up_bias, grad_down_bias = expert_grads_call(place, other, 1, hidden_width, half)
    input_grad = input_call(place, grad_mid, gins, order.seen)
    grad_qkv, grad_proj, grad_router, *vectors = shared_grads_call(place, every, width, expert_count)
    g1_gain, g1_bias, g_query_bias, g_value_bias, g2_gain, g2_bias, g_proj_bias = (
        v.reshape(share) for v in vectors
    )
    return (
        block_out.reshape(tokens.shape),
        input_grad.reshape(tokens.shape),
        g1_gain,
        g1_bias,
        grad_qkv,
        g_query_bias,
        g_value_bias,
        grad_proj,
        g_proj_bias,
        g2_gain,
        g2_bias,
        grad_router,
        grad_up[None],
        grad_up_bias,
        grad_down[None],
        grad_down_bias,
    )


def solution(mesh):
    images = P(("expert", "dp"), "ctx", None)
    ints = P(("expert", "dp"), "ctx")
    placed = (images, images, ints, images, ints) + (P(),) * 10 + (
        P("expert", None, None),
        P("expert", None),
        P("expert", None, None),
        P("expert", None),
    )
    sizes = tuple(mesh.shape[a] for a in ("expert", "ctx", "dp"))

    def run(*args):
        return local(sizes, *args)

    return jax.shard_map(
        run,
        mesh=mesh,
        in_specs=placed,
        out_specs=(
            images,
            images,
            P("expert"),
            P("expert"),
            P("expert", None),
            P("expert"),
            P("expert"),
            P("expert", None),
            P("expert"),
            P("expert"),
            P("expert"),
            P("expert", None),
            P("expert", None, None),
            P("expert", None),
            P("expert", None, None),
            P("expert", None),
        ),
        check_vma=False,
    )
```

```python
import jax
import jax.numpy as jnp
from jax import lax
from jax.experimental import pallas as pl
from jax.experimental.pallas import tpu as pltpu
from jax.sharding import PartitionSpec as P

HEADS = 8
EPS = 1e-06
NEG = -1e30
F32 = jnp.float32
BF16 = jnp.bfloat16
I32 = jnp.int32
LANES = 128
PAD = 16
EXPERT_CALLS = 4
EXPERT_CHUNK = 512


def dot_nn(a, b):
    return lax.dot_general(a, b, (((1,), (0,)), ((), ())), preferred_element_type=F32)


def dot_nt(a, b):
    return lax.dot_general(a, b, (((1,), (1,)), ((), ())), preferred_element_type=F32)


def iota(shape, axis):
    return lax.broadcasted_iota(I32, shape, axis)


def norm_stats(v):
    centre = v - jnp.mean(v, axis=1, keepdims=True)
    inv = lax.rsqrt(jnp.mean(centre * centre, axis=1, keepdims=True) + EPS)
    return centre * inv, inv


def norm_back(gy, xhat, inv):
    return (
        gy - jnp.mean(gy, axis=1, keepdims=True) - xhat * jnp.mean(gy * xhat, axis=1, keepdims=True)
    ) * inv


def soft_gates(logits, expert_count):
    logits = jnp.where(iota(logits.shape, 1) < expert_count, logits, NEG)
    e = jnp.exp(logits - jnp.max(logits, axis=1, keepdims=True))
    return e / jnp.sum(e, axis=1, keepdims=True)


ERF = (0.254829592, -0.284496736, 1.421413741, -1.453152027, 1.061405429)
ERF_P = 0.3275911 * 0.7071067811865476


def gelu_parts(h):
    t = 1.0 / (1.0 + ERF_P * jnp.abs(h))
    e = jnp.exp(-0.5 * h * h)
    poly = 0.5 * ERF[4]
    for c in ERF[3::-1]:
        poly = poly * t + 0.5 * c
    tail = poly * t * e
    cdf = jnp.where(h >= 0, 1.0 - tail, tail)
    return h * cdf, cdf + h * (e * 0.3989422804014327)


def params(mib):
    return pltpu.CompilerParams(vmem_limit_bytes=mib * 2**20)


def takes(us):
    return pl.CostEstimate(flops=int(us * 1.15e9), bytes_accessed=1 << 17, transcendentals=0)


ANY_SPEC = pl.BlockSpec(memory_space=pl.ANY)
SMEM_SPEC = pl.BlockSpec(memory_space=pltpu.SMEM)
VMEM_SPEC = pl.BlockSpec(memory_space=pltpu.VMEM)


def shape(dims, dtype):
    return jax.ShapeDtypeStruct(dims, dtype)


def pieces_call(place, tokens, mask):
    groups, body, width = tokens.shape
    rows = mask.shape[1]
    images = mask.shape[0] // groups

    def kernel(place_ref, tokens_ref, mask_ref, *outs):
        for d in range(groups):
            group = place_ref[0] ^ d
            outs[d][:body, :] = tokens_ref[group]
            outs[d][body:, :] = jnp.zeros((PAD, width), BF16)
            live = jnp.zeros((images, rows), F32)
            for g in range(groups):
                live = jnp.where(group == g, mask_ref[g * images : (g + 1) * images, :].astype(F32), live)
            live = jnp.concatenate([live, jnp.zeros((images, LANES - rows), F32)], axis=1)
            live = jnp.concatenate([live, jnp.zeros((PAD - images, LANES), F32)], axis=0)
            outs[d][body:, :LANES] = live.astype(BF16)

    return pl.pallas_call(
        kernel,
        in_specs=[SMEM_SPEC] + [VMEM_SPEC] * 2,
        out_specs=[VMEM_SPEC] * groups,
        out_shape=[shape((body + PAD, width), BF16)] * groups,
        compiler_params=params(58),
        cost_estimate=takes(1),
        name="pieces",
    )(place, tokens, mask)


def route_call(place, ints, cotangent, expert_count, capacity):
    groups, group_rows, width = cotangent.shape
    tok = groups * group_rows
    e_rows = max(PAD, expert_count)

    def kernel(place_ref, ints_ref, cot_ref, *outs):
        row_ref, col_ref = outs[:2]
        slots = outs[2:]
        ctx, expert = place_ref[0], place_ref[1]
        vals = ints_ref[...]
        ids = (vals[0:1], vals[1:2])
        key = vals[2:3]
        keys = jnp.broadcast_to(key.astype(F32), (8, tok))
        key_col = keys.T[:, :1]
        before = (key_col < keys[:1]).astype(BF16)
        hot = [(iota((e_rows, tok), 0) == i).astype(F32) for i in ids]
        counts = dot_nn(jnp.concatenate(hot, axis=0).astype(BF16), before)
        first_total = jnp.sum(hot[0], axis=1, keepdims=True)
        ranks = (
            jnp.sum(hot[0] * counts[:e_rows], axis=0, keepdims=True),
            jnp.sum(hot[1] * (counts[e_rows:] + first_total), axis=0, keepdims=True),
        )
        dest = [
            jnp.where(r < capacity, i.astype(F32) * capacity + r, -1.0)
            for r, i in zip(ranks, ids)
        ]
        rows = jnp.concatenate(
            [dest[0], dest[1], jnp.full((6, tok), -1.0, F32)], axis=0
        )
        row_ref[...] = rows.astype(I32)
        col_ref[...] = rows.T.astype(I32)
        d0, d1 = dest[0].astype(I32), dest[1].astype(I32)
        up = jnp.concatenate([cot_ref[ctx ^ d] for d in range(groups)], axis=0)
        for e in range(expert_count):
            ids_here = iota((capacity, tok), 0) + e * capacity
            pick = ((ids_here == d0) | (ids_here == d1)).astype(F32).astype(BF16)
            slots[0][e] = dot_nn(pick, up).astype(BF16)
        slots[1][0] = slots[0][expert]

    return pl.pallas_call(
        kernel,
        in_specs=[SMEM_SPEC, VMEM_SPEC, VMEM_SPEC],
        out_specs=[VMEM_SPEC] * 4,
        out_shape=[
            shape((8, tok), I32),
            shape((tok, 8), I32),
            shape((expert_count, capacity, width), BF16),
            shape((1, capacity, width), BF16),
        ],
        compiler_params=params(58),
        cost_estimate=takes(4),
        name="route",
    )(place, ints, cotangent)


def gather_image(pieces, i, rows):
    at = pl.ds(pl.multiple_of(i * rows, rows), rows)
    return jnp.concatenate([p[at, :] for p in pieces], axis=0).astype(F32)


def gather_mask(pieces, i, rows, body):
    cols = []
    for p in pieces:
        block = p[body : body + PAD, :LANES].astype(F32).T
        cols.append(
            jnp.sum(jnp.where(iota(block.shape, 1) == i, block, 0.0), axis=1, keepdims=True)[:rows]
        )
    return jnp.concatenate(cols, axis=0)


def two_heads(block, size):
    zero = jnp.zeros((size, block.shape[1]), block.dtype)
    return jnp.concatenate(
        [
            jnp.concatenate([block[:size], zero], axis=0),
            jnp.concatenate([zero, block[size:]], axis=0),
        ],
        axis=1,
    )


def attend_call(pieces, gain, shift, qkv, query_bias, value_bias, images, rows, after):
    count = len(pieces)
    width = qkv.shape[0]
    seq = count * rows
    size = width // HEADS
    body = images * rows
    scale = size ** (-0.5)

    def kernel(*refs):
        ps = refs[:count]
        gain_ref, shift_ref, qkv_ref, qb_ref, vb_ref = refs[count : count + 5]
        outs = refs[count + 6 : 2 * count + 6]
        qt_ref, k_ref, v_ref, lse_ref, ot, vt = refs[2 * count + 6 :]
        i = pl.program_id(0)
        x = gather_image(ps, i, rows)
        live = gather_mask(ps, i, rows, body) > 0
        xhat, _ = norm_stats(x)
        n = (xhat * gain_ref[...] + shift_ref[...]).astype(BF16)
        qt_ref[0] = ((dot_nn(n, qkv_ref[:, :width]) + qb_ref[...]) * scale).astype(BF16).T
        k_ref[0] = dot_nn(n, qkv_ref[:, width : 2 * width]).astype(BF16)
        v = (dot_nn(n, qkv_ref[:, 2 * width :]) + vb_ref[...]).astype(BF16)
        v_ref[0] = v
        vt[...] = v.T
        for h in range(0, HEADS, 2):
            pair = slice(h * size, (h + 2) * size)
            s = dot_nn(k_ref[0, :, pair], two_heads(qt_ref[0, pair, :], size))
            s = jnp.where(live, s, NEG)
            top = jnp.max(s, axis=0, keepdims=True)
            e = jnp.exp(s - top)
            total = jnp.sum(e, axis=0, keepdims=True)
            lse_ref[0, h // 2 : h // 2 + 1, :] = top + jnp.log(total)
            p = (e * (1.0 / total)).astype(BF16)
            for k in range(2):
                at = slice((h + k) * size, (h + k + 1) * size)
                ot[at, :] = dot_nn(vt[at, :], p[:, k * seq : (k + 1) * seq])
        o = ot[...].T.astype(BF16)
        at = pl.ds(pl.multiple_of(i * rows, rows), rows)
        for d in range(count):
            outs[d][at, :] = o[d * rows : (d + 1) * rows]

    full = lambda a: pl.BlockSpec(a.shape, lambda i: (0,) * a.ndim)
    ins = list(pieces) + [gain, shift, qkv, query_bias, value_bias]
    per_image = lambda dims: pl.BlockSpec((1,) + dims, lambda i: (i, 0, 0))
    saved = [(width, seq), (seq, width), (seq, width), (HEADS // 2, 2 * seq)]
    return pl.pallas_call(
        kernel,
        grid=(images,),
        in_specs=[full(a) for a in ins] + [ANY_SPEC],
        out_specs=[pl.BlockSpec((body, width), lambda i: (0, 0))] * count
        + [per_image(dims) for dims in saved],
        out_shape=[shape((body, width), BF16)] * count
        + [shape((images,) + dims, BF16) for dims in saved[:3]]
        + [shape((images,) + saved[3], F32)],
        scratch_shapes=[pltpu.VMEM((width, seq), F32), pltpu.VMEM((width, seq), BF16)],
        compiler_params=params(58),
        cost_estimate=takes(12),
        name="attend",
    )(*ins, after)


def middle_call(place, attended, pieces, proj, proj_bias, gain, shift, dest_rows, expert_count, capacity):
    count = len(attended)
    body, width = attended[0].shape
    tok = count * body

    def kernel(place_ref, *refs):
        att, ps = refs[:count], refs[count : 2 * count]
        proj_ref, pb_ref, gain_ref, shift_ref, dest_ref = refs[2 * count : 2 * count + 5]
        mid_ref, n_ref = refs[2 * count + 5 : 2 * count + 7]
        slots = refs[2 * count + 7 :]
        expert = place_ref[1]
        for d in range(count):
            at = slice(d * body, (d + 1) * body)
            mid = (
                ps[d][:body, :].astype(F32) + dot_nn(att[d][...], proj_ref[...]) + pb_ref[...]
            )
            mid_ref[at, :] = mid
            xhat, _ = norm_stats(mid)
            n_ref[at, :] = (xhat * gain_ref[...] + shift_ref[...]).astype(BF16)
        n = n_ref[...]
        d0, d1 = dest_ref[0:1, :], dest_ref[1:2, :]
        for d in range(expert_count):
            ids_here = iota((capacity, tok), 0) + (expert ^ d) * capacity
            pick = ((ids_here == d0) | (ids_here == d1)).astype(F32).astype(BF16)
            slots[d][...] = dot_nn(pick, n).astype(BF16)

    ins = list(attended) + list(pieces) + [proj, proj_bias, gain, shift, dest_rows]
    return pl.pallas_call(
        kernel,
        in_specs=[SMEM_SPEC] + [VMEM_SPEC] * len(ins),
        out_specs=[VMEM_SPEC] * (2 + expert_count),
        out_shape=[shape((tok, width), F32), shape((tok, width), BF16)]
        + [shape((capacity, width), BF16)] * expert_count,
        compiler_params=params(58),
        cost_estimate=takes(5),
        name="middle",
    )(place, *ins)


def expert_call(
    place, xs, upstream, first, router, up, up_bias, down, down_bias, held, expert_count, after
):
    blocks = len(xs)
    capacity, width = xs[0].shape
    hidden_width = up.shape[1]
    total = blocks * capacity
    chunk = EXPERT_CHUNK
    steps = hidden_width // chunk
    sub = min(total, 384)
    ins = list(xs) + [upstream, router, up, up_bias, down, down_bias]
    n_own = len(ins)
    ins += [] if held is None else list(held)
    n_in = len(ins) + len(after)

    def kernel(place_ref, *refs):
        x_refs, u_ref = refs[:blocks], refs[blocks]
        rw, up_ref, ub_ref, dn_ref, db_ref = refs[blocks + 1 : blocks + 6]
        o = refs[n_in:]
        out_ref, g_all, act, gh_all = o[:4]
        gx_refs = o[4 : 4 + blocks]
        x_all, gate, out_acc, gx_acc = o[4 + blocks :]
        j = pl.program_id(0)
        slots = [lax.rem(place_ref[1] ^ (first + b), blocks) for b in range(blocks)]

        @pl.when(j == 0)
        def _():
            expert = place_ref[1]
            for b in range(blocks):
                at = slice(b * capacity, (b + 1) * capacity)
                x = x_refs[b][...]
                gates = soft_gates(dot_nn(x, rw[...]), expert_count)
                mine = jnp.sum(
                    jnp.where(iota(gates.shape, 1) == expert, gates, 0.0), axis=1, keepdims=True
                )
                x_all[at, :] = x
                g_all[at, :] = (u_ref[slots[b]].astype(F32) * mine).astype(BF16)
                gate[at, :] = jnp.broadcast_to(mine, (capacity, LANES))
            out_acc[...] = jnp.zeros_like(out_acc)
            gx_acc[...] = jnp.zeros_like(gx_acc)

        w_up, w_dn = up_ref[...], dn_ref[...]
        for r in range(total // sub):
            at = slice(r * sub, (r + 1) * sub)
            h = dot_nn(x_all[at, :], w_up) + ub_ref[...]
            a, slope = gelu_parts(h)
            a = a.astype(BF16)
            act[at, :] = a
            out_acc[at, :] += dot_nn(a, w_dn)
            gh = (dot_nt(g_all[at, :], w_dn) * slope).astype(BF16)
            gh_all[at, :] = gh
            gx_acc[at, :] += dot_nt(gh, w_up)

        @pl.when(j == steps - 1)
        def _():
            for b in range(blocks):
                at = slice(b * capacity, (b + 1) * capacity)
                out = (out_acc[at, :] + db_ref[...]).astype(BF16).astype(F32)
                out_ref[slots[b]] = (out * gate[at, :1]).astype(BF16)
                gg = jnp.sum(out * u_ref[slots[b]].astype(F32), axis=1, keepdims=True)
                line = jnp.broadcast_to(gg, (capacity, LANES)).T[:PAD]
                high = line.astype(BF16).astype(F32)
                mean = (line - high).astype(BF16).astype(F32)
                k = iota(line.shape, 0)
                parts = jnp.where(
                    k == 0, high, jnp.where(k == 1, mean, jnp.where(k == 2, line - high - mean, 0.0))
                )
                gx_refs[b][:capacity, :] = gx_acc[at, :].astype(BF16)
                gx_refs[b][capacity:, :] = jnp.concatenate(
                    [parts, jnp.zeros((PAD, width - capacity), F32)], axis=1
                ).astype(BF16)

    full = lambda a: pl.BlockSpec(a.shape, lambda j, p: (0,) * a.ndim)
    const = lambda dims: pl.BlockSpec(dims, lambda j, p: (0,) * len(dims))
    blocks_of = pl.BlockSpec((blocks, capacity, width), lambda j, p: ((p[1] ^ first) // blocks, 0, 0))
    hidden_of = pl.BlockSpec((total, chunk), lambda j, p: (first // blocks, j))
    specs = (
        [full(a) for a in xs]
        + [full(upstream) if upstream.shape[0] == blocks else blocks_of]
        + [
            full(router),
            pl.BlockSpec((width, chunk), lambda j, p: (0, j)),
            pl.BlockSpec((1, chunk), lambda j, p: (0, j)),
            pl.BlockSpec((chunk, width), lambda j, p: (j, 0)),
            full(down_bias),
        ]
        + [ANY_SPEC] * (len(ins) - n_own)
    )
    return pl.pallas_call(
        kernel,
        grid_spec=pltpu.PrefetchScalarGridSpec(
            num_scalar_prefetch=1,
            grid=(steps,),
            in_specs=specs + [ANY_SPEC] * len(after),
            out_specs=[
                blocks_of,
                pl.BlockSpec((total, width), lambda j, p: (first // blocks, 0)),
                hidden_of,
                hidden_of,
            ]
            + [const((capacity + PAD, width))] * blocks,
            scratch_shapes=[
                pltpu.VMEM((total, width), BF16),
                pltpu.VMEM((total, LANES), F32),
                pltpu.VMEM((total, width), F32),
                pltpu.VMEM((total, width), F32),
            ],
        ),
        out_shape=[
            pltpu.HBM((expert_count, capacity, width), BF16),
            pltpu.HBM((expert_count * capacity, width), BF16),
            pltpu.HBM((expert_count * capacity, hidden_width), BF16),
            pltpu.HBM((expert_count * capacity, hidden_width), BF16),
        ]
        + [pltpu.HBM((capacity + PAD, width), BF16)] * blocks,
        input_output_aliases={} if held is None else {1 + n_own + k: k for k in range(4)},
        compiler_params=params(16),
        cost_estimate=takes(9),
        name="expert",
    )(place, *ins, *after)


def weights_call(place, xs, grads, act, grad_hidden, n_ctx, n_dp):
    capacity, width = xs[0].shape
    hidden_width = act.shape[1]
    total = len(xs) * capacity
    chunk = width
    steps = hidden_width // chunk
    per_step = n_ctx * n_dp // steps
    part = chunk // per_step
    piece_rows = 2 * part + PAD
    nx = len(xs)

    def kernel(place_ref, *refs):
        x_refs, (g_ref, act_ref, gh_ref), refs = refs[:nx], refs[nx : nx + 3], refs[nx + 3 :]
        grad_refs, (x_t, g_t, down_bias_sum) = refs[:n_dp], refs[n_dp:]
        j = pl.program_id(0)

        @pl.when(j == 0)
        def _():
            x_t[:width, :] = jnp.concatenate([r[...] for r in x_refs], axis=0).T
            x_t[width:, :] = jnp.ones((PAD, total), BF16)
            g_t[...] = g_ref[...].T
            down_bias_sum[...] = jnp.sum(g_ref[...].astype(F32), axis=0, keepdims=True)

        g_up = dot_nn(x_t[...], gh_ref[...])
        g_dn = dot_nn(g_t[...], act_ref[...]).T
        row = iota((PAD, width), 0)
        extra = jnp.where(row == 0, g_up[width:], 0.0)
        extra = jnp.where((row == 1) & (j == 0), down_bias_sum[...], extra)
        for k in range(per_step):
            vals = (
                g_up[k * part : (k + 1) * part].astype(BF16),
                g_dn[k * part : (k + 1) * part].astype(BF16),
                extra.astype(BF16) if k == 0 else jnp.zeros((PAD, width), BF16),
            )
            piece = j * per_step + k
            slot = lax.rem(piece, n_ctx) ^ place_ref[0]

            def put(ref):
                ref[slot, :part, :] = vals[0]
                ref[slot, part : 2 * part, :] = vals[1]
                ref[slot, 2 * part :, :] = vals[2]

            @pl.when(piece // n_ctx == place_ref[2])
            def _():
                put(grad_refs[0])

            @pl.when(piece // n_ctx != place_ref[2])
            def _():
                put(grad_refs[1])

    full = lambda a: pl.BlockSpec(a.shape, lambda j: (0,) * a.ndim)
    hidden_of = lambda a: pl.BlockSpec((a.shape[0], chunk), lambda j: (0, j))
    return pl.pallas_call(
        kernel,
        grid=(steps,),
        in_specs=[SMEM_SPEC]
        + [full(a) for a in xs]
        + [full(grads), hidden_of(act), hidden_of(grad_hidden)],
        out_specs=[pl.BlockSpec((n_ctx, piece_rows, width), lambda j: (0, 0, 0))] * n_dp,
        out_shape=[shape((n_ctx, piece_rows, width), BF16)] * n_dp,
        scratch_shapes=[
            pltpu.VMEM((width + PAD, total), BF16),
            pltpu.VMEM((width, total), BF16),
            pltpu.VMEM((1, width), F32),
        ],
        compiler_params=params(58),
        cost_estimate=takes(13),
        name="weights",
    )(place, *xs, grads, act, grad_hidden)


def slot_match(dest_ref, at, first, capacity):
    d = dest_ref[at, :]
    lanes = iota((d.shape[0], capacity), 1) + first
    return ((lanes == d[:, 0:1]) | (lanes == d[:, 1:2])).astype(F32).astype(BF16)


def output_call(place, results, mid, dest_cols, groups):
    blocks, capacity, width = results.shape
    tok = mid.shape[0]
    body = tok // groups

    def kernel(place_ref, o_ref, mid_ref, dest_ref, out_ref):
        rows = o_ref[...].reshape(blocks * capacity, width)
        for g in range(groups):
            at = slice(g * body, (g + 1) * body)
            acc = mid_ref[at, :] + dot_nn(slot_match(dest_ref, at, 0, blocks * capacity), rows)
            out_ref[place_ref[0] ^ g] = acc.astype(BF16)

    return pl.pallas_call(
        kernel,
        in_specs=[SMEM_SPEC] + [VMEM_SPEC] * 3,
        out_specs=VMEM_SPEC,
        out_shape=shape((groups, body, width), BF16),
        compiler_params=params(58),
        cost_estimate=takes(30),
        name="output",
    )(place, results, mid, dest_cols)


def middle_back_call(
    place, gxs, mid, normed, cotangent, dest_cols, attended, router, gain, proj, expert_count, after
):
    blocks = len(gxs)
    groups, body, width = cotangent.shape
    capacity = gxs[0].shape[0] - PAD
    tok = groups * body
    misc = -(-(expert_count + 3) // PAD) * PAD

    def kernel(place_ref, *refs):
        gx_refs = refs[:blocks]
        mid_ref, n_ref, cot_ref, dest_ref = refs[blocks : blocks + 4]
        att = refs[blocks + 4 : blocks + 4 + groups]
        router_ref, gain_ref, proj_ref = refs[blocks + 4 + groups : blocks + 7 + groups]
        refs = refs[blocks + 7 + groups + len(after) :]
        gmid_ref, ga_refs = refs[0], refs[1 : 1 + groups]
        shared_ref, branch_t, logit_t, att_all, slot_rows = refs[1 + groups :]
        ctx, expert = place_ref[0], place_ref[1]
        for d in range(blocks):
            at = pl.ds(pl.multiple_of((expert ^ d) * capacity, PAD), capacity)
            slot_rows[at, :width] = gx_refs[d][:capacity, :]
            cols = gx_refs[d][capacity:, :].astype(F32).T
            lane = iota((capacity, LANES), 1) == (expert ^ d)
            for k in range(3):
                slot_rows[at, width + k * LANES : width + (k + 1) * LANES] = jnp.where(
                    lane, cols[:capacity, k : k + 1], 0.0
                ).astype(BF16)
        g_gain = jnp.zeros((1, width), F32)
        g_shift = jnp.zeros((1, width), F32)
        g_proj_bias = jnp.zeros((1, width), F32)
        for g in range(groups):
            at = slice(g * body, (g + 1) * body)
            both = dot_nn(slot_match(dest_ref, at, 0, blocks * capacity), slot_rows[...])
            gn = both[:, :width]
            gg = both[:, width : width + LANES] + (
                both[:, width + LANES : width + 2 * LANES] + both[:, width + 2 * LANES :]
            )
            gates = soft_gates(dot_nn(n_ref[at, :], router_ref[...]), expert_count)
            logit = gates * (gg - jnp.sum(gates * gg, axis=1, keepdims=True))
            logit_t[:, at] = logit.T.astype(BF16)
            gn = gn + dot_nt(logit.astype(BF16), router_ref[...])
            xhat, inv = norm_stats(mid_ref[at, :])
            g_gain = g_gain + jnp.sum(gn * xhat, axis=0, keepdims=True)
            g_shift = g_shift + jnp.sum(gn, axis=0, keepdims=True)
            gmid = cot_ref[ctx ^ g].astype(F32) + norm_back(gn * gain_ref[...], xhat, inv)
            gmid_ref[at, :] = gmid
            branch = gmid.astype(BF16)
            g_proj_bias = g_proj_bias + jnp.sum(branch.astype(F32), axis=0, keepdims=True)
            branch_t[:, at] = branch.T
            att_all[at, :] = att[g][...]
            ga_refs[g][...] = dot_nt(branch, proj_ref[...]).astype(BF16)
        shared_ref[:width, :] = dot_nn(branch_t[...], att_all[...]).astype(BF16)
        rows = dot_nn(logit_t[...], n_ref[...])[:misc]
        k = iota((misc, width), 0)
        for s, vec in enumerate((g_gain, g_shift, g_proj_bias)):
            rows = jnp.where(k == expert_count + s, vec, rows)
        shared_ref[width:, :] = rows.astype(BF16)

    ins = (
        list(gxs) + [mid, normed, cotangent, dest_cols] + list(attended) + [router, gain, proj]
    )
    return pl.pallas_call(
        kernel,
        in_specs=[SMEM_SPEC] + [VMEM_SPEC] * len(ins) + [ANY_SPEC] * len(after),
        out_specs=[VMEM_SPEC] * (2 + groups),
        out_shape=[shape((tok, width), F32)]
        + [shape((body, width), BF16)] * groups
        + [shape((width + misc, width), BF16)],
        scratch_shapes=[
            pltpu.VMEM((width, tok), BF16),
            pltpu.VMEM((LANES, tok), BF16),
            pltpu.VMEM((tok, width), BF16),
            pltpu.VMEM((blocks * capacity, width + 3 * LANES), BF16),
        ],
        compiler_params=params(58),
        cost_estimate=takes(30),
        name="middle_back",
    )(place, *ins, *after)


def attend_back_call(
    place, pieces, grads, saved, shared, gain, shift, qkv, images, rows, n_dp, after
):
    count = len(pieces)
    width = qkv.shape[0]
    seq = count * rows
    size = width // HEADS
    body = images * rows
    scale = size ** (-0.5)
    part = (4 * width) // (n_dp * count)
    extra_rows = shared.shape[0] - width

    def kernel(place_ref, *refs):
        ps, gs = refs[:count], refs[count : 2 * count]
        qt_ref, k_ref, v_ref, lse_ref, shared_ref, gain_ref, shift_ref, qkv_ref = refs[
            2 * count : 2 * count + 8
        ]
        refs = refs[2 * count + 8 + len(after) :]
        gin_ref, sums = refs[0], refs[1 : 1 + n_dp]
        gt, w_acc, gain_acc, shift_acc, qb_acc, vb_acc = refs[1 + n_dp :]
        i = pl.program_id(0)
        x = gather_image(ps, i, rows)
        live = gather_mask(ps, i, rows, body) > 0
        xhat, inv = norm_stats(x)
        n = (xhat * gain_ref[...] + shift_ref[...]).astype(BF16)
        out_t = gather_image(gs, i, rows).astype(BF16).T
        k, v, qt = k_ref[0], v_ref[0], qt_ref[0]
        kt = k.T
        for h in range(0, HEADS, 2):
            pair = slice(h * size, (h + 2) * size)
            s = dot_nn(k[:, pair], two_heads(qt[pair], size))
            p = jnp.exp(jnp.where(live, s, NEG) - lse_ref[0, h // 2 : h // 2 + 1, :])
            dp = dot_nn(v[:, pair], two_heads(out_t[pair], size))
            pdp = p * dp
            ds = (pdp - p * jnp.sum(pdp, axis=0, keepdims=True)).astype(BF16)
            p = p.astype(BF16)
            for m in range(2):
                at = slice((h + m) * size, (h + m + 1) * size)
                one = slice(m * seq, (m + 1) * seq)
                gt[at, :] = (dot_nn(kt[at], ds[:, one]) * scale).astype(BF16)
                gt[width + at.start : width + at.stop, :] = dot_nt(qt[at], ds[:, one]).astype(BF16)
                gt[2 * width + at.start : 2 * width + at.stop, :] = dot_nt(
                    out_t[at], p[:, one]
                ).astype(BF16)
        gall = gt[...]
        gw = dot_nn(gall, n)
        gn = dot_nn(qkv_ref[...], gall).T
        qb = gall[:width].astype(F32)
        vb = gall[2 * width :].astype(F32)
        g_gain = jnp.sum(gn * xhat, axis=0, keepdims=True)
        g_shift = jnp.sum(gn, axis=0, keepdims=True)

        @pl.when(i == 0)
        def _():
            w_acc[...] = jnp.zeros_like(w_acc)
            gain_acc[...] = jnp.zeros_like(gain_acc)
            shift_acc[...] = jnp.zeros_like(shift_acc)
            qb_acc[...] = jnp.zeros_like(qb_acc)
            vb_acc[...] = jnp.zeros_like(vb_acc)

        w_acc[...] += gw
        gain_acc[...] += g_gain
        shift_acc[...] += g_shift
        qb_acc[...] += qb
        vb_acc[...] += vb
        gin = norm_back(gn * gain_ref[...], xhat, inv).astype(BF16)
        at = pl.ds(pl.multiple_of(i * rows, rows), rows)
        for d in range(count):
            gin_ref[place_ref[0] ^ d, at, :] = gin[d * rows : (d + 1) * rows]

        @pl.when(i == images - 1)
        def _():
            rows_of = [
                jnp.broadcast_to(jnp.sum(a[...], axis=1, keepdims=True), (width, LANES)).T[:1]
                for a in (qb_acc, vb_acc)
            ]
            k16 = iota((PAD, width), 0)
            vecs = jnp.zeros((PAD, width), F32)
            for s, vec in enumerate((gain_acc[...], shift_acc[...], *rows_of)):
                vecs = jnp.where(k16 == s, vec, vecs)
            for p in range(n_dp * count):
                first = p * part
                if first < 3 * width:
                    block = w_acc[first : first + part, :].astype(BF16)
                else:
                    block = shared_ref[first - 3 * width : first - 3 * width + part, :]
                if p == 0:
                    extra = vecs.astype(BF16)
                elif p * PAD <= extra_rows:
                    extra = shared_ref[width + (p - 1) * PAD : width + p * PAD, :]
                else:
                    extra = jnp.zeros((PAD, width), BF16)
                slot = p % count ^ place_ref[0]

                def put(ref):
                    ref[slot, :part, :] = block
                    ref[slot, part:, :] = extra

                @pl.when(place_ref[2] == p // count)
                def _():
                    put(sums[0])

                @pl.when(place_ref[2] != p // count)
                def _():
                    put(sums[1])

    full = lambda a: pl.BlockSpec(a.shape, lambda i: (0,) * a.ndim)
    const = lambda dims: pl.BlockSpec(dims, lambda i: (0,) * len(dims))
    per_image = lambda a: pl.BlockSpec((1,) + a.shape[1:], lambda i: (i, 0, 0))
    rest = [shared, gain, shift, qkv]
    return pl.pallas_call(
        kernel,
        grid=(images,),
        in_specs=[SMEM_SPEC] + [full(a) for a in pieces]
        + [full(a) for a in grads]
        + [per_image(a) for a in saved]
        + [full(a) for a in rest]
        + [ANY_SPEC] * len(after),
        out_specs=[const((count, body, width))] + [const((count, part + PAD, width))] * n_dp,
        out_shape=[shape((count, body, width), BF16)]
        + [shape((count, part + PAD, width), BF16)] * n_dp,
        scratch_shapes=[
            pltpu.VMEM((3 * width, seq), BF16),
            pltpu.VMEM((3 * width, width), F32),
            pltpu.VMEM((1, width), F32),
            pltpu.VMEM((1, width), F32),
            pltpu.VMEM((width, seq), F32),
            pltpu.VMEM((width, seq), F32),
        ],
        compiler_params=params(58),
        cost_estimate=takes(20),
        name="attend_back",
    )(place, *pieces, *grads, *saved, *rest, *after)


def input_call(place, gmid, gins, after):
    groups, body, width = gins.shape

    def kernel(place_ref, gmid_ref, gin_ref, *refs):
        for g in range(groups):
            group = place_ref[0] ^ g
            refs[-1][group] = (
                gmid_ref[g * body : (g + 1) * body, :] + gin_ref[group].astype(F32)
            ).astype(BF16)

    return pl.pallas_call(
        kernel,
        in_specs=[SMEM_SPEC] + [VMEM_SPEC] * 2 + [ANY_SPEC] * len(after),
        out_specs=VMEM_SPEC,
        out_shape=shape((groups, body, width), BF16),
        compiler_params=params(58),
        cost_estimate=takes(3),
        name="input",
    )(place, gmid, gins, *after)


def expert_grads_call(place, pieces, first, step, n_ctx, hidden_width, half):
    piece_rows, width = pieces[0].shape[1:]
    arrays = len(pieces)
    count = sum(a.shape[0] for a in pieces)
    chunk = width
    per_step = 2 * n_ctx * chunk // hidden_width
    part = chunk // per_step
    half = [] if half is None else list(half)

    def piece_of(q, p):
        return (p[2] ^ (first[0] + q * step[0])) * n_ctx + (p[0] ^ (first[1] + q * step[1]))

    def kernel(place_ref, *refs):
        ins, refs = refs[:arrays], refs[arrays:]
        up_ref, down_ref, up_bias_ref, down_bias_ref = refs[len(half) :]
        q = pl.program_id(0)
        piece = piece_of(q, place_ref)
        if half:

            @pl.when(q == 0)
            def _():
                up_bias_ref[...] = refs[2][...]
                down_bias_ref[...] = refs[3][...]

        extra = jnp.zeros((PAD, width), F32)
        for i, ref in enumerate(ins):
            here = (q == i) if arrays > 1 else (q >= 0)

            @pl.when(here)
            def _():
                up_ref[...] = ref[0, :part, :].astype(F32)
                down_ref[...] = ref[0, part : 2 * part, :].astype(F32)

            extra = jnp.where(here, ref[0, 2 * part :, :].astype(F32), extra)

        @pl.when(lax.rem(piece, per_step) == 0)
        def _():
            at = pl.multiple_of(piece // per_step * chunk, chunk)
            up_bias_ref[:, pl.ds(at, chunk)] = extra[0:1]

        @pl.when(piece == 0)
        def _():
            down_bias_ref[...] = extra[1:2]

    biases = [
        pl.BlockSpec((1, hidden_width), lambda q, p: (0, 0)),
        pl.BlockSpec((1, width), lambda q, p: (0, 0)),
    ]
    return pl.pallas_call(
        kernel,
        grid_spec=pltpu.PrefetchScalarGridSpec(
            num_scalar_prefetch=1,
            grid=(count,),
            in_specs=[
                pl.BlockSpec(
                    (1, piece_rows, width), lambda q, p: (q if arrays == 1 else 0, 0, 0)
                )
            ]
            * arrays
            + ([ANY_SPEC] * 2 + biases if half else []),
            out_specs=[
                pl.BlockSpec(
                    (part, chunk),
                    lambda q, p: (lax.rem(piece_of(q, p), per_step), piece_of(q, p) // per_step),
                ),
                pl.BlockSpec((part, width), lambda q, p: (piece_of(q, p), 0)),
            ]
            + biases,
        ),
        out_shape=[
            shape((width, hidden_width), F32),
            shape((hidden_width, width), F32),
            shape((1, hidden_width), F32),
            shape((1, width), F32),
        ],
        input_output_aliases={1 + arrays: 0, 2 + arrays: 1} if half else {},
        compiler_params=params(58),
        cost_estimate=takes(3),
        name="expert_grads",
    )(place, *pieces, *half)


def shared_grads_call(place, pieces, width, expert_count):
    n_ctx, rows, share = pieces[0].shape
    count = len(pieces) * n_ctx
    part = rows - PAD

    def kernel(place_ref, *refs):
        ins, refs = refs[: len(pieces)], refs[len(pieces) :]
        qkv_ref, proj_ref, router_ref = refs[:3]
        vec_refs, (hold, extra) = refs[3:10], refs[10:]
        for q in range(count):
            piece = (place_ref[2] ^ (q // n_ctx)) * n_ctx + (place_ref[0] ^ (q % n_ctx))
            hold[piece] = ins[q // n_ctx][q % n_ctx].astype(F32)
        for p in range(count):
            block = hold[p, :part, :].T
            if p * part < 3 * width:
                qkv_ref[:, p * part : (p + 1) * part] = block
            else:
                proj_ref[:, p * part - 3 * width : (p + 1) * part - 3 * width] = block
            extra[p * PAD : (p + 1) * PAD, :] = hold[p, part:, :]
        router_ref[...] = extra[PAD : PAD + expert_count, :]
        for s in range(4):
            vec_refs[s][...] = extra[s : s + 1, :]
        for s in range(3):
            vec_refs[4 + s][...] = extra[PAD + expert_count + s : PAD + expert_count + s + 1, :]

    return pl.pallas_call(
        kernel,
        in_specs=[SMEM_SPEC] + [VMEM_SPEC] * len(pieces),
        out_specs=[VMEM_SPEC] * 10,
        out_shape=[shape((share, 3 * width), F32), shape((share, width), F32), shape((expert_count, share), F32)]
        + [shape((1, share), F32)] * 7,
        scratch_shapes=[pltpu.VMEM((count, rows, share), F32), pltpu.VMEM((count * PAD, share), F32)],
        compiler_params=params(58),
        cost_estimate=takes(3),
        name="shared_grads",
    )(place, *pieces)


def swap(x, axis, d, size, what="sums"):
    with jax.named_scope(f"{what}_{axis}_{d}"):
        return lax.ppermute(x, axis, [(i, i ^ d) for i in range(size)])


def exchange(x, axis, what):
    with jax.named_scope(what):
        return lax.all_to_all(x, axis, split_axis=0, concat_axis=0, tiled=True)


def pick(x, i):
    return lax.dynamic_index_in_dim(x, i, 0, keepdims=False)


class Order:
    def __init__(self):
        self.seen = []

    def after(self, x, *others):
        x, others = lax.optimization_barrier((x, others))
        self.seen += others
        return x


def add_all(parts):
    acc = parts[0].astype(F32)
    for p in parts[1:]:
        acc = acc + p.astype(F32)
    return acc.astype(BF16)


def reduce_ctx(parts, n_ctx, what):
    return [parts[0]] + [swap(parts[d], "ctx", d, n_ctx, what) for d in range(1, n_ctx)]


def local(
    mesh_sizes,
    tokens,
    cotangent,
    key_mask,
    route_ids,
    priority,
    norm1_gain,
    norm1_bias,
    qkv_weight,
    query_bias,
    value_bias,
    proj_weight,
    proj_bias,
    norm2_gain,
    norm2_bias,
    router_weight,
    expert_up,
    expert_up_bias,
    expert_down,
    expert_down_bias,
):
    n_expert, n_ctx, n_dp = mesh_sizes
    order = Order()
    images_all, rows, width = tokens.shape
    tok = images_all * rows
    images = images_all // n_ctx
    body = images * rows
    expert_count = router_weight.shape[1]
    capacity = max(2, 2 * tok // expert_count)
    ctx, expert, core = (lax.axis_index(a) for a in ("ctx", "expert", "dp"))
    place = jnp.stack([ctx, expert, core]).astype(I32)

    mine = pieces_call(place, tokens.reshape(n_ctx, body, width), key_mask)
    pieces = [mine[0]] + [swap(mine[d], "ctx", d, n_ctx, "tokens") for d in range(1, n_ctx)]

    token_of = jnp.arange(tok, dtype=I32).reshape(n_ctx, body)
    ints4 = jnp.stack(
        [
            route_ids[..., 0].reshape(n_ctx, body),
            route_ids[..., 1].reshape(n_ctx, body),
            priority.reshape(n_ctx, body) * tok + token_of,
        ],
        axis=1,
    )
    ints = jnp.concatenate([pick(ints4, ctx ^ d) for d in range(n_ctx)], axis=1)
    ints = jnp.pad(ints, ((0, 5), (0, 0)))
    cot4 = cotangent.reshape(n_ctx, body, width)
    dest_rows, dest_cols, u_send, u_own = route_call(place, ints, cot4, expert_count, capacity)
    u_came = exchange(u_send, "expert", "upstream")

    row = lambda v: v.reshape(1, -1)
    att = attend_call(
        pieces, row(norm1_gain), row(norm1_bias), qkv_weight, row(query_bias), row(value_bias), images, rows,
        dest_rows,
    )
    att_out, saved = att[:n_ctx], att[n_ctx:]
    attended = [att_out[0]] + [swap(att_out[d], "ctx", d, n_ctx, "attended") for d in range(1, n_ctx)]

    mid, normed2, *x_send = middle_call(
        place, attended, mine, proj_weight, row(proj_bias), row(norm2_gain), row(norm2_bias), dest_rows,
        expert_count, capacity,
    )

    router = jnp.pad(router_weight, ((0, 0), (0, LANES - expert_count)))
    held, gxs = None, []
    group = max(1, n_expert // EXPERT_CALLS)
    late = n_expert - group if n_expert > group else n_expert
    xs = [x_send[0]] + [swap(x_send[d], "expert", d, n_expert, "rows") for d in range(1, late)]
    for first in range(0, n_expert, group):
        res = expert_call(
            place, xs[first : first + group], u_own if first + group == 1 else u_came, first, router, expert_up[0],
            expert_up_bias, expert_down[0], expert_down_bias, held, expert_count,
            gxs[1:2] if first + group == n_expert else [],
        )
        gxs += [
            g if first + b == 0 else swap(g, "expert", first + b, n_expert, "rows_grad")
            for b, g in enumerate(res[4:])
        ]
        held = res[:4]
        if first == 0:
            xs += [
                swap(order.after(x_send[d], gxs[0]), "expert", d, n_expert, "rows")
                for d in range(late, n_expert)
            ]
    results, *held = held
    stay, go = weights_call(place, xs, *held, n_ctx, n_dp)
    came = swap(order.after(go, gxs[2]), "dp", 1, n_dp, "expert_terms")
    gxs[0] = order.after(gxs[0], stay)
    grad_mid, *rest = middle_back_call(
        place, gxs, mid, normed2, cot4, dest_cols, attended, router, row(norm2_gain), proj_weight, expert_count,
        [],
    )
    ga_send, shared = rest[:n_ctx], rest[n_ctx]
    gas = [ga_send[0]] + [swap(ga_send[d], "ctx", d, n_ctx, "attended_grad") for d in range(1, n_ctx)]
    results = order.after(results, ga_send[0])
    came = order.after(came, ga_send[0])
    terms = [add_all([stay[g], came[g]]) for g in range(n_ctx)]
    gas[0] = order.after(gas[0], *terms)
    terms = reduce_ctx(order.after(terms, *gas), n_ctx, "expert_terms")
    results = exchange(results, "expert", "results")

    gin_send, flat_stay, flat_go = attend_back_call(
        place, pieces, gas, saved, shared, row(norm1_gain), row(norm1_bias), qkv_weight, images, rows, n_dp, [],
    )
    terms, flat_go = lax.optimization_barrier((terms, flat_go))
    sums = add_all(terms)
    own = [sums] + [swap(sums, "ctx", d, n_ctx, "expert_sums") for d in range(1, n_ctx - 1)]

    share = width // n_expert
    flat = add_all([flat_stay, swap(flat_go, "dp", 1, n_dp, "shared")])
    cut = [lax.dynamic_slice_in_dim(flat, (expert ^ d) * share, share, 2) for d in range(n_expert)]
    cut = [cut[0]] + [swap(cut[d], "expert", d, n_expert, "shared") for d in range(1, n_expert)]

    hidden_width = expert_up.shape[2]
    gins = exchange(order.after(gin_send, results, cut[1]), "ctx", "input_grad")
    last = swap(order.after(sums, gins), "ctx", n_ctx - 1, n_ctx, "expert_sums")
    block_out = output_call(place, order.after(results, cut[1]), mid, dest_cols, n_ctx)
    early = jnp.stack(order.after(own, cut[1]))
    grads = expert_grads_call(place, [early], (0, 0), (0, 1), n_ctx, hidden_width, None)
    early = swap(early, "dp", 1, n_dp, "expert_sums")
    grads = expert_grads_call(place, [early], (1, 0), (0, 1), n_ctx, hidden_width, grads)
    cut = order.after(cut, grads[3], block_out, gins)

    part = add_all(cut)
    part = add_all(reduce_ctx([part[g] for g in range(n_ctx)], n_ctx, "shared"))
    part = jnp.stack(order.after(reduce_ctx([part] * n_ctx, n_ctx, "shared_sums"), last))
    every = [part, swap(part, "dp", 1, n_dp, "shared_sums")]
    grad_up, grad_down, grad_up_bias, grad_down_bias = expert_grads_call(
        place, [last[None], swap(last, "dp", 1, n_dp, "expert_sums")[None]], (0, n_ctx - 1), (1, 0), n_ctx,
        hidden_width, grads,
    )
    input_grad = input_call(place, grad_mid, gins, order.seen)
    grad_qkv, grad_proj, grad_router, *vectors = shared_grads_call(place, every, width, expert_count)
    g1_gain, g1_bias, g_query_bias, g_value_bias, g2_gain, g2_bias, g_proj_bias = (
        v.reshape(share) for v in vectors
    )
    return (
        block_out.reshape(tokens.shape),
        input_grad.reshape(tokens.shape),
        g1_gain,
        g1_bias,
        grad_qkv,
        g_query_bias,
        g_value_bias,
        grad_proj,
        g_proj_bias,
        g2_gain,
        g2_bias,
        grad_router.T,
        grad_up[None],
        grad_up_bias,
        grad_down[None],
        grad_down_bias,
    )


def solution(mesh):
    images = P(("expert", "dp"), "ctx", None)
    ints = P(("expert", "dp"), "ctx")
    placed = (images, images, ints, images, ints) + (P(),) * 10 + (
        P("expert", None, None),
        P("expert", None),
        P("expert", None, None),
        P("expert", None),
    )
    sizes = tuple(mesh.shape[a] for a in ("expert", "ctx", "dp"))

    def run(*args):
        return local(sizes, *args)

    return jax.shard_map(
        run,
        mesh=mesh,
        in_specs=placed,
        out_specs=(
            images,
            images,
            P("expert"),
            P("expert"),
            P("expert", None),
            P("expert"),
            P("expert"),
            P("expert", None),
            P("expert"),
            P("expert"),
            P("expert"),
            P("expert", None),
            P("expert", None, None),
            P("expert", None),
            P("expert", None, None),
            P("expert", None),
        ),
        check_vma=False,
    )
```

```python
import jax
import jax.numpy as jnp
from jax import lax
from jax.experimental import pallas as pl
from jax.experimental.pallas import tpu as pltpu
from jax.sharding import PartitionSpec as P

HEADS = 8
EPS = 1e-06
NEG = -1e30
F32 = jnp.float32
BF16 = jnp.bfloat16
I32 = jnp.int32
LANES = 128
PAD = 16
EXPERT_CALLS = 4
EXPERT_CHUNK = 1024


def dot_nn(a, b):
    return lax.dot_general(a, b, (((1,), (0,)), ((), ())), preferred_element_type=F32)


def dot_nt(a, b):
    return lax.dot_general(a, b, (((1,), (1,)), ((), ())), preferred_element_type=F32)


def iota(shape, axis):
    return lax.broadcasted_iota(I32, shape, axis)


def norm_stats(v):
    centre = v - jnp.mean(v, axis=1, keepdims=True)
    inv = lax.rsqrt(jnp.mean(centre * centre, axis=1, keepdims=True) + EPS)
    return centre * inv, inv


def norm_back(gy, xhat, inv):
    return (
        gy - jnp.mean(gy, axis=1, keepdims=True) - xhat * jnp.mean(gy * xhat, axis=1, keepdims=True)
    ) * inv


def soft_gates(logits, expert_count):
    logits = jnp.where(iota(logits.shape, 1) < expert_count, logits, NEG)
    e = jnp.exp(logits - jnp.max(logits, axis=1, keepdims=True))
    return e / jnp.sum(e, axis=1, keepdims=True)


ERF = (0.254829592, -0.284496736, 1.421413741, -1.453152027, 1.061405429)
ERF_P = 0.3275911 * 0.7071067811865476


def gelu_parts(h):
    t = 1.0 / (1.0 + ERF_P * jnp.abs(h))
    e = jnp.exp(-0.5 * h * h)
    poly = 0.5 * ERF[4]
    for c in ERF[3::-1]:
        poly = poly * t + 0.5 * c
    tail = poly * t * e
    cdf = jnp.where(h >= 0, 1.0 - tail, tail)
    return h * cdf, cdf + h * (e * 0.3989422804014327)


def params(mib):
    return pltpu.CompilerParams(vmem_limit_bytes=mib * 2**20)


def takes(us):
    return pl.CostEstimate(flops=int(us * 1.15e9), bytes_accessed=1 << 17, transcendentals=0)


ANY_SPEC = pl.BlockSpec(memory_space=pl.ANY)
SMEM_SPEC = pl.BlockSpec(memory_space=pltpu.SMEM)
VMEM_SPEC = pl.BlockSpec(memory_space=pltpu.VMEM)


def shape(dims, dtype):
    return jax.ShapeDtypeStruct(dims, dtype)


def pieces_call(place, tokens, mask):
    groups, body, width = tokens.shape
    rows = mask.shape[1]
    images = mask.shape[0] // groups

    def kernel(place_ref, tokens_ref, mask_ref, *outs):
        for d in range(groups):
            group = place_ref[0] ^ d
            outs[d][:body, :] = tokens_ref[group]
            outs[d][body:, :] = jnp.zeros((PAD, width), BF16)
            live = jnp.zeros((images, rows), F32)
            for g in range(groups):
                live = jnp.where(group == g, mask_ref[g * images : (g + 1) * images, :].astype(F32), live)
            live = jnp.concatenate([live, jnp.zeros((images, LANES - rows), F32)], axis=1)
            live = jnp.concatenate([live, jnp.zeros((PAD - images, LANES), F32)], axis=0)
            outs[d][body:, :LANES] = live.astype(BF16)

    return pl.pallas_call(
        kernel,
        in_specs=[SMEM_SPEC] + [VMEM_SPEC] * 2,
        out_specs=[VMEM_SPEC] * groups,
        out_shape=[shape((body + PAD, width), BF16)] * groups,
        compiler_params=params(58),
        cost_estimate=takes(1),
        name="pieces",
    )(place, tokens, mask)


def route_call(place, ints, cotangent, expert_count, capacity):
    groups, group_rows, width = cotangent.shape
    tok = groups * group_rows
    e_rows = max(PAD, expert_count)

    def kernel(place_ref, ints_ref, cot_ref, *outs):
        row_ref, col_ref = outs[:2]
        slots = outs[2:]
        ctx, expert = place_ref[0], place_ref[1]
        vals = ints_ref[...]
        ids = (vals[0:1], vals[1:2])
        key = vals[2:3]
        keys = jnp.broadcast_to(key.astype(F32), (8, tok))
        key_col = keys.T[:, :1]
        before = (key_col < keys[:1]).astype(BF16)
        hot = [(iota((e_rows, tok), 0) == i).astype(F32) for i in ids]
        counts = dot_nn(jnp.concatenate(hot, axis=0).astype(BF16), before)
        first_total = jnp.sum(hot[0], axis=1, keepdims=True)
        ranks = (
            jnp.sum(hot[0] * counts[:e_rows], axis=0, keepdims=True),
            jnp.sum(hot[1] * (counts[e_rows:] + first_total), axis=0, keepdims=True),
        )
        dest = [
            jnp.where(r < capacity, i.astype(F32) * capacity + r, -1.0)
            for r, i in zip(ranks, ids)
        ]
        rows = jnp.concatenate(
            [dest[0], dest[1], jnp.full((6, tok), -1.0, F32)], axis=0
        )
        row_ref[...] = rows.astype(I32)
        col_ref[...] = rows.T.astype(I32)
        d0, d1 = dest[0].astype(I32), dest[1].astype(I32)
        up = jnp.concatenate([cot_ref[ctx ^ d] for d in range(groups)], axis=0)
        for e in range(expert_count):
            ids_here = iota((capacity, tok), 0) + e * capacity
            pick = ((ids_here == d0) | (ids_here == d1)).astype(F32).astype(BF16)
            slots[0][e] = dot_nn(pick, up).astype(BF16)
        slots[1][0] = slots[0][expert]

    return pl.pallas_call(
        kernel,
        in_specs=[SMEM_SPEC, VMEM_SPEC, VMEM_SPEC],
        out_specs=[VMEM_SPEC] * 4,
        out_shape=[
            shape((8, tok), I32),
            shape((tok, 8), I32),
            shape((expert_count, capacity, width), BF16),
            shape((1, capacity, width), BF16),
        ],
        compiler_params=params(58),
        cost_estimate=takes(4),
        name="route",
    )(place, ints, cotangent)


def gather_image(pieces, i, rows):
    at = pl.ds(pl.multiple_of(i * rows, rows), rows)
    return jnp.concatenate([p[at, :] for p in pieces], axis=0).astype(F32)


def gather_mask(pieces, i, rows, body):
    cols = []
    for p in pieces:
        block = p[body : body + PAD, :LANES].astype(F32).T
        cols.append(
            jnp.sum(jnp.where(iota(block.shape, 1) == i, block, 0.0), axis=1, keepdims=True)[:rows]
        )
    return jnp.concatenate(cols, axis=0)


def two_heads(block, size):
    zero = jnp.zeros((size, block.shape[1]), block.dtype)
    return jnp.concatenate(
        [
            jnp.concatenate([block[:size], zero], axis=0),
            jnp.concatenate([zero, block[size:]], axis=0),
        ],
        axis=1,
    )


def attend_call(pieces, gain, shift, qkv, query_bias, value_bias, images, rows, after):
    count = len(pieces)
    width = qkv.shape[0]
    seq = count * rows
    size = width // HEADS
    body = images * rows
    scale = size ** (-0.5)

    def kernel(*refs):
        ps = refs[:count]
        gain_ref, shift_ref, qkv_ref, qb_ref, vb_ref = refs[count : count + 5]
        outs = refs[count + 6 : 2 * count + 6]
        qt_ref, k_ref, v_ref, lse_ref, ot, vt = refs[2 * count + 6 :]
        i = pl.program_id(0)
        x = gather_image(ps, i, rows)
        live = gather_mask(ps, i, rows, body) > 0
        xhat, _ = norm_stats(x)
        n = (xhat * gain_ref[...] + shift_ref[...]).astype(BF16)
        qt_ref[0] = ((dot_nn(n, qkv_ref[:, :width]) + qb_ref[...]) * scale).astype(BF16).T
        k_ref[0] = dot_nn(n, qkv_ref[:, width : 2 * width]).astype(BF16)
        v = (dot_nn(n, qkv_ref[:, 2 * width :]) + vb_ref[...]).astype(BF16)
        v_ref[0] = v
        vt[...] = v.T
        for h in range(0, HEADS, 2):
            pair = slice(h * size, (h + 2) * size)
            s = dot_nn(k_ref[0, :, pair], two_heads(qt_ref[0, pair, :], size))
            s = jnp.where(live, s, NEG)
            top = jnp.max(s, axis=0, keepdims=True)
            e = jnp.exp(s - top)
            total = jnp.sum(e, axis=0, keepdims=True)
            lse_ref[0, h // 2 : h // 2 + 1, :] = top + jnp.log(total)
            p = (e * (1.0 / total)).astype(BF16)
            for k in range(2):
                at = slice((h + k) * size, (h + k + 1) * size)
                ot[at, :] = dot_nn(vt[at, :], p[:, k * seq : (k + 1) * seq])
        o = ot[...].T.astype(BF16)
        at = pl.ds(pl.multiple_of(i * rows, rows), rows)
        for d in range(count):
            outs[d][at, :] = o[d * rows : (d + 1) * rows]

    full = lambda a: pl.BlockSpec(a.shape, lambda i: (0,) * a.ndim)
    ins = list(pieces) + [gain, shift, qkv, query_bias, value_bias]
    per_image = lambda dims: pl.BlockSpec((1,) + dims, lambda i: (i, 0, 0))
    saved = [(width, seq), (seq, width), (seq, width), (HEADS // 2, 2 * seq)]
    return pl.pallas_call(
        kernel,
        grid=(images,),
        in_specs=[full(a) for a in ins] + [ANY_SPEC],
        out_specs=[pl.BlockSpec((body, width), lambda i: (0, 0))] * count
        + [per_image(dims) for dims in saved],
        out_shape=[shape((body, width), BF16)] * count
        + [shape((images,) + dims, BF16) for dims in saved[:3]]
        + [shape((images,) + saved[3], F32)],
        scratch_shapes=[pltpu.VMEM((width, seq), F32), pltpu.VMEM((width, seq), BF16)],
        compiler_params=params(58),
        cost_estimate=takes(12),
        name="attend",
    )(*ins, after)


def middle_call(place, attended, pieces, proj, proj_bias, gain, shift, dest_rows, expert_count, capacity):
    count = len(attended)
    body, width = attended[0].shape
    tok = count * body

    def kernel(place_ref, *refs):
        att, ps = refs[:count], refs[count : 2 * count]
        proj_ref, pb_ref, gain_ref, shift_ref, dest_ref = refs[2 * count : 2 * count + 5]
        mid_ref, n_ref = refs[2 * count + 5 : 2 * count + 7]
        slots = refs[2 * count + 7 :]
        expert = place_ref[1]
        for d in range(count):
            at = slice(d * body, (d + 1) * body)
            mid = (
                ps[d][:body, :].astype(F32) + dot_nn(att[d][...], proj_ref[...]) + pb_ref[...]
            )
            mid_ref[at, :] = mid
            xhat, _ = norm_stats(mid)
            n_ref[at, :] = (xhat * gain_ref[...] + shift_ref[...]).astype(BF16)
        n = n_ref[...]
        d0, d1 = dest_ref[0:1, :], dest_ref[1:2, :]
        for d in range(expert_count):
            ids_here = iota((capacity, tok), 0) + (expert ^ d) * capacity
            pick = ((ids_here == d0) | (ids_here == d1)).astype(F32).astype(BF16)
            slots[d][...] = dot_nn(pick, n).astype(BF16)

    ins = list(attended) + list(pieces) + [proj, proj_bias, gain, shift, dest_rows]
    return pl.pallas_call(
        kernel,
        in_specs=[SMEM_SPEC] + [VMEM_SPEC] * len(ins),
        out_specs=[VMEM_SPEC] * (2 + expert_count),
        out_shape=[shape((tok, width), F32), shape((tok, width), BF16)]
        + [shape((capacity, width), BF16)] * expert_count,
        compiler_params=params(58),
        cost_estimate=takes(5),
        name="middle",
    )(place, *ins)


def expert_call(
    place, xs, upstream, first, router, up, up_bias, down, down_bias, held, expert_count, after
):
    blocks = len(xs)
    capacity, width = xs[0].shape
    hidden_width = up.shape[1]
    total = blocks * capacity
    chunk = EXPERT_CHUNK
    steps = hidden_width // chunk
    sub = min(total, 384)
    ins = list(xs) + [upstream, router, up, up_bias, down, down_bias]
    n_own = len(ins)
    ins += [] if held is None else list(held)
    n_in = len(ins) + len(after)

    def kernel(place_ref, *refs):
        x_refs, u_ref = refs[:blocks], refs[blocks]
        rw, up_ref, ub_ref, dn_ref, db_ref = refs[blocks + 1 : blocks + 6]
        o = refs[n_in:]
        out_ref, g_all, act, gh_all = o[:4]
        gx_refs = o[4 : 4 + blocks]
        x_all, gate, out_acc, gx_acc = o[4 + blocks :]
        j = pl.program_id(0)
        slots = [lax.rem(place_ref[1] ^ (first + b), blocks) for b in range(blocks)]

        @pl.when(j == 0)
        def _():
            expert = place_ref[1]
            for b in range(blocks):
                at = slice(b * capacity, (b + 1) * capacity)
                x = x_refs[b][...]
                gates = soft_gates(dot_nn(x, rw[...]), expert_count)
                mine = jnp.sum(
                    jnp.where(iota(gates.shape, 1) == expert, gates, 0.0), axis=1, keepdims=True
                )
                x_all[at, :] = x
                g_all[at, :] = (u_ref[slots[b]].astype(F32) * mine).astype(BF16)
                gate[at, :] = jnp.broadcast_to(mine, (capacity, LANES))
            out_acc[...] = jnp.zeros_like(out_acc)
            gx_acc[...] = jnp.zeros_like(gx_acc)

        w_up, w_dn = up_ref[...], dn_ref[...]
        for r in range(total // sub):
            at = slice(r * sub, (r + 1) * sub)
            h = dot_nn(x_all[at, :], w_up) + ub_ref[...]
            a, slope = gelu_parts(h)
            a = a.astype(BF16)
            act[at, :] = a
            out_acc[at, :] += dot_nn(a, w_dn)
            gh = (dot_nt(g_all[at, :], w_dn) * slope).astype(BF16)
            gh_all[at, :] = gh
            gx_acc[at, :] += dot_nt(gh, w_up)

        @pl.when(j == steps - 1)
        def _():
            for b in range(blocks):
                at = slice(b * capacity, (b + 1) * capacity)
                out = (out_acc[at, :] + db_ref[...]).astype(BF16).astype(F32)
                out_ref[slots[b]] = (out * gate[at, :1]).astype(BF16)
                gg = jnp.sum(out * u_ref[slots[b]].astype(F32), axis=1, keepdims=True)
                line = jnp.broadcast_to(gg, (capacity, LANES)).T[:PAD]
                high = line.astype(BF16).astype(F32)
                mean = (line - high).astype(BF16).astype(F32)
                k = iota(line.shape, 0)
                parts = jnp.where(
                    k == 0, high, jnp.where(k == 1, mean, jnp.where(k == 2, line - high - mean, 0.0))
                )
                gx_refs[b][:capacity, :] = gx_acc[at, :].astype(BF16)
                gx_refs[b][capacity:, :] = jnp.concatenate(
                    [parts, jnp.zeros((PAD, width - capacity), F32)], axis=1
                ).astype(BF16)

    full = lambda a: pl.BlockSpec(a.shape, lambda j, p: (0,) * a.ndim)
    const = lambda dims: pl.BlockSpec(dims, lambda j, p: (0,) * len(dims))
    blocks_of = pl.BlockSpec((blocks, capacity, width), lambda j, p: ((p[1] ^ first) // blocks, 0, 0))
    hidden_of = pl.BlockSpec((total, chunk), lambda j, p: (first // blocks, j))
    specs = (
        [full(a) for a in xs]
        + [full(upstream) if upstream.shape[0] == blocks else blocks_of]
        + [
            full(router),
            pl.BlockSpec((width, chunk), lambda j, p: (0, j)),
            pl.BlockSpec((1, chunk), lambda j, p: (0, j)),
            pl.BlockSpec((chunk, width), lambda j, p: (j, 0)),
            full(down_bias),
        ]
        + [ANY_SPEC] * (len(ins) - n_own)
    )
    return pl.pallas_call(
        kernel,
        grid_spec=pltpu.PrefetchScalarGridSpec(
            num_scalar_prefetch=1,
            grid=(steps,),
            in_specs=specs + [ANY_SPEC] * len(after),
            out_specs=[
                blocks_of,
                pl.BlockSpec((total, width), lambda j, p: (first // blocks, 0)),
                hidden_of,
                hidden_of,
            ]
            + [const((capacity + PAD, width))] * blocks,
            scratch_shapes=[
                pltpu.VMEM((total, width), BF16),
                pltpu.VMEM((total, LANES), F32),
                pltpu.VMEM((total, width), F32),
                pltpu.VMEM((total, width), F32),
            ],
        ),
        out_shape=[
            pltpu.HBM((expert_count, capacity, width), BF16),
            pltpu.HBM((expert_count * capacity, width), BF16),
            pltpu.HBM((expert_count * capacity, hidden_width), BF16),
            pltpu.HBM((expert_count * capacity, hidden_width), BF16),
        ]
        + [pltpu.HBM((capacity + PAD, width), BF16)] * blocks,
        input_output_aliases={} if held is None else {1 + n_own + k: k for k in range(4)},
        compiler_params=params(24),
        cost_estimate=takes(9),
        name="expert",
    )(place, *ins, *after)


def weights_call(place, xs, grads, act, grad_hidden, n_ctx, n_dp):
    capacity, width = xs[0].shape
    hidden_width = act.shape[1]
    total = len(xs) * capacity
    chunk = width
    steps = hidden_width // chunk
    per_step = n_ctx * n_dp // steps
    part = chunk // per_step
    piece_rows = 2 * part + PAD
    nx = len(xs)

    def kernel(place_ref, *refs):
        x_refs, (g_ref, act_ref, gh_ref), refs = refs[:nx], refs[nx : nx + 3], refs[nx + 3 :]
        grad_refs, (x_t, g_t, down_bias_sum) = refs[:n_dp], refs[n_dp:]
        j = pl.program_id(0)

        @pl.when(j == 0)
        def _():
            x_t[:width, :] = jnp.concatenate([r[...] for r in x_refs], axis=0).T
            x_t[width:, :] = jnp.ones((PAD, total), BF16)
            g_t[...] = g_ref[...].T
            down_bias_sum[...] = jnp.sum(g_ref[...].astype(F32), axis=0, keepdims=True)

        g_up = dot_nn(x_t[...], gh_ref[...])
        g_dn = dot_nn(g_t[...], act_ref[...]).T
        row = iota((PAD, width), 0)
        extra = jnp.where(row == 0, g_up[width:], 0.0)
        extra = jnp.where((row == 1) & (j == 0), down_bias_sum[...], extra)
        for k in range(per_step):
            vals = (
                g_up[k * part : (k + 1) * part].astype(BF16),
                g_dn[k * part : (k + 1) * part].astype(BF16),
                extra.astype(BF16) if k == 0 else jnp.zeros((PAD, width), BF16),
            )
            piece = j * per_step + k
            slot = lax.rem(piece, n_ctx) ^ place_ref[0]

            def put(ref):
                ref[slot, :part, :] = vals[0]
                ref[slot, part : 2 * part, :] = vals[1]
                ref[slot, 2 * part :, :] = vals[2]

            @pl.when(piece // n_ctx == place_ref[2])
            def _():
                put(grad_refs[0])

            @pl.when(piece // n_ctx != place_ref[2])
            def _():
                put(grad_refs[1])

    full = lambda a: pl.BlockSpec(a.shape, lambda j: (0,) * a.ndim)
    hidden_of = lambda a: pl.BlockSpec((a.shape[0], chunk), lambda j: (0, j))
    return pl.pallas_call(
        kernel,
        grid=(steps,),
        in_specs=[SMEM_SPEC]
        + [full(a) for a in xs]
        + [full(grads), hidden_of(act), hidden_of(grad_hidden)],
        out_specs=[pl.BlockSpec((n_ctx, piece_rows, width), lambda j: (0, 0, 0))] * n_dp,
        out_shape=[shape((n_ctx, piece_rows, width), BF16)] * n_dp,
        scratch_shapes=[
            pltpu.VMEM((width + PAD, total), BF16),
            pltpu.VMEM((width, total), BF16),
            pltpu.VMEM((1, width), F32),
        ],
        compiler_params=params(58),
        cost_estimate=takes(13),
        name="weights",
    )(place, *xs, grads, act, grad_hidden)


def slot_match(dest_ref, at, first, capacity):
    d = dest_ref[at, :]
    lanes = iota((d.shape[0], capacity), 1) + first
    return ((lanes == d[:, 0:1]) | (lanes == d[:, 1:2])).astype(F32).astype(BF16)


def output_call(place, results, mid, dest_cols, groups):
    blocks, capacity, width = results.shape
    tok = mid.shape[0]
    body = tok // groups

    def kernel(place_ref, o_ref, mid_ref, dest_ref, out_ref):
        rows = o_ref[...].reshape(blocks * capacity, width)
        for g in range(groups):
            at = slice(g * body, (g + 1) * body)
            acc = mid_ref[at, :] + dot_nn(slot_match(dest_ref, at, 0, blocks * capacity), rows)
            out_ref[place_ref[0] ^ g] = acc.astype(BF16)

    return pl.pallas_call(
        kernel,
        in_specs=[SMEM_SPEC] + [VMEM_SPEC] * 3,
        out_specs=VMEM_SPEC,
        out_shape=shape((groups, body, width), BF16),
        compiler_params=params(58),
        cost_estimate=takes(30),
        name="output",
    )(place, results, mid, dest_cols)


def middle_back_call(
    place, gxs, mid, normed, cotangent, dest_cols, router, gain, proj, expert_count, after
):
    blocks = len(gxs)
    groups, body, width = cotangent.shape
    capacity = gxs[0].shape[0] - PAD
    tok = groups * body
    def kernel(place_ref, *refs):
        gx_refs = refs[:blocks]
        mid_ref, n_ref, cot_ref, dest_ref = refs[blocks : blocks + 4]
        router_ref, gain_ref, proj_ref = refs[blocks + 4 : blocks + 7]
        refs = refs[blocks + 7 + len(after) :]
        gmid_ref, ga_refs = refs[0], refs[1 : 1 + groups]
        branch_t, logit_t, vec_ref, slot_rows = refs[1 + groups :]
        ctx, expert = place_ref[0], place_ref[1]
        for d in range(blocks):
            at = pl.ds(pl.multiple_of((expert ^ d) * capacity, PAD), capacity)
            slot_rows[at, :width] = gx_refs[d][:capacity, :]
            cols = gx_refs[d][capacity:, :].astype(F32).T
            lane = iota((capacity, LANES), 1) == (expert ^ d)
            for k in range(3):
                slot_rows[at, width + k * LANES : width + (k + 1) * LANES] = jnp.where(
                    lane, cols[:capacity, k : k + 1], 0.0
                ).astype(BF16)
        g_gain = jnp.zeros((1, width), F32)
        g_shift = jnp.zeros((1, width), F32)
        g_proj_bias = jnp.zeros((1, width), F32)
        for g in range(groups):
            at = slice(g * body, (g + 1) * body)
            both = dot_nn(slot_match(dest_ref, at, 0, blocks * capacity), slot_rows[...])
            gn = both[:, :width]
            gg = both[:, width : width + LANES] + (
                both[:, width + LANES : width + 2 * LANES] + both[:, width + 2 * LANES :]
            )
            gates = soft_gates(dot_nn(n_ref[at, :], router_ref[...]), expert_count)
            logit = gates * (gg - jnp.sum(gates * gg, axis=1, keepdims=True))
            logit_t[:, at] = logit.T.astype(BF16)
            gn = gn + dot_nt(logit.astype(BF16), router_ref[...])
            xhat, inv = norm_stats(mid_ref[at, :])
            g_gain = g_gain + jnp.sum(gn * xhat, axis=0, keepdims=True)
            g_shift = g_shift + jnp.sum(gn, axis=0, keepdims=True)
            gmid = cot_ref[ctx ^ g].astype(F32) + norm_back(gn * gain_ref[...], xhat, inv)
            gmid_ref[at, :] = gmid
            branch = gmid.astype(BF16)
            g_proj_bias = g_proj_bias + jnp.sum(branch.astype(F32), axis=0, keepdims=True)
            branch_t[:, at] = branch.T
            ga_refs[g][...] = dot_nt(branch, proj_ref[...]).astype(BF16)
        k = iota((PAD, width), 0)
        rows = jnp.zeros((PAD, width), F32)
        for s, vec in enumerate((g_gain, g_shift, g_proj_bias)):
            rows = jnp.where(k == s, vec, rows)
        vec_ref[...] = rows

    ins = (
        list(gxs) + [mid, normed, cotangent, dest_cols] + [router, gain, proj]
    )
    return pl.pallas_call(
        kernel,
        in_specs=[SMEM_SPEC] + [VMEM_SPEC] * len(ins) + [ANY_SPEC] * len(after),
        out_specs=[VMEM_SPEC] * (4 + groups),
        out_shape=[shape((tok, width), F32)]
        + [shape((body, width), BF16)] * groups
        + [shape((width, tok), BF16), shape((LANES, tok), BF16), shape((PAD, width), F32)],
        scratch_shapes=[pltpu.VMEM((blocks * capacity, width + 3 * LANES), BF16)],
        compiler_params=params(58),
        cost_estimate=takes(30),
        name="middle_back",
    )(place, *ins, *after)


def shared_back_call(branch_t, logit_t, vectors, normed, attended, expert_count):
    groups = len(attended)
    width, tok = branch_t.shape
    body = tok // groups
    misc = -(-(expert_count + 3) // PAD) * PAD

    def kernel(branch_ref, logit_ref, vec_ref, n_ref, *refs):
        shared_ref, att_all = refs[groups:]
        for g in range(groups):
            att_all[g * body : (g + 1) * body, :] = refs[g][...]
        shared_ref[:width, :] = dot_nn(branch_ref[...], att_all[...]).astype(BF16)
        rows = dot_nn(logit_ref[...], n_ref[...])[:misc]
        k = iota((misc, width), 0)
        for s in range(3):
            rows = jnp.where(k == expert_count + s, vec_ref[s : s + 1, :], rows)
        shared_ref[width:, :] = rows.astype(BF16)

    return pl.pallas_call(
        kernel,
        in_specs=[VMEM_SPEC] * (4 + groups),
        out_specs=VMEM_SPEC,
        out_shape=shape((width + misc, width), BF16),
        scratch_shapes=[pltpu.VMEM((tok, width), BF16)],
        compiler_params=params(58),
        cost_estimate=takes(3),
        name="shared_back",
    )(branch_t, logit_t, vectors, normed, *attended)


def attend_back_call(
    place, pieces, grads, saved, shared, gain, shift, qkv, images, rows, n_dp, after
):
    count = len(pieces)
    width = qkv.shape[0]
    seq = count * rows
    size = width // HEADS
    body = images * rows
    scale = size ** (-0.5)
    part = (4 * width) // (n_dp * count)
    extra_rows = shared.shape[0] - width

    def kernel(place_ref, *refs):
        ps, gs = refs[:count], refs[count : 2 * count]
        qt_ref, k_ref, v_ref, lse_ref, shared_ref, gain_ref, shift_ref, qkv_ref = refs[
            2 * count : 2 * count + 8
        ]
        refs = refs[2 * count + 8 + len(after) :]
        gin_ref, sums = refs[0], refs[1 : 1 + n_dp]
        gt, w_acc, gain_acc, shift_acc, qb_acc, vb_acc = refs[1 + n_dp :]
        i = pl.program_id(0)
        x = gather_image(ps, i, rows)
        live = gather_mask(ps, i, rows, body) > 0
        xhat, inv = norm_stats(x)
        n = (xhat * gain_ref[...] + shift_ref[...]).astype(BF16)
        out_t = gather_image(gs, i, rows).astype(BF16).T
        k, v, qt = k_ref[0], v_ref[0], qt_ref[0]
        kt = k.T
        for h in range(0, HEADS, 2):
            pair = slice(h * size, (h + 2) * size)
            s = dot_nn(k[:, pair], two_heads(qt[pair], size))
            p = jnp.exp(jnp.where(live, s, NEG) - lse_ref[0, h // 2 : h // 2 + 1, :])
            dp = dot_nn(v[:, pair], two_heads(out_t[pair], size))
            pdp = p * dp
            ds = (pdp - p * jnp.sum(pdp, axis=0, keepdims=True)).astype(BF16)
            p = p.astype(BF16)
            for m in range(2):
                at = slice((h + m) * size, (h + m + 1) * size)
                one = slice(m * seq, (m + 1) * seq)
                gt[at, :] = (dot_nn(kt[at], ds[:, one]) * scale).astype(BF16)
                gt[width + at.start : width + at.stop, :] = dot_nt(qt[at], ds[:, one]).astype(BF16)
                gt[2 * width + at.start : 2 * width + at.stop, :] = dot_nt(
                    out_t[at], p[:, one]
                ).astype(BF16)
        gall = gt[...]
        gw = dot_nn(gall, n)
        gn = dot_nn(qkv_ref[...], gall).T
        qb = gall[:width].astype(F32)
        vb = gall[2 * width :].astype(F32)
        g_gain = jnp.sum(gn * xhat, axis=0, keepdims=True)
        g_shift = jnp.sum(gn, axis=0, keepdims=True)

        @pl.when(i == 0)
        def _():
            w_acc[...] = jnp.zeros_like(w_acc)
            gain_acc[...] = jnp.zeros_like(gain_acc)
            shift_acc[...] = jnp.zeros_like(shift_acc)
            qb_acc[...] = jnp.zeros_like(qb_acc)
            vb_acc[...] = jnp.zeros_like(vb_acc)

        w_acc[...] += gw
        gain_acc[...] += g_gain
        shift_acc[...] += g_shift
        qb_acc[...] += qb
        vb_acc[...] += vb
        gin = norm_back(gn * gain_ref[...], xhat, inv).astype(BF16)
        at = pl.ds(pl.multiple_of(i * rows, rows), rows)
        for d in range(count):
            gin_ref[place_ref[0] ^ d, at, :] = gin[d * rows : (d + 1) * rows]

        @pl.when(i == images - 1)
        def _():
            rows_of = [
                jnp.broadcast_to(jnp.sum(a[...], axis=1, keepdims=True), (width, LANES)).T[:1]
                for a in (qb_acc, vb_acc)
            ]
            k16 = iota((PAD, width), 0)
            vecs = jnp.zeros((PAD, width), F32)
            for s, vec in enumerate((gain_acc[...], shift_acc[...], *rows_of)):
                vecs = jnp.where(k16 == s, vec, vecs)
            for p in range(n_dp * count):
                first = p * part
                if first < 3 * width:
                    block = w_acc[first : first + part, :].astype(BF16)
                else:
                    block = shared_ref[first - 3 * width : first - 3 * width + part, :]
                if p == 0:
                    extra = vecs.astype(BF16)
                elif p * PAD <= extra_rows:
                    extra = shared_ref[width + (p - 1) * PAD : width + p * PAD, :]
                else:
                    extra = jnp.zeros((PAD, width), BF16)
                slot = p % count ^ place_ref[0]

                def put(ref):
                    ref[slot, :part, :] = block
                    ref[slot, part:, :] = extra

                @pl.when(place_ref[2] == p // count)
                def _():
                    put(sums[0])

                @pl.when(place_ref[2] != p // count)
                def _():
                    put(sums[1])

    full = lambda a: pl.BlockSpec(a.shape, lambda i: (0,) * a.ndim)
    const = lambda dims: pl.BlockSpec(dims, lambda i: (0,) * len(dims))
    per_image = lambda a: pl.BlockSpec((1,) + a.shape[1:], lambda i: (i, 0, 0))
    rest = [shared, gain, shift, qkv]
    return pl.pallas_call(
        kernel,
        grid=(images,),
        in_specs=[SMEM_SPEC] + [full(a) for a in pieces]
        + [full(a) for a in grads]
        + [per_image(a) for a in saved]
        + [full(a) for a in rest]
        + [ANY_SPEC] * len(after),
        out_specs=[const((count, body, width))] + [const((count, part + PAD, width))] * n_dp,
        out_shape=[shape((count, body, width), BF16)]
        + [shape((count, part + PAD, width), BF16)] * n_dp,
        scratch_shapes=[
            pltpu.VMEM((3 * width, seq), BF16),
            pltpu.VMEM((3 * width, width), F32),
            pltpu.VMEM((1, width), F32),
            pltpu.VMEM((1, width), F32),
            pltpu.VMEM((width, seq), F32),
            pltpu.VMEM((width, seq), F32),
        ],
        compiler_params=params(58),
        cost_estimate=takes(20),
        name="attend_back",
    )(place, *pieces, *grads, *saved, *rest, *after)


def input_call(place, gmid, gins, after):
    groups, body, width = gins.shape

    def kernel(place_ref, gmid_ref, gin_ref, *refs):
        for g in range(groups):
            group = place_ref[0] ^ g
            refs[-1][group] = (
                gmid_ref[g * body : (g + 1) * body, :] + gin_ref[group].astype(F32)
            ).astype(BF16)

    return pl.pallas_call(
        kernel,
        in_specs=[SMEM_SPEC] + [VMEM_SPEC] * 2 + [ANY_SPEC] * len(after),
        out_specs=VMEM_SPEC,
        out_shape=shape((groups, body, width), BF16),
        compiler_params=params(58),
        cost_estimate=takes(3),
        name="input",
    )(place, gmid, gins, *after)


def expert_grads_call(place, pieces, first, step, n_ctx, hidden_width, half):
    piece_rows, width = pieces[0].shape[1:]
    arrays = len(pieces)
    count = sum(a.shape[0] for a in pieces)
    chunk = width
    per_step = 2 * n_ctx * chunk // hidden_width
    part = chunk // per_step
    half = [] if half is None else list(half)

    def piece_of(q, p):
        return (p[2] ^ (first[0] + q * step[0])) * n_ctx + (p[0] ^ (first[1] + q * step[1]))

    def kernel(place_ref, *refs):
        ins, refs = refs[:arrays], refs[arrays:]
        up_ref, down_ref, up_bias_ref, down_bias_ref = refs[len(half) :]
        q = pl.program_id(0)
        piece = piece_of(q, place_ref)
        if half:

            @pl.when(q == 0)
            def _():
                up_bias_ref[...] = refs[2][...]
                down_bias_ref[...] = refs[3][...]

        extra = jnp.zeros((PAD, width), F32)
        for i, ref in enumerate(ins):
            here = (q == i) if arrays > 1 else (q >= 0)

            @pl.when(here)
            def _():
                up_ref[...] = ref[0, :part, :].astype(F32)
                down_ref[...] = ref[0, part : 2 * part, :].astype(F32)

            extra = jnp.where(here, ref[0, 2 * part :, :].astype(F32), extra)

        @pl.when(lax.rem(piece, per_step) == 0)
        def _():
            at = pl.multiple_of(piece // per_step * chunk, chunk)
            up_bias_ref[:, pl.ds(at, chunk)] = extra[0:1]

        @pl.when(piece == 0)
        def _():
            down_bias_ref[...] = extra[1:2]

    biases = [
        pl.BlockSpec((1, hidden_width), lambda q, p: (0, 0)),
        pl.BlockSpec((1, width), lambda q, p: (0, 0)),
    ]
    return pl.pallas_call(
        kernel,
        grid_spec=pltpu.PrefetchScalarGridSpec(
            num_scalar_prefetch=1,
            grid=(count,),
            in_specs=[
                pl.BlockSpec(
                    (1, piece_rows, width), lambda q, p: (q if arrays == 1 else 0, 0, 0)
                )
            ]
            * arrays
            + ([ANY_SPEC] * 2 + biases if half else []),
            out_specs=[
                pl.BlockSpec(
                    (part, chunk),
                    lambda q, p: (lax.rem(piece_of(q, p), per_step), piece_of(q, p) // per_step),
                ),
                pl.BlockSpec((part, width), lambda q, p: (piece_of(q, p), 0)),
            ]
            + biases,
        ),
        out_shape=[
            shape((width, hidden_width), F32),
            shape((hidden_width, width), F32),
            shape((1, hidden_width), F32),
            shape((1, width), F32),
        ],
        input_output_aliases={1 + arrays: 0, 2 + arrays: 1} if half else {},
        compiler_params=params(58),
        cost_estimate=takes(3),
        name="expert_grads",
    )(place, *pieces, *half)


def shared_grads_call(place, pieces, width, expert_count):
    n_ctx, rows, share = pieces[0].shape
    count = len(pieces) * n_ctx
    part = rows - PAD

    def kernel(place_ref, *refs):
        ins, refs = refs[: len(pieces)], refs[len(pieces) :]
        qkv_ref, proj_ref, router_ref = refs[:3]
        vec_refs, (hold, extra) = refs[3:10], refs[10:]
        for q in range(count):
            piece = (place_ref[2] ^ (q // n_ctx)) * n_ctx + (place_ref[0] ^ (q % n_ctx))
            hold[piece] = ins[q // n_ctx][q % n_ctx].astype(F32)
        for p in range(count):
            block = hold[p, :part, :].T
            if p * part < 3 * width:
                qkv_ref[:, p * part : (p + 1) * part] = block
            else:
                proj_ref[:, p * part - 3 * width : (p + 1) * part - 3 * width] = block
            extra[p * PAD : (p + 1) * PAD, :] = hold[p, part:, :]
        router_ref[...] = extra[PAD : PAD + expert_count, :]
        for s in range(4):
            vec_refs[s][...] = extra[s : s + 1, :]
        for s in range(3):
            vec_refs[4 + s][...] = extra[PAD + expert_count + s : PAD + expert_count + s + 1, :]

    return pl.pallas_call(
        kernel,
        in_specs=[SMEM_SPEC] + [VMEM_SPEC] * len(pieces),
        out_specs=[VMEM_SPEC] * 10,
        out_shape=[shape((share, 3 * width), F32), shape((share, width), F32), shape((expert_count, share), F32)]
        + [shape((1, share), F32)] * 7,
        scratch_shapes=[pltpu.VMEM((count, rows, share), F32), pltpu.VMEM((count * PAD, share), F32)],
        compiler_params=params(58),
        cost_estimate=takes(3),
        name="shared_grads",
    )(place, *pieces)


def swap(x, axis, d, size, what="sums"):
    with jax.named_scope(f"{what}_{axis}_{d}"):
        return lax.ppermute(x, axis, [(i, i ^ d) for i in range(size)])


def exchange(x, axis, what):
    with jax.named_scope(what):
        return lax.all_to_all(x, axis, split_axis=0, concat_axis=0, tiled=True)


def pick(x, i):
    return lax.dynamic_index_in_dim(x, i, 0, keepdims=False)


class Order:
    def __init__(self):
        self.seen = []

    def after(self, x, *others):
        x, others = lax.optimization_barrier((x, others))
        self.seen += others
        return x


def add_all(parts):
    acc = parts[0].astype(F32)
    for p in parts[1:]:
        acc = acc + p.astype(F32)
    return acc.astype(BF16)


def reduce_ctx(parts, n_ctx, what):
    return [parts[0]] + [swap(parts[d], "ctx", d, n_ctx, what) for d in range(1, n_ctx)]


def local(
    mesh_sizes,
    tokens,
    cotangent,
    key_mask,
    route_ids,
    priority,
    norm1_gain,
    norm1_bias,
    qkv_weight,
    query_bias,
    value_bias,
    proj_weight,
    proj_bias,
    norm2_gain,
    norm2_bias,
    router_weight,
    expert_up,
    expert_up_bias,
    expert_down,
    expert_down_bias,
):
    n_expert, n_ctx, n_dp = mesh_sizes
    order = Order()
    images_all, rows, width = tokens.shape
    tok = images_all * rows
    images = images_all // n_ctx
    body = images * rows
    expert_count = router_weight.shape[1]
    capacity = max(2, 2 * tok // expert_count)
    ctx, expert, core = (lax.axis_index(a) for a in ("ctx", "expert", "dp"))
    place = jnp.stack([ctx, expert, core]).astype(I32)

    mine = pieces_call(place, tokens.reshape(n_ctx, body, width), key_mask)
    pieces = [mine[0]] + [swap(mine[d], "ctx", d, n_ctx, "tokens") for d in range(1, n_ctx)]

    token_of = jnp.arange(tok, dtype=I32).reshape(n_ctx, body)
    ints4 = jnp.stack(
        [
            route_ids[..., 0].reshape(n_ctx, body),
            route_ids[..., 1].reshape(n_ctx, body),
            priority.reshape(n_ctx, body) * tok + token_of,
        ],
        axis=1,
    )
    ints = jnp.concatenate([pick(ints4, ctx ^ d) for d in range(n_ctx)], axis=1)
    ints = jnp.pad(ints, ((0, 5), (0, 0)))
    cot4 = cotangent.reshape(n_ctx, body, width)
    dest_rows, dest_cols, u_send, u_own = route_call(place, ints, cot4, expert_count, capacity)
    u_came = exchange(u_send, "expert", "upstream")

    row = lambda v: v.reshape(1, -1)
    att = attend_call(
        pieces, row(norm1_gain), row(norm1_bias), qkv_weight, row(query_bias), row(value_bias), images, rows,
        dest_rows,
    )
    att_out, saved = att[:n_ctx], att[n_ctx:]
    attended = [att_out[0]] + [swap(att_out[d], "ctx", d, n_ctx, "attended") for d in range(1, n_ctx)]

    mid, normed2, *x_send = middle_call(
        place, attended, mine, proj_weight, row(proj_bias), row(norm2_gain), row(norm2_bias), dest_rows,
        expert_count, capacity,
    )

    router = jnp.pad(router_weight, ((0, 0), (0, LANES - expert_count)))
    held, gxs = None, []
    group = max(1, n_expert // EXPERT_CALLS)
    late = n_expert - group if n_expert > group else n_expert
    xs = [x_send[0]] + [swap(x_send[d], "expert", d, n_expert, "rows") for d in range(1, late)]
    for first in range(0, n_expert, group):
        res = expert_call(
            place, xs[first : first + group], u_own if first + group == 1 else u_came, first, router, expert_up[0],
            expert_up_bias, expert_down[0], expert_down_bias, held, expert_count,
            gxs[1:2] if first + group == n_expert else [],
        )
        gxs += [
            g if first + b == 0 else swap(g, "expert", first + b, n_expert, "rows_grad")
            for b, g in enumerate(res[4:])
        ]
        held = res[:4]
        if first == 0:
            xs += [
                swap(order.after(x_send[d], gxs[0]), "expert", d, n_expert, "rows")
                for d in range(late, n_expert)
            ]
    results, *held = held
    stay, go = weights_call(place, xs, *held, n_ctx, n_dp)
    came = swap(order.after(go, gxs[2]), "dp", 1, n_dp, "expert_terms")
    gxs[0] = order.after(gxs[0], stay)
    grad_mid, *rest = middle_back_call(
        place, gxs, mid, normed2, cot4, dest_cols, router, row(norm2_gain), proj_weight, expert_count,
        [],
    )
    ga_send, rest = rest[:n_ctx], rest[n_ctx:]
    shared = shared_back_call(*rest, normed2, attended, expert_count)
    gas = [ga_send[0]] + [swap(ga_send[d], "ctx", d, n_ctx, "attended_grad") for d in range(1, n_ctx)]
    results = order.after(results, ga_send[0])
    came = order.after(came, ga_send[0])
    terms = [add_all([stay[g], came[g]]) for g in range(n_ctx)]
    gas[0] = order.after(gas[0], *terms)
    terms = reduce_ctx(order.after(terms, *gas), n_ctx, "expert_terms")
    results = exchange(results, "expert", "results")

    gin_send, flat_stay, flat_go = attend_back_call(
        place, pieces, gas, saved, shared, row(norm1_gain), row(norm1_bias), qkv_weight, images, rows, n_dp, [],
    )
    terms, flat_go = lax.optimization_barrier((terms, flat_go))
    sums = add_all(terms)
    own = [sums] + [swap(sums, "ctx", d, n_ctx, "expert_sums") for d in range(1, n_ctx - 1)]

    share = width // n_expert
    flat = add_all([flat_stay, swap(flat_go, "dp", 1, n_dp, "shared")])
    cut = [lax.dynamic_slice_in_dim(flat, (expert ^ d) * share, share, 2) for d in range(n_expert)]
    cut = [cut[0]] + [swap(cut[d], "expert", d, n_expert, "shared") for d in range(1, n_expert)]

    hidden_width = expert_up.shape[2]
    gins = exchange(order.after(gin_send, results, cut[1]), "ctx", "input_grad")
    last = swap(order.after(sums, gins), "ctx", n_ctx - 1, n_ctx, "expert_sums")
    block_out = output_call(place, order.after(results, cut[1]), mid, dest_cols, n_ctx)
    early = jnp.stack(order.after(own, cut[1]))
    grads = expert_grads_call(place, [early], (0, 0), (0, 1), n_ctx, hidden_width, None)
    early = swap(early, "dp", 1, n_dp, "expert_sums")
    grads = expert_grads_call(place, [early], (1, 0), (0, 1), n_ctx, hidden_width, grads)
    cut = order.after(cut, grads[3], block_out, gins)

    part = add_all(cut)
    part = add_all(reduce_ctx([part[g] for g in range(n_ctx)], n_ctx, "shared"))
    part = jnp.stack(order.after(reduce_ctx([part] * n_ctx, n_ctx, "shared_sums"), last))
    every = [part, swap(part, "dp", 1, n_dp, "shared_sums")]
    grad_up, grad_down, grad_up_bias, grad_down_bias = expert_grads_call(
        place, [last[None], swap(last, "dp", 1, n_dp, "expert_sums")[None]], (0, n_ctx - 1), (1, 0), n_ctx,
        hidden_width, grads,
    )
    input_grad = input_call(place, grad_mid, gins, order.seen)
    grad_qkv, grad_proj, grad_router, *vectors = shared_grads_call(place, every, width, expert_count)
    g1_gain, g1_bias, g_query_bias, g_value_bias, g2_gain, g2_bias, g_proj_bias = (
        v.reshape(share) for v in vectors
    )
    return (
        block_out.reshape(tokens.shape),
        input_grad.reshape(tokens.shape),
        g1_gain,
        g1_bias,
        grad_qkv,
        g_query_bias,
        g_value_bias,
        grad_proj,
        g_proj_bias,
        g2_gain,
        g2_bias,
        grad_router.T,
        grad_up[None],
        grad_up_bias,
        grad_down[None],
        grad_down_bias,
    )


def solution(mesh):
    images = P(("expert", "dp"), "ctx", None)
    ints = P(("expert", "dp"), "ctx")
    placed = (images, images, ints, images, ints) + (P(),) * 10 + (
        P("expert", None, None),
        P("expert", None),
        P("expert", None, None),
        P("expert", None),
    )
    sizes = tuple(mesh.shape[a] for a in ("expert", "ctx", "dp"))

    def run(*args):
        return local(sizes, *args)

    return jax.shard_map(
        run,
        mesh=mesh,
        in_specs=placed,
        out_specs=(
            images,
            images,
            P("expert"),
            P("expert"),
            P("expert", None),
            P("expert"),
            P("expert"),
            P("expert", None),
            P("expert"),
            P("expert"),
            P("expert"),
            P("expert", None),
            P("expert", None, None),
            P("expert", None),
            P("expert", None, None),
            P("expert", None),
        ),
        check_vma=False,
    )
```
